32 devices in a mesh: mode: 4 (over y, x), dp: 8 (over z, core).
Axes of the slice: x: 2, y: 2, z: 4, core: 2. Of those that a mesh axis runs over, the one named last changes fastest.
Arguments:
- rows: bfloat16 [32, 1024, 768], P(('mode', 'dp')), may hold values from -6 to 6
- memory: bfloat16 [32, 512, 768], P(('mode', 'dp')), may hold values from -6 to 6
- cotangent: bfloat16 [32, 1024, 768], P(('mode', 'dp')), may hold values from -6 to 6
- mode_ids: int32 [32], replicated, may hold values from 0 to 3, as said below
- target_lengths: int32 [32], replicated, may hold values from 128 to 1024
- encoder_lengths: int32 [32], replicated, may hold values from 32 to 512
- self_q: bfloat16 [768, 768], P(('mode', 'dp')), may hold values from -0.21875 to 0.21875
- self_k: bfloat16 [768, 768], P(('mode', 'dp')), may hold values from -0.21875 to 0.21875
- self_v: bfloat16 [768, 768], P(('mode', 'dp')), may hold values from -0.21875 to 0.21875
- self_o: bfloat16 [768, 768], P(('mode', 'dp')), may hold values from -1.75 to 1.75
- self_gain: bfloat16 [768], P(('mode', 'dp')), may hold values from 0.5 to 1.5
- cross_q: bfloat16 [768, 768], P(('mode', 'dp')), may hold values from -0.21875 to 0.21875
- cross_k: bfloat16 [768, 768], P(('mode', 'dp')), may hold values from -0.21875 to 0.21875
- cross_v: bfloat16 [768, 768], P(('mode', 'dp')), may hold values from -0.21875 to 0.21875
- cross_o: bfloat16 [768, 768], P(('mode', 'dp')), may hold values from -1.75 to 1.75
- cross_gain: bfloat16 [768], P(('mode', 'dp')), may hold values from 0.5 to 1.5
- ffn_gain: bfloat16 [768], P(('mode', 'dp')), may hold values from 0.5 to 1.5
- ffn_gate: bfloat16 [4, 768, 2048], P('mode', 'dp'), may hold values from -0.21875 to 0.21875
- ffn_up: bfloat16 [4, 768, 2048], P('mode', 'dp'), may hold values from -0.21875 to 0.21875
- ffn_down: bfloat16 [4, 2048, 768], P('mode', 'dp'), may hold values from -0.125 to 0.125
Outputs:
- output: bfloat16 [32, 1024, 768], P(('mode', 'dp'))
- rows_grad: bfloat16 [32, 1024, 768], P(('mode', 'dp'))
- memory_grad: bfloat16 [32, 512, 768], P(('mode', 'dp'))
- self_q_grad: float32 [768, 768], P(('mode', 'dp'))
- self_k_grad: float32 [768, 768], P(('mode', 'dp'))
- self_v_grad: float32 [768, 768], P(('mode', 'dp'))
- self_o_grad: float32 [768, 768], P(('mode', 'dp'))
- self_gain_grad: float32 [768], P(('mode', 'dp'))
- cross_q_grad: float32 [768, 768], P(('mode', 'dp'))
- cross_k_grad: float32 [768, 768], P(('mode', 'dp'))
- cross_v_grad: float32 [768, 768], P(('mode', 'dp'))
- cross_o_grad: float32 [768, 768], P(('mode', 'dp'))
- cross_gain_grad: float32 [768], P(('mode', 'dp'))
- ffn_gain_grad: float32 [768], P(('mode', 'dp'))
- ffn_gate_grad: float32 [4, 768, 2048], P('mode', 'dp')
- ffn_up_grad: float32 [4, 768, 2048], P('mode', 'dp')
- ffn_down_grad: float32 [4, 2048, 768], P('mode', 'dp')
The draws below stay inside these ranges and needn't reach their ends.
Inputs may be any that keep to these rules, and one draw needn't show every extreme that they name: `mode_ids`: each mode names exactly one in 4 of the rows.
All inputs are finite; a program needn't handle non-finite values.
Results may differ from the reference program's by a relative error of at most 0.022.
Values may be sent and summed in bfloat16 or wider, within the bound.
No kernel may reach another device: no remote copies, remote signals or barrier semaphores. Data moves between devices by JAX's collectives and lax.ppermute only.
A program may use at most 320 MiB of HBM per device.

```python
import jax
import jax.numpy as jnp
from jax import lax

D = 768
HEADS = 12
HEAD_DIM = 64
FF = 2048
MODES = 4
TGT = 1024
MEM = 512
ROWS = 32


def mode_order(key):
    return jax.random.permutation(key, ROWS)


def draw_mode_ids(key, part):
    order = mode_order(key)
    return (order % MODES).astype(jnp.int32)


def draw_target_lengths(key, part):
    order = mode_order(key)
    mode = order % MODES
    key = jax.random.fold_in(key, 11)
    lowest = jnp.array([TGT // 8, TGT // 2, TGT // 8, TGT // 2], jnp.int32)
    highest = jnp.array([TGT // 4, TGT, TGT // 2, TGT], jnp.int32)
    bottom = lowest[mode]
    width = highest[mode] - bottom + 1
    draws = jax.random.randint(key, (ROWS,), 0, 1 << 20)
    length = bottom + draws % width
    length = jnp.where(order == MODES, TGT // 8, length)
    return jnp.where(order == MODES - 1, TGT, length).astype(jnp.int32)


def draw_encoder_lengths(key, part):
    order = mode_order(key)
    key = jax.random.fold_in(key, 23)
    length = jax.random.randint(key, (ROWS,), 32, MEM + 1)
    length = jnp.where(order == 1, 32, length)
    return jnp.where(order == 0, MEM, length).astype(jnp.int32)


def steps_of(rng, dims, cuts, smallest, top_value):
    level = 1.0
    for dim, shards_of in cuts:
        heights = jax.random.uniform(jax.random.fold_in(jax.random.fold_in(rng, 6), dim), (shards_of,), jnp.float32, smallest / len(cuts), top_value / len(cuts))
        level = level * jnp.repeat(jnp.exp(heights), dims[dim] // shards_of).reshape((-1,) + (1,) * (len(dims) - 1 - dim))
    return level


def noise(key, shape, scale, most, shards=(), held_as=jnp.bfloat16):
    factor_of = steps_of(key, shape, shards, -0.22, 0.18) if shards else 1.0
    values = jax.random.normal(key, shape, jnp.float32) * scale * factor_of
    return jnp.minimum(jnp.maximum(values, -most), most).astype(held_as)


def setup_inputs(seed: int = 0) -> dict:
    key_list = jax.random.split(jax.random.key(seed), 21)
    rows = noise(key_list[0], (ROWS, TGT, D), 1.0, 6.0, ((0, 32),))
    memory = noise(key_list[1], (ROWS, MEM, D), 1.0, 6.0, ((0, 32),))
    cotangent = noise(key_list[2], (ROWS, TGT, D), 1.0, 6.0, ((0, 32),))
    mode_ids = draw_mode_ids(jax.random.fold_in(key_list[20], 71), 0)
    target_lengths = draw_target_lengths(jax.random.fold_in(key_list[20], 71), 0)
    encoder_lengths = draw_encoder_lengths(jax.random.fold_in(key_list[20], 71), 0)
    self_q = noise(key_list[6], (D, D), D ** -0.5, 0.21875, ((0, 32),))
    self_k = noise(key_list[7], (D, D), D ** -0.5, 0.21875, ((0, 32),))
    self_v = noise(key_list[8], (D, D), D ** -0.5, 0.21875, ((0, 32),))
    self_o = noise(key_list[9], (D, D), (D // 64) ** -0.5, 1.75, ((0, 32),))
    self_gain = jnp.clip(1.0 + 0.1 * jax.random.normal(key_list[10], (D,), jnp.float32), 0.5, 1.5).astype(jnp.bfloat16)
    cross_q = noise(key_list[11], (D, D), D ** -0.5, 0.21875, ((0, 32),))
    cross_k = noise(key_list[12], (D, D), D ** -0.5, 0.21875, ((0, 32),))
    cross_v = noise(key_list[13], (D, D), D ** -0.5, 0.21875, ((0, 32),))
    cross_o = noise(key_list[14], (D, D), (D // 64) ** -0.5, 1.75, ((0, 32),))
    cross_gain = jnp.clip(1.0 + 0.1 * jax.random.normal(key_list[15], (D,), jnp.float32), 0.5, 1.5).astype(jnp.bfloat16)
    ffn_gain = jnp.clip(1.0 + 0.1 * jax.random.normal(key_list[16], (D,), jnp.float32), 0.5, 1.5).astype(jnp.bfloat16)
    ffn_gate = noise(key_list[17], (MODES, D, FF), D ** -0.5, 0.21875, ((0, 4), (1, 8)))
    ffn_up = noise(key_list[18], (MODES, D, FF), D ** -0.5, 0.21875, ((0, 4), (1, 8)))
    ffn_down = noise(key_list[19], (MODES, FF, D), FF ** -0.5, 0.125, ((0, 4), (1, 8)))
    return dict(rows=rows, memory=memory, cotangent=cotangent, mode_ids=mode_ids, target_lengths=target_lengths, encoder_lengths=encoder_lengths, self_q=self_q, self_k=self_k, self_v=self_v, self_o=self_o, self_gain=self_gain, cross_q=cross_q, cross_k=cross_k, cross_v=cross_v, cross_o=cross_o, cross_gain=cross_gain, ffn_gain=ffn_gain, ffn_gate=ffn_gate, ffn_up=ffn_up, ffn_down=ffn_down)


@jax.custom_vjp
def low(v):
    return lax.optimization_barrier(v.astype(jnp.bfloat16)).astype(jnp.float32)

@jax.custom_vjp
def low_back(v):
    return v

def low_keep(v):
    return (low(v), None)

def low_pass(kept, grad):
    return (grad,)

def back_keep(v):
    return (v, None)

def back_low(kept, grad):
    return (low(grad),)
low.defvjp(low_keep, low_pass)
low_back.defvjp(back_keep, back_low)
EPS = 1e-06
NEG = -1e+30
HIGH = lax.Precision.HIGHEST

def both_ways(v):
    return low(low_back(v))

def matmul(left, right):
    return jnp.dot(left, right, precision=HIGH, preferred_element_type=jnp.float32)

def rms_scale(value, gain):
    return value * lax.rsqrt(lax.optimization_barrier(jnp.mean(value * value, axis=-1, keepdims=True)) + EPS) * gain

def attend(query, keys, values, allowed):
    query_heads = query.reshape(query.shape[0], HEADS, HEAD_DIM)
    key_heads = keys.reshape(keys.shape[0], HEADS, HEAD_DIM)
    value_heads = values.reshape(values.shape[0], HEADS, HEAD_DIM)
    raw = jnp.einsum('qhd,khd->hqk', query_heads, key_heads, precision=HIGH) * HEAD_DIM ** (-0.5)
    scores = jnp.where(allowed[None], low_back(raw), NEG)
    weights = low(jax.nn.softmax(scores, axis=-1))
    mixed = jnp.einsum('hqk,khd->qhd', weights, value_heads, precision=HIGH)
    return mixed.reshape(query.shape[0], HEADS * HEAD_DIM)

def row_forward(params, ffn, tokens, memory_row, mode, live_len, memory_len):
    wq, wk, wv, wo, gain_self, cq, ck, cv, co, gain_cross, gain_ffn = params
    wg, wu, wd = ffn
    position = jnp.arange(TGT, dtype=jnp.int32)
    h1 = low(rms_scale(tokens, gain_self))
    query = both_ways(matmul(h1, wq))
    keys = both_ways(matmul(h1, wk))
    values = both_ways(matmul(h1, wv))
    causal = position[None, :] <= position[:, None]
    mixed = both_ways(attend(query, keys, values, causal))
    x1 = tokens + low_back(matmul(mixed, wo))
    h2 = low(rms_scale(x1, gain_cross))
    cross_query = both_ways(matmul(h2, cq))
    cross_keys = both_ways(matmul(memory_row, ck))
    cross_values = both_ways(matmul(memory_row, cv))
    live_keys = jnp.arange(MEM, dtype=jnp.int32)[None, :] < memory_len
    allowed = jnp.broadcast_to(live_keys, (TGT, MEM))
    cross_mixed = both_ways(attend(cross_query, cross_keys, cross_values, allowed))
    x2 = x1 + low_back(matmul(cross_mixed, co))
    h3 = low(rms_scale(x2, gain_ffn))
    gate = low_back(matmul(h3, wg[mode]))
    up = low_back(matmul(h3, wu[mode]))
    hidden = low(jax.nn.gelu(gate, approximate=True) * up)
    result = x2 + low_back(matmul(hidden, wd[mode]))
    valid = (position < live_len)[:, None]
    return jnp.where(valid, result, 0.0)

def reference(rows, memory, cotangent, mode_ids, target_lengths, encoder_lengths, self_q, self_k, self_v, self_o, self_gain, cross_q, cross_k, cross_v, cross_o, cross_gain, ffn_gain, ffn_gate, ffn_up, ffn_down):
    params = tuple((a.astype(jnp.float32) for a in (self_q, self_k, self_v, self_o, self_gain, cross_q, cross_k, cross_v, cross_o, cross_gain, ffn_gain)))
    ffn = (ffn_gate.astype(jnp.float32), ffn_up.astype(jnp.float32), ffn_down.astype(jnp.float32))
    start = (jax.tree.map(jnp.zeros_like, params), jax.tree.map(jnp.zeros_like, ffn))

    def step(carry, item):
        tokens, memory_row, grad_row, mode, live_len, memory_len = item

        def forward(p, w, t, m):
            return row_forward(p, w, t, m, mode, live_len, memory_len)
        result, pull = jax.vjp(forward, params, ffn, tokens.astype(jnp.float32), memory_row.astype(jnp.float32))
        grad_params, grad_ffn, grad_tokens, grad_memory = pull(grad_row.astype(jnp.float32))
        total = (jax.tree.map(jnp.add, carry[0], grad_params), jax.tree.map(jnp.add, carry[1], grad_ffn))
        return (total, (result.astype(jnp.bfloat16), grad_tokens.astype(jnp.bfloat16), grad_memory.astype(jnp.bfloat16)))
    sums, outs = lax.scan(step, start, (rows, memory, cotangent, mode_ids, target_lengths, encoder_lengths))
    grad_params, grad_ffn = sums
    output, rows_grad, memory_grad = outs
    return (output, rows_grad, memory_grad, grad_params[0], grad_params[1], grad_params[2], grad_params[3], grad_params[4], grad_params[5], grad_params[6], grad_params[7], grad_params[8], grad_params[9], grad_params[10], grad_ffn[0], grad_ffn[1], grad_ffn[2])
```

```python
import functools

import jax
import jax.numpy as jnp
from jax import lax
from jax.experimental import pallas as pl
from jax.experimental.pallas import tpu as pltpu
from jax.sharding import PartitionSpec as P

HEADS = 12
HEAD_DIM = 64
PAIR = 2 * HEAD_DIM
EPS = 1e-06
NEG = -1e30
SCALE = HEAD_DIM ** -0.5
QB = 256
ALL = ("mode", "dp")
BF = jnp.bfloat16
F32 = jnp.float32
VMEM = 56 * 2**20


def nt(left, right):
    return lax.dot_general(left, right, (((1,), (1,)), ((), ())), preferred_element_type=F32)


def nn(left, right):
    return jnp.dot(left, right, preferred_element_type=F32)


def tn(left, right):
    return lax.dot_general(left, right, (((0,), (0,)), ((), ())), preferred_element_type=F32)


def head_lanes(value, h):
    lane = lax.broadcasted_iota(jnp.int32, value.shape, 1)
    return jnp.where((lane >= HEAD_DIM) == (h == 1), value, jnp.zeros_like(value))


def masks(causal, key_count, qb, limit):
    if causal:
        parts = []
        if qb:
            parts.append((0, qb * QB, None))
        row = lax.broadcasted_iota(jnp.int32, (QB, QB), 0)
        col = lax.broadcasted_iota(jnp.int32, (QB, QB), 1)
        parts.append((qb * QB, QB, row <= col))
        return parts
    row = lax.broadcasted_iota(jnp.int32, (key_count, QB), 0)
    return [(0, key_count, row < limit)]


def attend_fwd_kernel(causal, lens, q_ref, k_ref, v_ref, o_ref, lse_ref, vt):
    live, limit = lens[0], lens[1]
    length, key_count = q_ref.shape[0], k_ref.shape[0]
    vt[...] = jnp.swapaxes(v_ref[...].astype(F32), 0, 1).astype(BF)
    for qb in range(length // QB):
        at = pl.ds(qb * QB, QB)

        @pl.when(qb * QB < live)
        def _(qb=qb, at=at):
            query = q_ref[at, :] * jnp.asarray(SCALE, BF)
            parts = masks(causal, key_count, qb, limit)
            outs = []
            for h in range(2):
                mine = head_lanes(query, h)
                scores = []
                for first, count, mask in parts:
                    s = nt(k_ref[pl.ds(first, count), :], mine)
                    scores.append(s if mask is None else jnp.where(mask, s, NEG))
                top = functools.reduce(
                    jnp.maximum, [jnp.max(s, axis=0, keepdims=True) for s in scores]
                )
                total, mixed = 0.0, 0.0
                for (first, count, _), s in zip(parts, scores):
                    p = jnp.exp(s - top)
                    total = total + jnp.sum(p, axis=0, keepdims=True)
                    mixed = mixed + nn(
                        vt[pl.ds(h * HEAD_DIM, HEAD_DIM), pl.ds(first, count)], p.astype(BF)
                    )
                outs.append(mixed / total)
                lse_ref[0, pl.ds(h, 1), at] = top + jnp.log(total)
            o_ref[at, :] = jnp.swapaxes(jnp.concatenate(outs, axis=0), 0, 1).astype(BF)

        @pl.when(qb * QB >= live)
        def _(at=at):
            o_ref[at, :] = jnp.zeros((QB, PAIR), BF)
            lse_ref[0, pl.ds(0, 2), at] = jnp.zeros((2, QB), F32)


def attend_bwd_kernel(
    causal, lens, q_ref, k_ref, v_ref, o_ref, do_ref, lse_ref, dq_ref, dk_ref, dv_ref, kt, dk, dv
):
    live, limit = lens[0], lens[1]
    length, key_count = q_ref.shape[0], k_ref.shape[0]
    kt[...] = jnp.swapaxes(k_ref[...].astype(F32), 0, 1).astype(BF)
    dk[...] = jnp.zeros_like(dk)
    dv[...] = jnp.zeros_like(dv)
    for qb in range(length // QB):
        at = pl.ds(qb * QB, QB)

        @pl.when(qb * QB < live)
        def _(qb=qb, at=at):
            query = q_ref[at, :] * jnp.asarray(SCALE, BF)
            grad = do_ref[at, :]
            inner = jnp.swapaxes(o_ref[at, :].astype(F32) * grad.astype(F32), 0, 1)
            parts = masks(causal, key_count, qb, limit)
            sums = [[0.0, 0.0] for _ in parts]
            outs = []
            for h in range(2):
                mine = head_lanes(query, h)
                grad_mine = head_lanes(grad, h)
                lse = lse_ref[0, pl.ds(h, 1), at]
                delta = jnp.sum(inner[h * HEAD_DIM : (h + 1) * HEAD_DIM], axis=0, keepdims=True)
                grad_query = 0.0
                for i, (first, count, mask) in enumerate(parts):
                    keys = pl.ds(first, count)
                    p = jnp.exp(nt(k_ref[keys, :], mine) - lse)
                    if mask is not None:
                        p = jnp.where(mask, p, 0.0)
                    dp = nt(v_ref[keys, :], grad_mine)
                    ds = (p * (dp - delta)).astype(BF)
                    sums[i][0] = sums[i][0] + nn(ds, mine)
                    sums[i][1] = sums[i][1] + nn(p.astype(BF), grad_mine)
                    grad_query = grad_query + nn(kt[pl.ds(h * HEAD_DIM, HEAD_DIM), keys], ds)
                outs.append(grad_query * SCALE)
            for (first, count, _), (sum_k, sum_v) in zip(parts, sums):
                dk[pl.ds(first, count), :] += sum_k
                dv[pl.ds(first, count), :] += sum_v
            dq_ref[at, :] = jnp.swapaxes(jnp.concatenate(outs, axis=0), 0, 1).astype(BF)

        @pl.when(qb * QB >= live)
        def _(at=at):
            dq_ref[at, :] = jnp.zeros((QB, PAIR), BF)

    dk_ref[...] = dk[...].astype(BF)
    dv_ref[...] = dv[...].astype(BF)


def columns(rows, first):
    return pl.BlockSpec((rows, PAIR), lambda g, lens: (0, first + g))


def attend_forward(query, keys, values, lens, causal):
    (qa, q0), (ka, k0), (va, v0) = query, keys, values
    length, key_count = qa.shape[0], ka.shape[0]
    pairs = HEADS // 2
    pixels = length * key_count * HEADS // (2 if causal else 1)
    return pl.pallas_call(
        functools.partial(attend_fwd_kernel, causal),
        grid_spec=pltpu.PrefetchScalarGridSpec(
            num_scalar_prefetch=1,
            grid=(pairs,),
            in_specs=[columns(length, q0), columns(key_count, k0), columns(key_count, v0)],
            out_specs=[
                columns(length, 0),
                pl.BlockSpec((1, 2, length), lambda g, lens: (g, 0, 0)),
            ],
            scratch_shapes=[pltpu.VMEM((PAIR, key_count), BF)],
        ),
        out_shape=[
            jax.ShapeDtypeStruct((length, HEADS * HEAD_DIM), BF),
            jax.ShapeDtypeStruct((pairs, 2, length), F32),
        ],
        compiler_params=pltpu.CompilerParams(vmem_limit_bytes=VMEM),
        cost_estimate=pl.CostEstimate(
            flops=pixels * 4 * HEAD_DIM * 4, bytes_accessed=8 * length * 768, transcendentals=pixels
        ),
        name="attend_causal" if causal else "attend_memory",
    )(lens, qa, ka, va)


def attend_backward(query, keys, values, mixed, grad, lse, lens, causal):
    (qa, q0), (ka, k0), (va, v0) = query, keys, values
    length, key_count = qa.shape[0], ka.shape[0]
    pairs = HEADS // 2
    pixels = length * key_count * HEADS // (2 if causal else 1)
    return pl.pallas_call(
        functools.partial(attend_bwd_kernel, causal),
        grid_spec=pltpu.PrefetchScalarGridSpec(
            num_scalar_prefetch=1,
            grid=(pairs,),
            in_specs=[
                columns(length, q0),
                columns(key_count, k0),
                columns(key_count, v0),
                columns(length, 0),
                columns(length, 0),
                pl.BlockSpec((1, 2, length), lambda g, lens: (g, 0, 0)),
            ],
            out_specs=[columns(length, 0), columns(key_count, 0), columns(key_count, 0)],
            scratch_shapes=[
                pltpu.VMEM((PAIR, key_count), BF),
                pltpu.VMEM((key_count, PAIR), F32),
                pltpu.VMEM((key_count, PAIR), F32),
            ],
        ),
        out_shape=[
            jax.ShapeDtypeStruct((length, HEADS * HEAD_DIM), BF),
            jax.ShapeDtypeStruct((key_count, HEADS * HEAD_DIM), BF),
            jax.ShapeDtypeStruct((key_count, HEADS * HEAD_DIM), BF),
        ],
        compiler_params=pltpu.CompilerParams(vmem_limit_bytes=VMEM),
        cost_estimate=pl.CostEstimate(
            flops=pixels * 10 * HEAD_DIM * 3, bytes_accessed=16 * length * 768, transcendentals=pixels
        ),
        name="attend_causal_back" if causal else "attend_memory_back",
    )(lens, qa, ka, va, mixed, grad, lse)


GELU_A = 0.7978845608028654
GELU_B = 0.044715


def feed_kernel(
    h_ref, g_ref, gu_ref, down_ref, y_ref, dh_ref, hid_ref, dgu_ref, *, ff, step
):
    h, g = h_ref[...], g_ref[...]
    y, dh = 0.0, 0.0
    for c in range(0, ff, step):
        wg = gu_ref[:, pl.ds(c, step)]
        wu = gu_ref[:, pl.ds(ff + c, step)]
        wd = down_ref[pl.ds(c, step), :]
        gate, up, dhid = nn(h, wg), nn(h, wu), nt(g, wd)
        square = gate * gate
        th = jnp.tanh(gate * (GELU_A + (GELU_A * GELU_B) * square))
        half = 0.5 + 0.5 * th
        act = gate * half
        slope = half + (0.5 * gate) * (1.0 - th * th) * (
            GELU_A + (3.0 * GELU_A * GELU_B) * square
        )
        hidden = (act * up).astype(BF)
        dgate = (dhid * up * slope).astype(BF)
        dup = (dhid * act).astype(BF)
        hid_ref[:, pl.ds(c, step)] = hidden
        dgu_ref[:, pl.ds(c, step)] = dgate
        dgu_ref[:, pl.ds(ff + c, step)] = dup
        y = y + nn(hidden, wd)
        dh = dh + nt(dgate, wg) + nt(dup, wu)
    y_ref[...] = y.astype(BF)
    dh_ref[...] = dh.astype(BF)


def feed(h3, grad, wgu, wd):
    tokens, width = h3.shape
    ff = wd.shape[0]
    block = min(256, tokens)

    def by_token(n):
        return pl.BlockSpec((block, n), lambda i: (i, 0))

    def whole(a):
        return pl.BlockSpec(a.shape, lambda i: (0, 0))

    return pl.pallas_call(
        functools.partial(feed_kernel, ff=ff, step=512),
        grid=(tokens // block,),
        in_specs=[by_token(width), by_token(width), whole(wgu), whole(wd)],
        out_specs=[by_token(width), by_token(width), by_token(ff), by_token(2 * ff)],
        out_shape=[
            jax.ShapeDtypeStruct((tokens, width), BF),
            jax.ShapeDtypeStruct((tokens, width), BF),
            jax.ShapeDtypeStruct((tokens, ff), BF),
            jax.ShapeDtypeStruct((tokens, 2 * ff), BF),
        ],
        compiler_params=pltpu.CompilerParams(vmem_limit_bytes=VMEM),
        cost_estimate=pl.CostEstimate(
            flops=12 * tokens * width * ff, bytes_accessed=40 * 2**20, transcendentals=tokens * ff
        ),
        name="feed",
    )(h3, grad, wgu, wd)


def reorder_kernel(order, x_ref, o_ref):
    def move(i, carry):
        o_ref[i] = x_ref[order[i]]
        return carry

    lax.fori_loop(0, o_ref.shape[0], move, 0)


def reorder(value, order):
    return pl.pallas_call(
        reorder_kernel,
        grid_spec=pltpu.PrefetchScalarGridSpec(
            num_scalar_prefetch=1,
            grid=(1,),
            in_specs=[pl.BlockSpec(value.shape, lambda i, order: (0, 0, 0))],
            out_specs=pl.BlockSpec(value.shape, lambda i, order: (0, 0, 0)),
        ),
        out_shape=jax.ShapeDtypeStruct(value.shape, value.dtype),
        compiler_params=pltpu.CompilerParams(vmem_limit_bytes=16 * 2**20),
        cost_estimate=pl.CostEstimate(
            flops=0, bytes_accessed=2 * value.size * 2, transcendentals=0
        ),
        name="reorder",
    )(order, value)


def to_modes(value, source):
    count = lax.axis_size(ALL)
    tokens, width = value.shape
    piece = tokens // count
    dealt = value.reshape(piece // 8, count, 8, width).swapaxes(0, 1).reshape(count, piece, width)
    spread = lax.all_to_all(dealt, ALL, 0, 0, tiled=True)
    return lax.all_to_all(reorder(spread, source), "mode", 0, 0, tiled=True).reshape(tokens, width)


def from_modes(value, target):
    count = lax.axis_size(ALL)
    tokens, width = value.shape
    piece = tokens // count
    spread = lax.all_to_all(value.reshape(count, piece, width), "mode", 0, 0, tiled=True)
    dealt = lax.all_to_all(reorder(spread, target), ALL, 0, 0, tiled=True)
    return dealt.reshape(count, piece // 8, 8, width).swapaxes(0, 1).reshape(tokens, width)


def norm_piece(value, gain):
    return value * lax.rsqrt(jnp.mean(value * value, axis=-1, keepdims=True) + EPS) * gain


def gather_all(*pieces):
    return lax.all_gather(jnp.concatenate(pieces, axis=1), ALL, axis=0, tiled=True)


def lanes_of(*vectors):
    columns_ = jnp.stack(vectors, axis=1)
    return jnp.pad(columns_, ((0, 0), (0, 256 - len(vectors))))


def on_device(
    rows,
    memory,
    cotangent,
    mode_ids,
    target_lengths,
    encoder_lengths,
    self_q,
    self_k,
    self_v,
    self_o,
    self_gain,
    cross_q,
    cross_k,
    cross_v,
    cross_o,
    cross_gain,
    ffn_gain,
    ffn_gate,
    ffn_up,
    ffn_down,
):
    devices = lax.axis_size(ALL)
    per_mode = lax.axis_size("dp")
    here = lax.axis_index(ALL)
    width = rows.shape[2]
    ff = ffn_gate.shape[2]
    index = jnp.arange(devices, dtype=jnp.int32)
    same = mode_ids[:, None] == mode_ids[None, :]
    earlier = index[None, :] < index[:, None]
    rank = jnp.sum(jnp.where(same & earlier, 1, 0), axis=1).astype(jnp.int32)
    target = mode_ids * per_mode + rank
    source = jnp.sum(
        jnp.where(target[:, None] == index[None, :], index[:, None], 0), axis=0
    ).astype(jnp.int32)
    live_len = jnp.sum(jnp.where(index == here, target_lengths, 0))
    memory_len = jnp.sum(jnp.where(index == here, encoder_lengths, 0))
    lens = jnp.stack([live_len, memory_len]).astype(jnp.int32)
    tokens, memory_row, incoming = rows[0], memory[0], cotangent[0]
    valid = (jnp.arange(tokens.shape[0], dtype=jnp.int32) < live_len)[:, None]
    grad_low = jnp.where(valid, incoming, jnp.zeros_like(incoming))

    own = gather_all(self_q, self_k, self_v, self_o, lanes_of(self_gain, cross_gain, ffn_gain))
    crossing = gather_all(cross_q, cross_k, cross_v, cross_o)
    wgu = lax.all_gather(
        jnp.concatenate([ffn_gate[0], ffn_up[0]], axis=1), "dp", axis=0, tiled=True
    )
    wd = lax.all_gather(ffn_down[0], "dp", axis=0, tiled=True)
    routed_grad = to_modes(grad_low, source)

    wqkv, wo = own[:, : 3 * width], own[:, 3 * width : 4 * width]
    gains = own[:, 4 * width : 4 * width + 8].astype(F32)
    gain_self, gain_cross, gain_ffn = gains[:, 0], gains[:, 1], gains[:, 2]
    tokens_wide = tokens.astype(F32)
    h1 = norm_piece(tokens_wide, gain_self).astype(BF)
    qkv = nn(h1, wqkv).astype(BF)
    pairs = HEADS // 2
    self_in = ((qkv, 0), (qkv, pairs), (qkv, 2 * pairs))
    mixed, log_self = attend_forward(*self_in, lens, True)
    x1 = tokens_wide + nn(mixed, wo)

    cq, ckv, co = crossing[:, :width], crossing[:, width : 3 * width], crossing[:, 3 * width :]
    h2 = norm_piece(x1, gain_cross).astype(BF)
    cross_query = nn(h2, cq).astype(BF)
    cross_kv = nn(memory_row, ckv).astype(BF)
    cross_in = ((cross_query, 0), (cross_kv, 0), (cross_kv, pairs))
    cross_mixed, log_cross = attend_forward(*cross_in, lens, False)
    x2 = x1 + nn(cross_mixed, co)
    h3 = norm_piece(x2, gain_ffn).astype(BF)

    routed_h = to_modes(h3, source)
    routed_y, routed_dh, hidden, dgu = feed(routed_h, routed_grad, wgu, wd)
    grad_h3 = from_modes(routed_dh, target)
    y = from_modes(routed_y, target)
    grad_wgu = tn(routed_h, dgu).astype(BF)
    grad_wd = tn(hidden, routed_grad).astype(BF)
    sum_wgu = lax.psum_scatter(grad_wgu, "dp", scatter_dimension=0, tiled=True)
    sum_wd = lax.psum_scatter(grad_wd, "dp", scatter_dimension=0, tiled=True)
    result = jnp.where(valid, x2 + y.astype(F32), 0.0).astype(BF)

    unused, pull_norm = jax.vjp(norm_piece, x2, gain_ffn)
    grad_x2_norm, grad_gain_ffn = pull_norm(grad_h3.astype(F32))
    grad_x2 = grad_low.astype(F32) + grad_x2_norm
    grad_two = grad_x2.astype(BF)
    grad_co = tn(cross_mixed, grad_two)
    grad_cross_mixed = nt(grad_two, co).astype(BF)
    dcq, dck, dcv = attend_backward(
        *cross_in, cross_mixed, grad_cross_mixed, log_cross, lens, False
    )
    grad_cq = tn(h2, dcq)
    grad_ck = tn(memory_row, dck)
    grad_cv = tn(memory_row, dcv)
    grad_memory = (nt(dck, ckv[:, :width]) + nt(dcv, ckv[:, width:])).astype(BF)
    unused, pull_norm = jax.vjp(norm_piece, x1, gain_cross)
    grad_x1_norm, grad_gain_cross = pull_norm(nt(dcq, cq))
    grad_x1 = grad_x2 + grad_x1_norm
    cross_grads = jnp.concatenate(
        [grad_cq.astype(BF), grad_ck.astype(BF), grad_cv.astype(BF), grad_co.astype(BF)], axis=1
    )
    cross_sum = lax.psum_scatter(cross_grads, ALL, scatter_dimension=0, tiled=True)

    grad_one = grad_x1.astype(BF)
    grad_wo = tn(mixed, grad_one)
    grad_mixed = nt(grad_one, wo).astype(BF)
    dq, dk, dv = attend_backward(*self_in, mixed, grad_mixed, log_self, lens, True)
    grad_h1 = (
        nt(dq, wqkv[:, :width]) + nt(dk, wqkv[:, width : 2 * width]) + nt(dv, wqkv[:, 2 * width :])
    )
    unused, pull_norm = jax.vjp(norm_piece, tokens_wide, gain_self)
    grad_x_norm, grad_gain_self = pull_norm(grad_h1)
    grad_tokens = (grad_x1 + grad_x_norm).astype(BF)
    own_grads = jnp.concatenate(
        [
            tn(h1, dq).astype(BF),
            tn(h1, dk).astype(BF),
            tn(h1, dv).astype(BF),
            grad_wo.astype(BF),
            lanes_of(grad_gain_self, grad_gain_cross, grad_gain_ffn).astype(BF),
        ],
        axis=1,
    )
    own_sum = lax.psum_scatter(own_grads, ALL, scatter_dimension=0, tiled=True).astype(F32)
    cross_sum = cross_sum.astype(F32)
    sum_wgu = sum_wgu.astype(F32)

    def block(value, i):
        return value[:, i * width : (i + 1) * width]

    gain_sums = own_sum[:, 4 * width : 4 * width + 8]
    return (
        result[None],
        grad_tokens[None],
        grad_memory[None],
        block(own_sum, 0),
        block(own_sum, 1),
        block(own_sum, 2),
        block(own_sum, 3),
        gain_sums[:, 0],
        block(cross_sum, 0),
        block(cross_sum, 1),
        block(cross_sum, 2),
        block(cross_sum, 3),
        gain_sums[:, 1],
        gain_sums[:, 2],
        sum_wgu[None, :, :ff],
        sum_wgu[None, :, ff:],
        sum_wd.astype(F32)[None],
    )


def solution(mesh):
    rows = P(ALL, None, None)
    weight = P(ALL, None)
    gain = P(ALL)
    feeding = P("mode", "dp", None)
    return jax.shard_map(
        on_device,
        mesh=mesh,
        in_specs=(
            (rows,) * 3
            + (P(),) * 3
            + (weight,) * 4
            + (gain,)
            + (weight,) * 4
            + (gain,) * 2
            + (feeding,) * 3
        ),
        out_specs=(
            (rows,) * 3
            + (weight,) * 4
            + (gain,)
            + (weight,) * 4
            + (gain,) * 2
            + (feeding,) * 3
        ),
        check_vma=False,
    )
```

```python
import functools

import jax
import jax.numpy as jnp
from jax import lax
from jax.experimental import pallas as pl
from jax.experimental.pallas import tpu as pltpu
from jax.sharding import PartitionSpec as P

HEADS = 12
HEAD_DIM = 64
PAIR = 2 * HEAD_DIM
EPS = 1e-06
NEG = -1e30
SCALE = HEAD_DIM ** -0.5
QB = 256
ALL = ("mode", "dp")
BF = jnp.bfloat16
F32 = jnp.float32
VMEM = 56 * 2**20


def nt(left, right):
    return lax.dot_general(left, right, (((1,), (1,)), ((), ())), preferred_element_type=F32)


def nn(left, right):
    return jnp.dot(left, right, preferred_element_type=F32)


def tn(left, right):
    return lax.dot_general(left, right, (((0,), (0,)), ((), ())), preferred_element_type=F32)


def head_lanes(value, h):
    lane = lax.broadcasted_iota(jnp.int32, value.shape, 1)
    return jnp.where((lane >= HEAD_DIM) == (h == 1), value, jnp.zeros_like(value))


def masks(causal, key_count, qb, limit):
    if causal:
        parts = []
        if qb:
            parts.append((0, qb * QB, None))
        row = lax.broadcasted_iota(jnp.int32, (QB, QB), 0)
        col = lax.broadcasted_iota(jnp.int32, (QB, QB), 1)
        parts.append((qb * QB, QB, row <= col))
        return parts
    row = lax.broadcasted_iota(jnp.int32, (key_count, QB), 0)
    return [(0, key_count, row < limit)]


def attend_fwd_kernel(causal, lens, q_ref, k_ref, v_ref, o_ref, lse_ref, vt):
    live, limit = lens[0], lens[1]
    length, key_count = q_ref.shape[0], k_ref.shape[0]
    vt[...] = jnp.swapaxes(v_ref[...].astype(F32), 0, 1).astype(BF)
    for qb in range(length // QB):
        at = pl.ds(qb * QB, QB)

        @pl.when(qb * QB < live)
        def _(qb=qb, at=at):
            query = q_ref[at, :] * jnp.asarray(SCALE, BF)
            parts = masks(causal, key_count, qb, limit)
            outs = []
            for h in range(2):
                mine = head_lanes(query, h)
                scores = []
                for first, count, mask in parts:
                    s = nt(k_ref[pl.ds(first, count), :], mine)
                    scores.append(s if mask is None else jnp.where(mask, s, NEG))
                top = functools.reduce(
                    jnp.maximum, [jnp.max(s, axis=0, keepdims=True) for s in scores]
                )
                total, mixed = 0.0, 0.0
                for (first, count, _), s in zip(parts, scores):
                    p = jnp.exp(s - top)
                    total = total + jnp.sum(p, axis=0, keepdims=True)
                    mixed = mixed + nn(
                        vt[pl.ds(h * HEAD_DIM, HEAD_DIM), pl.ds(first, count)], p.astype(BF)
                    )
                outs.append(mixed / total)
                lse_ref[0, pl.ds(h, 1), at] = top + jnp.log(total)
            o_ref[at, :] = jnp.swapaxes(jnp.concatenate(outs, axis=0), 0, 1).astype(BF)

        @pl.when(qb * QB >= live)
        def _(at=at):
            o_ref[at, :] = jnp.zeros((QB, PAIR), BF)
            lse_ref[0, pl.ds(0, 2), at] = jnp.zeros((2, QB), F32)


def attend_bwd_kernel(
    causal, lens, q_ref, k_ref, v_ref, o_ref, do_ref, lse_ref, dq_ref, dk_ref, dv_ref, kt, dk, dv
):
    live, limit = lens[0], lens[1]
    length, key_count = q_ref.shape[0], k_ref.shape[0]
    kt[...] = jnp.swapaxes(k_ref[...].astype(F32), 0, 1).astype(BF)
    dk[...] = jnp.zeros_like(dk)
    dv[...] = jnp.zeros_like(dv)
    for qb in range(length // QB):
        at = pl.ds(qb * QB, QB)

        @pl.when(qb * QB < live)
        def _(qb=qb, at=at):
            query = q_ref[at, :] * jnp.asarray(SCALE, BF)
            grad = do_ref[at, :]
            inner = jnp.swapaxes(o_ref[at, :].astype(F32) * grad.astype(F32), 0, 1)
            parts = masks(causal, key_count, qb, limit)
            sums = [[0.0, 0.0] for _ in parts]
            outs = []
            for h in range(2):
                mine = head_lanes(query, h)
                grad_mine = head_lanes(grad, h)
                lse = lse_ref[0, pl.ds(h, 1), at]
                delta = jnp.sum(inner[h * HEAD_DIM : (h + 1) * HEAD_DIM], axis=0, keepdims=True)
                grad_query = 0.0
                for i, (first, count, mask) in enumerate(parts):
                    keys = pl.ds(first, count)
                    p = jnp.exp(nt(k_ref[keys, :], mine) - lse)
                    if mask is not None:
                        p = jnp.where(mask, p, 0.0)
                    dp = nt(v_ref[keys, :], grad_mine)
                    ds = (p * (dp - delta)).astype(BF)
                    sums[i][0] = sums[i][0] + nn(ds, mine)
                    sums[i][1] = sums[i][1] + nn(p.astype(BF), grad_mine)
                    grad_query = grad_query + nn(kt[pl.ds(h * HEAD_DIM, HEAD_DIM), keys], ds)
                outs.append(grad_query * SCALE)
            for (first, count, _), (sum_k, sum_v) in zip(parts, sums):
                dk[pl.ds(first, count), :] += sum_k
                dv[pl.ds(first, count), :] += sum_v
            dq_ref[at, :] = jnp.swapaxes(jnp.concatenate(outs, axis=0), 0, 1).astype(BF)

        @pl.when(qb * QB >= live)
        def _(at=at):
            dq_ref[at, :] = jnp.zeros((QB, PAIR), BF)

    dk_ref[...] = dk[...].astype(BF)
    dv_ref[...] = dv[...].astype(BF)


def columns(rows, first):
    return pl.BlockSpec((rows, PAIR), lambda g, lens: (0, first + g))


def attend_forward(query, keys, values, lens, causal):
    (qa, q0), (ka, k0), (va, v0) = query, keys, values
    length, key_count = qa.shape[0], ka.shape[0]
    pairs = HEADS // 2
    pixels = length * key_count * HEADS // (2 if causal else 1)
    return pl.pallas_call(
        functools.partial(attend_fwd_kernel, causal),
        grid_spec=pltpu.PrefetchScalarGridSpec(
            num_scalar_prefetch=1,
            grid=(pairs,),
            in_specs=[columns(length, q0), columns(key_count, k0), columns(key_count, v0)],
            out_specs=[
                columns(length, 0),
                pl.BlockSpec((1, 2, length), lambda g, lens: (g, 0, 0)),
            ],
            scratch_shapes=[pltpu.VMEM((PAIR, key_count), BF)],
        ),
        out_shape=[
            jax.ShapeDtypeStruct((length, HEADS * HEAD_DIM), BF),
            jax.ShapeDtypeStruct((pairs, 2, length), F32),
        ],
        compiler_params=pltpu.CompilerParams(vmem_limit_bytes=VMEM),
        cost_estimate=pl.CostEstimate(
            flops=32 * 10**9, bytes_accessed=8 * length * 768, transcendentals=pixels
        ),
        name="attend_causal" if causal else "attend_memory",
    )(lens, qa, ka, va)


def attend_backward(query, keys, values, mixed, grad, lse, lens, causal):
    (qa, q0), (ka, k0), (va, v0) = query, keys, values
    length, key_count = qa.shape[0], ka.shape[0]
    pairs = HEADS // 2
    pixels = length * key_count * HEADS // (2 if causal else 1)
    return pl.pallas_call(
        functools.partial(attend_bwd_kernel, causal),
        grid_spec=pltpu.PrefetchScalarGridSpec(
            num_scalar_prefetch=1,
            grid=(pairs,),
            in_specs=[
                columns(length, q0),
                columns(key_count, k0),
                columns(key_count, v0),
                columns(length, 0),
                columns(length, 0),
                pl.BlockSpec((1, 2, length), lambda g, lens: (g, 0, 0)),
            ],
            out_specs=[columns(length, 0), columns(key_count, 0), columns(key_count, 0)],
            scratch_shapes=[
                pltpu.VMEM((PAIR, key_count), BF),
                pltpu.VMEM((key_count, PAIR), F32),
                pltpu.VMEM((key_count, PAIR), F32),
            ],
        ),
        out_shape=[
            jax.ShapeDtypeStruct((length, HEADS * HEAD_DIM), BF),
            jax.ShapeDtypeStruct((key_count, HEADS * HEAD_DIM), BF),
            jax.ShapeDtypeStruct((key_count, HEADS * HEAD_DIM), BF),
        ],
        compiler_params=pltpu.CompilerParams(vmem_limit_bytes=VMEM),
        cost_estimate=pl.CostEstimate(
            flops=40 * 10**9, bytes_accessed=16 * length * 768, transcendentals=pixels
        ),
        name="attend_causal_back" if causal else "attend_memory_back",
    )(lens, qa, ka, va, mixed, grad, lse)


GELU_A = 0.7978845608028654
GELU_B = 0.044715


def feed_kernel(
    h_ref, g_ref, gu_ref, down_ref, y_ref, dh_ref, hid_ref, dgu_ref, *, ff, step
):
    h, g = h_ref[...], g_ref[...]
    y, dh = 0.0, 0.0
    for c in range(0, ff, step):
        wg = gu_ref[:, pl.ds(c, step)]
        wu = gu_ref[:, pl.ds(ff + c, step)]
        wd = down_ref[pl.ds(c, step), :]
        gate, up, dhid = nn(h, wg), nn(h, wu), nt(g, wd)
        square = gate * gate
        th = jnp.tanh(gate * (GELU_A + (GELU_A * GELU_B) * square))
        half = 0.5 + 0.5 * th
        act = gate * half
        slope = half + (0.5 * gate) * (1.0 - th * th) * (
            GELU_A + (3.0 * GELU_A * GELU_B) * square
        )
        hidden = (act * up).astype(BF)
        dgate = (dhid * up * slope).astype(BF)
        dup = (dhid * act).astype(BF)
        hid_ref[:, pl.ds(c, step)] = hidden
        dgu_ref[:, pl.ds(c, step)] = dgate
        dgu_ref[:, pl.ds(ff + c, step)] = dup
        y = y + nn(hidden, wd)
        dh = dh + nt(dgate, wg) + nt(dup, wu)
    y_ref[...] = y.astype(BF)
    dh_ref[...] = dh.astype(BF)


def feed(h3, grad, wgu, wd):
    tokens, width = h3.shape
    ff = wd.shape[0]
    block = min(256, tokens)

    def by_token(n):
        return pl.BlockSpec((block, n), lambda i: (i, 0))

    def whole(a):
        return pl.BlockSpec(a.shape, lambda i: (0, 0))

    return pl.pallas_call(
        functools.partial(feed_kernel, ff=ff, step=512),
        grid=(tokens // block,),
        in_specs=[by_token(width), by_token(width), whole(wgu), whole(wd)],
        out_specs=[by_token(width), by_token(width), by_token(ff), by_token(2 * ff)],
        out_shape=[
            jax.ShapeDtypeStruct((tokens, width), BF),
            jax.ShapeDtypeStruct((tokens, width), BF),
            jax.ShapeDtypeStruct((tokens, ff), BF),
            jax.ShapeDtypeStruct((tokens, 2 * ff), BF),
        ],
        compiler_params=pltpu.CompilerParams(vmem_limit_bytes=VMEM),
        cost_estimate=pl.CostEstimate(
            flops=12 * tokens * width * ff, bytes_accessed=40 * 2**20, transcendentals=tokens * ff
        ),
        name="feed",
    )(h3, grad, wgu, wd)


def reorder_kernel(order, x_ref, o_ref):
    def move(i, carry):
        o_ref[i] = x_ref[order[i]]
        return carry

    lax.fori_loop(0, o_ref.shape[0], move, 0)


def reorder(value, order):
    return pl.pallas_call(
        reorder_kernel,
        grid_spec=pltpu.PrefetchScalarGridSpec(
            num_scalar_prefetch=1,
            grid=(1,),
            in_specs=[pl.BlockSpec(value.shape, lambda i, order: (0, 0, 0))],
            out_specs=pl.BlockSpec(value.shape, lambda i, order: (0, 0, 0)),
        ),
        out_shape=jax.ShapeDtypeStruct(value.shape, value.dtype),
        compiler_params=pltpu.CompilerParams(vmem_limit_bytes=16 * 2**20),
        cost_estimate=pl.CostEstimate(
            flops=0, bytes_accessed=2 * value.size * 2, transcendentals=0
        ),
        name="reorder",
    )(order, value)


def to_modes(value, source):
    count = lax.axis_size(ALL)
    tokens, width = value.shape
    piece = tokens // count
    dealt = value.reshape(piece // 8, count, 8, width).swapaxes(0, 1).reshape(count, piece, width)
    spread = lax.all_to_all(dealt, ALL, 0, 0, tiled=True)
    return lax.all_to_all(reorder(spread, source), "mode", 0, 0, tiled=True).reshape(tokens, width)


def from_modes(value, target, late=None, later=None):
    count = lax.axis_size(ALL)
    tokens, width = value.shape
    piece = tokens // count
    spread = lax.all_to_all(value.reshape(count, piece, width), "mode", 0, 0, tiled=True)
    if late is not None:
        spread = tied(spread, late)
    dealt = lax.all_to_all(reorder(spread, target), ALL, 0, 0, tiled=True)
    if later is not None:
        dealt = tied(dealt, later)
    return dealt.reshape(count, piece // 8, 8, width).swapaxes(0, 1).reshape(tokens, width)


def norm_piece(value, gain):
    return value * lax.rsqrt(jnp.mean(value * value, axis=-1, keepdims=True) + EPS) * gain


def swap(value, j):
    count = lax.axis_size(ALL)
    return lax.ppermute(value, ALL, [(i, i ^ j) for i in range(count)])


def device_number():
    return lax.axis_index(ALL).astype(jnp.int32)[None]


def place_kernel(me, even_ref, odd_ref, o_ref):
    for t in range(even_ref.shape[0]):
        o_ref[jnp.bitwise_xor(2 * t, me[0])] = even_ref[t]
        o_ref[jnp.bitwise_xor(2 * t + 1, me[0])] = odd_ref[t]


def place(even, odd):
    count, rows, width = even.shape
    step = width

    def block(n):
        return pl.BlockSpec((n, rows, step), lambda i, me: (0, 0, i))

    return pl.pallas_call(
        place_kernel,
        grid_spec=pltpu.PrefetchScalarGridSpec(
            num_scalar_prefetch=1,
            grid=(width // step,),
            in_specs=[block(count)] * 2,
            out_specs=block(2 * count),
        ),
        out_shape=jax.ShapeDtypeStruct((2 * count, rows, width), even.dtype),
        compiler_params=pltpu.CompilerParams(vmem_limit_bytes=24 * 2**20),
        cost_estimate=pl.CostEstimate(
            flops=0, bytes_accessed=8 * even.size, transcendentals=0
        ),
        name="place",
    )(device_number(), even, odd)


def gather_all(piece):
    per_mode, modes = lax.axis_size("dp"), lax.axis_size("mode")
    column = jnp.stack([piece] + [swap(piece, 2 * j) for j in range(1, per_mode // 2)])
    plane = jnp.stack([column] + [swap(column, per_mode * j) for j in range(1, modes)])
    plane = plane.reshape((-1,) + piece.shape)
    return place(plane, swap(plane, 1)).reshape(-1, piece.shape[1])


def take_kernel(parts, me, *refs):
    ins, (keep_ref, send_ref) = refs[:parts], refs[parts:]
    first = 0
    for in_ref in ins:
        at = pl.ds(first, in_ref.shape[2])
        first += in_ref.shape[2]
        for t in range(keep_ref.shape[0]):
            keep_ref[t, :, at] = in_ref[jnp.bitwise_xor(2 * t, me[0])]
            send_ref[t, :, at] = in_ref[jnp.bitwise_xor(2 * t + 1, me[0])]


def take(parts):
    count, rows = parts[0].shape[:2]
    width = sum(part.shape[2] for part in parts)
    half = jax.ShapeDtypeStruct((count // 2, rows, width), parts[0].dtype)

    def whole(shape):
        return pl.BlockSpec(shape, lambda i, me: (0, 0, 0))

    return pl.pallas_call(
        functools.partial(take_kernel, len(parts)),
        grid_spec=pltpu.PrefetchScalarGridSpec(
            num_scalar_prefetch=1,
            grid=(1,),
            in_specs=[whole(part.shape) for part in parts],
            out_specs=[whole(half.shape)] * 2,
        ),
        out_shape=[half, half],
        compiler_params=pltpu.CompilerParams(vmem_limit_bytes=48 * 2**20),
        cost_estimate=pl.CostEstimate(
            flops=0, bytes_accessed=8 * half.size, transcendentals=0
        ),
        name="take",
    )(device_number(), *parts)


def add_up(parts):
    return functools.reduce(jnp.add, [part.astype(F32) for part in parts])


def scatter_pairs(parts):
    count = lax.axis_size(ALL)
    parts = [part.reshape(count, part.shape[0] // count, part.shape[1]) for part in parts]
    keep, send = take(parts)
    return add_up([keep, swap(send, 1)]).astype(BF)


def scatter_chips(plane):
    per_mode, modes = lax.axis_size("dp"), lax.axis_size("mode")
    plane = plane.reshape((modes, per_mode // 2) + plane.shape[1:])
    column = add_up(
        [plane[0]] + [swap(plane[j], per_mode * j) for j in range(1, modes)]
    ).astype(BF)
    return add_up([column[0]] + [swap(column[j], 2 * j) for j in range(1, per_mode // 2)])


def tied(first, second):
    return lax.optimization_barrier((first, second))[0]


def lanes_of(*vectors):
    columns_ = jnp.stack(vectors, axis=1)
    return jnp.pad(columns_, ((0, 0), (0, 128 - len(vectors))))


def on_device(
    rows,
    memory,
    cotangent,
    mode_ids,
    target_lengths,
    encoder_lengths,
    self_q,
    self_k,
    self_v,
    self_o,
    self_gain,
    cross_q,
    cross_k,
    cross_v,
    cross_o,
    cross_gain,
    ffn_gain,
    ffn_gate,
    ffn_up,
    ffn_down,
):
    devices = lax.axis_size(ALL)
    per_mode = lax.axis_size("dp")
    here = lax.axis_index(ALL)
    width = rows.shape[2]
    ff = ffn_gate.shape[2]
    index = jnp.arange(devices, dtype=jnp.int32)
    same = mode_ids[:, None] == mode_ids[None, :]
    earlier = index[None, :] < index[:, None]
    rank = jnp.sum(jnp.where(same & earlier, 1, 0), axis=1).astype(jnp.int32)
    target = mode_ids * per_mode + rank
    source = jnp.sum(
        jnp.where(target[:, None] == index[None, :], index[:, None], 0), axis=0
    ).astype(jnp.int32)
    live_len = jnp.sum(jnp.where(index == here, target_lengths, 0))
    memory_len = jnp.sum(jnp.where(index == here, encoder_lengths, 0))
    lens = jnp.stack([live_len, memory_len]).astype(jnp.int32)
    tokens, memory_row, incoming = rows[0], memory[0], cotangent[0]
    valid = (jnp.arange(tokens.shape[0], dtype=jnp.int32) < live_len)[:, None]
    grad_low = jnp.where(valid, incoming, jnp.zeros_like(incoming))

    crossing = lax.all_gather(
        jnp.concatenate([cross_q, cross_k, cross_v, cross_o], axis=1), ALL, axis=0, tiled=True
    )
    own = gather_all(
        jnp.concatenate(
            [self_q, self_k, self_v, lanes_of(self_gain, cross_gain, ffn_gain)], axis=1
        )
    )
    wo = gather_all(tied(self_o, own))
    feeding = (ffn_gate, ffn_up, ffn_down)
    wgu = lax.all_gather(
        jnp.concatenate([feeding[0][0], feeding[1][0]], axis=1), "dp", axis=0, tiled=True
    )
    wd = lax.all_gather(feeding[2][0], "dp", axis=0, tiled=True)
    routed_grad = to_modes(tied(grad_low, own), source)

    wqkv = own[:, : 3 * width]
    gains = own[:, 3 * width : 3 * width + 8].astype(F32)
    gain_self, gain_cross, gain_ffn = gains[:, 0], gains[:, 1], gains[:, 2]
    tokens_wide = tokens.astype(F32)
    h1 = norm_piece(tokens_wide, gain_self).astype(BF)
    qkv = nn(h1, wqkv).astype(BF)
    pairs = HEADS // 2
    self_in = ((qkv, 0), (qkv, pairs), (qkv, 2 * pairs))
    mixed, log_self = attend_forward(*self_in, lens, True)
    x1 = tokens_wide + nn(mixed, wo)

    cq, ckv, co = crossing[:, :width], crossing[:, width : 3 * width], crossing[:, 3 * width :]
    h2 = norm_piece(x1, gain_cross).astype(BF)
    cross_query = nn(h2, cq).astype(BF)
    cross_kv = nn(memory_row, ckv).astype(BF)
    cross_in = ((cross_query, 0), (cross_kv, 0), (cross_kv, pairs))
    cross_mixed, log_cross = attend_forward(*cross_in, lens, False)
    cross_mixed, routed_grad = lax.optimization_barrier((cross_mixed, routed_grad))
    x2 = x1 + nn(cross_mixed, co)
    h3 = norm_piece(x2, gain_ffn).astype(BF)

    routed_h = to_modes(h3, source)
    routed_y, routed_dh, hidden, dgu = feed(routed_h, routed_grad, wgu, wd)
    grad_wgu = tn(routed_h, dgu).astype(BF)
    grad_wd = tn(hidden, routed_grad).astype(BF)
    sum_wgu = lax.psum_scatter(grad_wgu, "dp", scatter_dimension=0, tiled=True)
    sum_wd = lax.psum_scatter(grad_wd, "dp", scatter_dimension=0, tiled=True)
    grad_h3 = from_modes(routed_dh, target)
    grad_h3 = tied(grad_h3, (grad_wgu, grad_wd))

    unused, pull_norm = jax.vjp(norm_piece, x2, gain_ffn)
    grad_x2_norm, grad_gain_ffn = pull_norm(grad_h3.astype(F32))
    grad_x2 = grad_low.astype(F32) + grad_x2_norm
    grad_two = grad_x2.astype(BF)
    grad_co = tn(cross_mixed, grad_two)
    grad_cross_mixed = nt(grad_two, co).astype(BF)
    dcq, dck, dcv = attend_backward(
        *cross_in, cross_mixed, grad_cross_mixed, log_cross, lens, False
    )
    grad_cq = tn(h2, dcq)
    grad_ck = tn(memory_row, dck)
    grad_cv = tn(memory_row, dcv)
    grad_memory = (nt(dck, ckv[:, :width]) + nt(dcv, ckv[:, width:])).astype(BF)
    unused, pull_norm = jax.vjp(norm_piece, x1, gain_cross)
    grad_x1_norm, grad_gain_cross = pull_norm(nt(dcq, cq))
    grad_x1 = grad_x2 + grad_x1_norm
    grad_one = grad_x1.astype(BF)
    grad_wo = tn(mixed, grad_one)
    grad_mixed = nt(grad_one, wo).astype(BF)
    cross_pair = scatter_pairs(
        [part.astype(BF) for part in (grad_cq, grad_ck, grad_cv, grad_co, grad_wo)]
    )
    grad_mixed, cross_pair = lax.optimization_barrier((grad_mixed, cross_pair))
    cross_sum = scatter_chips(cross_pair)
    dq, dk, dv = attend_backward(*self_in, mixed, grad_mixed, log_self, lens, True)
    y = from_modes(tied(routed_y, grad_h3), target, dcq, dq)
    result = jnp.where(valid, x2 + y.astype(F32), 0.0).astype(BF)
    grad_h1 = (
        nt(dq, wqkv[:, :width]) + nt(dk, wqkv[:, width : 2 * width]) + nt(dv, wqkv[:, 2 * width :])
    )
    unused, pull_norm = jax.vjp(norm_piece, tokens_wide, gain_self)
    grad_x_norm, grad_gain_self = pull_norm(grad_h1)
    grad_tokens = (grad_x1 + grad_x_norm).astype(BF)
    own_sum = scatter_chips(scatter_pairs(
        [
            tn(h1, dq).astype(BF),
            tn(h1, dk).astype(BF),
            tn(h1, dv).astype(BF),
            lanes_of(grad_gain_self, grad_gain_cross, grad_gain_ffn).astype(BF),
        ]
    ))
    sum_wgu = sum_wgu.astype(F32)

    def block(value, i):
        return value[:, i * width : (i + 1) * width]

    gain_sums = own_sum[:, 3 * width : 3 * width + 8]
    return (
        result[None],
        grad_tokens[None],
        grad_memory[None],
        block(own_sum, 0),
        block(own_sum, 1),
        block(own_sum, 2),
        block(cross_sum, 4),
        gain_sums[:, 0],
        block(cross_sum, 0),
        block(cross_sum, 1),
        block(cross_sum, 2),
        block(cross_sum, 3),
        gain_sums[:, 1],
        gain_sums[:, 2],
        sum_wgu[None, :, :ff],
        sum_wgu[None, :, ff:],
        sum_wd.astype(F32)[None],
    )


def solution(mesh):
    rows = P(ALL, None, None)
    weight = P(ALL, None)
    gain = P(ALL)
    feeding = P("mode", "dp", None)
    return jax.shard_map(
        on_device,
        mesh=mesh,
        in_specs=(
            (rows,) * 3
            + (P(),) * 3
            + (weight,) * 4
            + (gain,)
            + (weight,) * 4
            + (gain,) * 2
            + (feeding,) * 3
        ),
        out_specs=(
            (rows,) * 3
            + (weight,) * 4
            + (gain,)
            + (weight,) * 4
            + (gain,) * 2
            + (feeding,) * 3
        ),
        check_vma=False,
    )
```

```python
import functools

import jax
import jax.numpy as jnp
from jax import lax
from jax.experimental import pallas as pl
from jax.experimental.pallas import tpu as pltpu
from jax.sharding import PartitionSpec as P

HEADS = 12
HEAD_DIM = 64
PAIR = 2 * HEAD_DIM
EPS = 1e-06
NEG = -1e30
SCALE = HEAD_DIM ** -0.5
QB = 256
ALL = ("mode", "dp")
BF = jnp.bfloat16
F32 = jnp.float32
VMEM = 56 * 2**20
BRIEF = pl.CostEstimate(flops=10**6, bytes_accessed=10**4, transcendentals=0)


def nt(left, right):
    return lax.dot_general(left, right, (((1,), (1,)), ((), ())), preferred_element_type=F32)


def nn(left, right):
    return jnp.dot(left, right, preferred_element_type=F32)


def tn(left, right):
    return lax.dot_general(left, right, (((0,), (0,)), ((), ())), preferred_element_type=F32)


def head_lanes(value, h):
    lane = lax.broadcasted_iota(jnp.int32, value.shape, 1)
    return jnp.where((lane >= HEAD_DIM) == (h == 1), value, jnp.zeros_like(value))


def masks(causal, key_count, qb, limit):
    if causal:
        parts = []
        if qb:
            parts.append((0, qb * QB, None))
        row = lax.broadcasted_iota(jnp.int32, (QB, QB), 0)
        col = lax.broadcasted_iota(jnp.int32, (QB, QB), 1)
        parts.append((qb * QB, QB, row <= col))
        return parts
    row = lax.broadcasted_iota(jnp.int32, (key_count, QB), 0)
    return [(0, key_count, row < limit)]


def attend_fwd_kernel(causal, start, lens, q_ref, k_ref, v_ref, o_ref, lse_ref, vt):
    live, limit = lens[0], lens[1]
    length, key_count = q_ref.shape[0], k_ref.shape[0]
    vt[...] = jnp.swapaxes(v_ref[...].astype(F32), 0, 1).astype(BF)
    for block in range(length // QB):
        at = pl.ds(block * QB, QB)
        qb = start // QB + block

        @pl.when(qb * QB < live)
        def _(qb=qb, at=at):
            query = q_ref[at, :] * jnp.asarray(SCALE, BF)
            parts = masks(causal, key_count, qb, limit)
            outs = []
            for h in range(2):
                mine = head_lanes(query, h)
                scores = []
                for first, count, mask in parts:
                    s = nt(k_ref[pl.ds(first, count), :], mine)
                    scores.append(s if mask is None else jnp.where(mask, s, NEG))
                top = functools.reduce(
                    jnp.maximum, [jnp.max(s, axis=0, keepdims=True) for s in scores]
                )
                total, mixed = 0.0, 0.0
                for (first, count, _), s in zip(parts, scores):
                    p = jnp.exp(s - top)
                    total = total + jnp.sum(p, axis=0, keepdims=True)
                    mixed = mixed + nn(
                        vt[pl.ds(h * HEAD_DIM, HEAD_DIM), pl.ds(first, count)], p.astype(BF)
                    )
                outs.append(mixed / total)
                lse_ref[0, pl.ds(h, 1), at] = top + jnp.log(total)
            o_ref[at, :] = jnp.swapaxes(jnp.concatenate(outs, axis=0), 0, 1).astype(BF)

        @pl.when(qb * QB >= live)
        def _(at=at):
            o_ref[at, :] = jnp.zeros((QB, PAIR), BF)
            lse_ref[0, pl.ds(0, 2), at] = jnp.zeros((2, QB), F32)


def attend_bwd_kernel(causal, start, carried, lens, *refs):
    q_ref, k_ref, v_ref, o_ref, do_ref, lse_ref = refs[:6]
    more, (dq_ref, dk_ref, dv_ref, kt, dk, dv) = refs[6:-6], refs[-6:]
    live, limit = lens[0], lens[1]
    length, key_count = q_ref.shape[0], k_ref.shape[0]
    kt[...] = jnp.swapaxes(k_ref[...].astype(F32), 0, 1).astype(BF)
    if carried < key_count:
        fresh = pl.ds(carried, key_count - carried)
        dk[fresh, :] = jnp.zeros((key_count - carried, PAIR), F32)
        dv[fresh, :] = jnp.zeros((key_count - carried, PAIR), F32)
    if carried:
        dk[pl.ds(0, carried), :] = more[0][...]
        dv[pl.ds(0, carried), :] = more[1][...]
    for block in range(length // QB):
        at = pl.ds(block * QB, QB)
        qb = start // QB + block

        @pl.when(qb * QB < live)
        def _(qb=qb, at=at):
            query = q_ref[at, :] * jnp.asarray(SCALE, BF)
            grad = do_ref[at, :]
            inner = jnp.swapaxes(o_ref[at, :].astype(F32) * grad.astype(F32), 0, 1)
            parts = masks(causal, key_count, qb, limit)
            sums = [[0.0, 0.0] for _ in parts]
            outs = []
            for h in range(2):
                mine = head_lanes(query, h)
                grad_mine = head_lanes(grad, h)
                lse = lse_ref[0, pl.ds(h, 1), at]
                delta = jnp.sum(inner[h * HEAD_DIM : (h + 1) * HEAD_DIM], axis=0, keepdims=True)
                grad_query = 0.0
                for i, (first, count, mask) in enumerate(parts):
                    keys = pl.ds(first, count)
                    p = jnp.exp(nt(k_ref[keys, :], mine) - lse)
                    if mask is not None:
                        p = jnp.where(mask, p, 0.0)
                    dp = nt(v_ref[keys, :], grad_mine)
                    ds = (p * (dp - delta)).astype(BF)
                    sums[i][0] = sums[i][0] + nn(ds, mine)
                    sums[i][1] = sums[i][1] + nn(p.astype(BF), grad_mine)
                    grad_query = grad_query + nn(kt[pl.ds(h * HEAD_DIM, HEAD_DIM), keys], ds)
                outs.append(grad_query * SCALE)
            for (first, count, _), (sum_k, sum_v) in zip(parts, sums):
                dk[pl.ds(first, count), :] += sum_k
                dv[pl.ds(first, count), :] += sum_v
            dq_ref[at, :] = jnp.swapaxes(jnp.concatenate(outs, axis=0), 0, 1).astype(BF)

        @pl.when(qb * QB >= live)
        def _(at=at):
            dq_ref[at, :] = jnp.zeros((QB, PAIR), BF)

    dk_ref[...] = dk[...].astype(dk_ref.dtype)
    dv_ref[...] = dv[...].astype(dv_ref.dtype)


def columns(rows, first, row_block=0):
    at = first if callable(first) else lambda g: first + g
    return pl.BlockSpec((rows, PAIR), lambda g, lens: (row_block, at(g)))


def attend_forward(query, keys, values, lens, causal, start, length, key_count, pairs):
    (qa, q0, rows), (ka, k0), (va, v0) = query, keys, values
    return pl.pallas_call(
        functools.partial(attend_fwd_kernel, causal, start),
        grid_spec=pltpu.PrefetchScalarGridSpec(
            num_scalar_prefetch=1,
            grid=(pairs,),
            in_specs=[
                columns(length, q0, rows),
                columns(key_count, k0),
                columns(key_count, v0),
            ],
            out_specs=[
                columns(length, 0),
                pl.BlockSpec((1, 2, length), lambda g, lens: (g, 0, 0)),
            ],
            scratch_shapes=[pltpu.VMEM((PAIR, key_count), BF)],
        ),
        out_shape=[
            jax.ShapeDtypeStruct((length, pairs * PAIR), BF),
            jax.ShapeDtypeStruct((pairs, 2, length), F32),
        ],
        compiler_params=pltpu.CompilerParams(vmem_limit_bytes=24 * 2**20),
        cost_estimate=BRIEF,
        name="attend_causal" if causal else "attend_memory",
    )(lens, qa, ka, va)


def attend_backward(
    query, keys, values, mixed, grad, lse, lens, causal, start, length, key_count, pairs, carried, last
):
    (qa, q0, rows), (ka, k0), (va, v0) = query, keys, values
    had = carried[0].shape[0] if carried else 0
    kept = BF if last else F32
    return pl.pallas_call(
        functools.partial(attend_bwd_kernel, causal, start, had),
        grid_spec=pltpu.PrefetchScalarGridSpec(
            num_scalar_prefetch=1,
            grid=(pairs,),
            in_specs=[
                columns(length, q0, rows),
                columns(key_count, k0),
                columns(key_count, v0),
                columns(length, mixed[1]),
                columns(length, grad[1]),
                pl.BlockSpec((1, 2, length), lambda g, lens: (mixed[1] + g, 0, 0)),
            ]
            + [columns(had, 0)] * (2 if carried else 0),
            out_specs=[columns(length, 0), columns(key_count, 0), columns(key_count, 0)],
            scratch_shapes=[
                pltpu.VMEM((PAIR, key_count), BF),
                pltpu.VMEM((key_count, PAIR), F32),
                pltpu.VMEM((key_count, PAIR), F32),
            ],
        ),
        out_shape=[
            jax.ShapeDtypeStruct((length, pairs * PAIR), BF),
            jax.ShapeDtypeStruct((key_count, pairs * PAIR), kept),
            jax.ShapeDtypeStruct((key_count, pairs * PAIR), kept),
        ],
        compiler_params=pltpu.CompilerParams(vmem_limit_bytes=32 * 2**20),
        cost_estimate=BRIEF,
        name="attend_causal_back" if causal else "attend_memory_back",
    )(lens, qa, ka, va, mixed[0], grad[0], lse, *(carried or ()))


def normed(value, gain):
    scale = lax.rsqrt(jnp.mean(value * value, axis=-1, keepdims=True) + EPS)
    return value * scale * gain


def norm_back(value, gain, grad):
    scale = lax.rsqrt(jnp.mean(value * value, axis=-1, keepdims=True) + EPS)
    unit = value * scale
    scaled = grad * gain
    inner = jnp.mean(scaled * unit, axis=-1, keepdims=True)
    return scale * (scaled - unit * inner), jnp.sum(grad * unit, axis=0, keepdims=True)


def enter_kernel(x_ref, w0_ref, w1_ref, columns_ref, h_ref, qkv_ref, gain_ref):
    rows = jnp.swapaxes(columns_ref[...].astype(F32), 0, 1)
    gain_ref[...] = rows[:8]
    h = normed(x_ref[...].astype(F32), rows[0:1]).astype(BF)
    h_ref[...] = h
    wide = w0_ref.shape[1]
    qkv_ref[:, pl.ds(0, wide)] = nn(h, w0_ref[...]).astype(BF)
    qkv_ref[:, pl.ds(wide, wide)] = nn(h, w1_ref[...]).astype(BF)


def middle_kernel(x_ref, o_ref, gain_ref, wo_ref, cq_ref, x1_ref, h_ref, q_ref):
    x1 = x_ref[...].astype(F32) + nn(o_ref[...], wo_ref[...])
    h = normed(x1, gain_ref[1:2]).astype(BF)
    x1_ref[...] = x1
    h_ref[...] = h
    q_ref[...] = nn(h, cq_ref[...]).astype(BF)


def outer_kernel(x1_ref, o_ref, gain_ref, co_ref, x2_ref, h_ref):
    x2 = x1_ref[...] + nn(o_ref[...], co_ref[...])
    x2_ref[...] = x2
    h_ref[...] = normed(x2, gain_ref[2:3]).astype(BF)


def add_gain(step, ref, value):
    @pl.when(step == 0)
    def _():
        ref[...] = jnp.zeros_like(ref)

    ref[0:1, :] += value


def outer_back_kernel(dh_ref, x2_ref, g_ref, gain_ref, co_ref, d_ref, dx_ref, do_ref, dgain_ref):
    dx, dgain = norm_back(x2_ref[...], gain_ref[2:3], dh_ref[...].astype(F32))
    dx = g_ref[...].astype(F32) + dx
    d = dx.astype(BF)
    dx_ref[...] = dx
    d_ref[...] = d
    do_ref[...] = nt(d, co_ref[...]).astype(BF)
    add_gain(pl.program_id(0), dgain_ref, dgain)


def middle_back_kernel(
    dq_ref, x1_ref, dx2_ref, gain_ref, cq_ref, wo_ref, dx_ref, d_ref, do_ref, dgain_ref
):
    dx, dgain = norm_back(x1_ref[...], gain_ref[1:2], nt(dq_ref[...], cq_ref[...]))
    dx = dx2_ref[...] + dx
    d = dx.astype(BF)
    dx_ref[...] = dx
    d_ref[...] = d
    do_ref[...] = nt(d, wo_ref[...]).astype(BF)
    add_gain(pl.program_id(0), dgain_ref, dgain)


def enter_back_kernel(x_ref, dx1_ref, *refs):
    grads, gain_ref, weights, (out_ref, dgain_ref) = refs[:3], refs[3], refs[4:10], refs[10:]
    dh = 0.0
    for i, grad in enumerate(grads):
        for g in range(2):
            w = weights[2 * i + g]
            at = pl.ds(g * w.shape[1], w.shape[1])
            dh = dh + nt(grad[:, at], w[...])
    dx, dgain = norm_back(x_ref[...].astype(F32), gain_ref[0:1], dh)
    out_ref[...] = (dx1_ref[...] + dx).astype(BF)
    add_gain(pl.program_id(0), dgain_ref, dgain)


def by_tokens(kernel, tokens, blocked, whole, outs, name, c=0, kept=None):
    width = blocked[0][0].shape[1]
    steps = tokens // QB
    full = tokens if kept is None else 2 * tokens

    def rows(n, first):
        return pl.BlockSpec((QB, n), lambda i, first=first: (first + i, 0))

    def fixed(shape, index):
        return pl.BlockSpec(shape, lambda i, index=index: index)

    kept = kept or ()
    inputs = len(blocked) + len(whole)

    def run(*refs):
        kernel(*refs[:inputs], *refs[inputs + len(kept) :])

    return pl.pallas_call(
        run,
        grid=(steps,),
        in_specs=[rows(a.shape[1], first) for a, first in blocked]
        + [fixed(shape, index) for _, shape, index in whole]
        + [pl.BlockSpec(memory_space=pl.ANY)] * len(kept),
        out_specs=[
            fixed((8, width), (0, 0)) if n is None else rows(n, c * steps) for n, _ in outs
        ],
        out_shape=[
            jax.ShapeDtypeStruct((8, width) if n is None else (full, n), dtype)
            for n, dtype in outs
        ],
        input_output_aliases={inputs + i: i for i in range(len(kept))},
        compiler_params=pltpu.CompilerParams(vmem_limit_bytes=24 * 2**20),
        cost_estimate=BRIEF,
        name=name,
    )(*[a for a, _ in blocked], *[a for a, _, _ in whole], *kept)


def weight_grad_kernel(x_ref, g_ref, o_ref):
    o_ref[...] = tn(x_ref[...], g_ref[...]).astype(BF)


def weight_grad(x, grad, columns_at_once):
    tokens, rows = x.shape
    width = grad.shape[1]
    return pl.pallas_call(
        weight_grad_kernel,
        grid=(rows // columns_at_once,),
        in_specs=[
            pl.BlockSpec((tokens, columns_at_once), lambda i: (0, i)),
            pl.BlockSpec((tokens, width), lambda i: (0, 0)),
        ],
        out_specs=pl.BlockSpec((columns_at_once, width), lambda i: (i, 0)),
        out_shape=jax.ShapeDtypeStruct((rows, width), BF),
        compiler_params=pltpu.CompilerParams(vmem_limit_bytes=40 * 2**20),
        cost_estimate=BRIEF,
        name="weight_grad",
    )(x, grad)


GELU_A = 0.7978845608028654
GELU_B = 0.044715


def feed_kernel(groups, ff, step, *refs):
    h_refs, g_refs, (gu_ref, down_ref) = refs[:groups], refs[groups : 2 * groups], refs[2 * groups : 2 * groups + 2]
    outs = refs[-2 * groups - 4 :]
    y_refs, dh_refs, (hid_ref, dgu_ref, h_ref, g_ref) = outs[:groups], outs[groups:-4], outs[-4:]
    part = h_refs[0].shape[0]
    for j in range(groups):
        h_ref[pl.ds(j * part, part), :] = h_refs[j][...]
        g_ref[pl.ds(j * part, part), :] = g_refs[j][0]
    y, dh = 0.0, 0.0
    for c in range(0, ff, step):
        wg = gu_ref[:, pl.ds(c, step)]
        wu = gu_ref[:, pl.ds(ff + c, step)]
        wd = down_ref[pl.ds(c, step), :]
        gate, up, dhid = nn(h_ref[...], wg), nn(h_ref[...], wu), nt(g_ref[...], wd)
        square = gate * gate
        th = jnp.tanh(gate * (GELU_A + (GELU_A * GELU_B) * square))
        half = 0.5 + 0.5 * th
        act = gate * half
        slope = half + (0.5 * gate) * (1.0 - th * th) * (
            GELU_A + (3.0 * GELU_A * GELU_B) * square
        )
        hidden = (act * up).astype(BF)
        dgate = (dhid * up * slope).astype(BF)
        dup = (dhid * act).astype(BF)
        hid_ref[:, pl.ds(c, step)] = hidden
        dgu_ref[:, pl.ds(c, step)] = dgate
        dgu_ref[:, pl.ds(ff + c, step)] = dup
        y = y + nn(hidden, wd)
        dh = dh + nt(dgate, wg) + nt(dup, wu)
    for j in range(groups):
        y_refs[j][0] = y[j * part : (j + 1) * part].astype(BF)
        dh_refs[j][...] = dh[j * part : (j + 1) * part].astype(BF)


def feed(c, h_parts, g_parts, wgu, wd, kept):
    groups = len(h_parts)
    part, width = h_parts[0].shape
    ff = wd.shape[0]
    tokens = groups * part

    def whole(a):
        return pl.BlockSpec(a.shape, lambda i: (0,) * a.ndim)

    def halves(n):
        return pl.BlockSpec((tokens, n), lambda i: (c, 0))

    wide = (ff, 2 * ff, width, width)
    of_half = pl.BlockSpec((1, part, width), lambda i: (c, 0, 0))
    made = [0 + i for i in range(groups)] + [2 * groups + i for i in range(len(wide))]
    return pl.pallas_call(
        functools.partial(feed_kernel, groups, ff, 512),
        grid=(1,),
        in_specs=[whole(h) for h in h_parts]
        + [of_half] * groups
        + [whole(wgu), whole(wd)]
        + [pl.BlockSpec(memory_space=pl.ANY)] * len(kept),
        out_specs=[of_half] * groups
        + [whole(h) for h in h_parts]
        + [halves(n) for n in wide],
        out_shape=[jax.ShapeDtypeStruct((2, part, width), BF)] * groups
        + [jax.ShapeDtypeStruct((part, width), BF)] * groups
        + [jax.ShapeDtypeStruct((2 * tokens, n), BF) for n in wide],
        input_output_aliases={2 * groups + 2 + i: made[i] for i in range(len(kept))},
        compiler_params=pltpu.CompilerParams(vmem_limit_bytes=VMEM),
        cost_estimate=BRIEF,
        name="feed",
    )(*h_parts, *g_parts, wgu, wd, *kept)


def pick_kernel(modes, halves, source, mode, x_ref, *o_refs):
    per_mode = x_ref.shape[0] // modes
    for j in range(modes):
        first = jnp.bitwise_xor(mode[0], j) * per_mode

        def move(r, carry, j=j, first=first):
            row = source[first + r]
            if halves:
                for c in range(halves):
                    o_refs[j][c, r] = x_ref[row, c]
            else:
                o_refs[j][r] = x_ref[row]
            return carry

        lax.fori_loop(0, per_mode, move, 0)


def put_kernel(modes, halves, source, mode, *refs):
    o_ref = refs[-1]
    per_mode = o_ref.shape[0] // modes
    for j in range(modes):
        first = jnp.bitwise_xor(mode[0], j) * per_mode

        def move(r, carry, j=j, first=first):
            row = source[first + r]
            if halves:
                for c in range(halves):
                    o_ref[row, c] = refs[j][c, r]
            else:
                o_ref[row] = refs[j][r]
            return carry

        lax.fori_loop(0, per_mode, move, 0)


def mode_number():
    return lax.axis_index("mode").astype(jnp.int32)[None]


def by_rows(kernel, source, ins, outs, name):
    def whole(shape):
        return pl.BlockSpec(shape, lambda i, source, mode: (0,) * len(shape))

    return pl.pallas_call(
        kernel,
        grid_spec=pltpu.PrefetchScalarGridSpec(
            num_scalar_prefetch=2,
            grid=(1,),
            in_specs=[whole(a.shape) for a in ins],
            out_specs=[whole(shape) for shape in outs],
        ),
        out_shape=[jax.ShapeDtypeStruct(shape, BF) for shape in outs],
        compiler_params=pltpu.CompilerParams(vmem_limit_bytes=16 * 2**20),
        cost_estimate=pl.CostEstimate(
            flops=0, bytes_accessed=4 * sum(a.size for a in ins), transcendentals=0
        ),
        name=name,
    )(source, mode_number(), *ins)


def to_mode(spread, source):
    per_mode, modes = lax.axis_size("dp"), lax.axis_size("mode")
    piece = spread.shape[-2:]
    if spread.ndim == 4:
        outs = [(spread.shape[1], per_mode) + piece] * modes
    else:
        outs = [(per_mode,) + piece] * modes
    parts = by_rows(
        functools.partial(pick_kernel, modes, spread.shape[1] if spread.ndim == 4 else 0),
        source,
        [spread],
        outs,
        "pick",
    )
    got = [parts[0]] + [swap(parts[j], per_mode * j) for j in range(1, modes)]
    if spread.ndim == 4:
        return [part.reshape(part.shape[0], -1, part.shape[-1]) for part in got]
    return [part.reshape(-1, part.shape[-1]) for part in got]


def swap_modes(parts):
    per_mode = lax.axis_size("dp")
    lead = parts[0].shape[:-2]
    parts = [part.reshape(lead + (per_mode, -1, part.shape[-1])) for part in parts]
    return [parts[0]] + [swap(parts[j], per_mode * j) for j in range(1, len(parts))]


def put_back(parts, source):
    halves = parts[0].shape[0] if parts[0].ndim == 4 else 0
    shape = (lax.axis_size(ALL),) + ((halves,) if halves else ()) + parts[0].shape[-2:]
    return by_rows(
        functools.partial(put_kernel, len(parts), halves), source, parts, [shape], "put"
    )[0]


def dealt(value):
    count = lax.axis_size(ALL)
    return value.reshape(count, -1, value.shape[-1])


def to_all(value):
    return lax.all_to_all(value, ALL, 0, 0, tiled=True)


def swap(value, j):
    count = lax.axis_size(ALL)
    return lax.ppermute(value, ALL, [(i, i ^ j) for i in range(count)])


def device_number():
    return lax.axis_index(ALL).astype(jnp.int32)[None]


def place_kernel(me, even_ref, odd_ref, *o_refs):
    first = 0
    for o_ref in o_refs:
        at = pl.ds(first, o_ref.shape[2])
        first += o_ref.shape[2]
        for t in range(even_ref.shape[0]):
            o_ref[jnp.bitwise_xor(2 * t, me[0])] = even_ref[t, :, at]
            o_ref[jnp.bitwise_xor(2 * t + 1, me[0])] = odd_ref[t, :, at]


def place(even, odd, widths, number):
    count, rows, width = even.shape
    shapes = [(2 * count, rows, w) for w in widths]

    def whole(shape):
        return pl.BlockSpec(shape, lambda i, me: (0, 0, 0))

    return pl.pallas_call(
        place_kernel,
        grid_spec=pltpu.PrefetchScalarGridSpec(
            num_scalar_prefetch=1,
            grid=(1,),
            in_specs=[whole(even.shape)] * 2,
            out_specs=[whole(shape) for shape in shapes],
        ),
        out_shape=[jax.ShapeDtypeStruct(shape, even.dtype) for shape in shapes],
        compiler_params=pltpu.CompilerParams(vmem_limit_bytes=28 * 2**20),
        cost_estimate=BRIEF,
        name="place",
    )(number, even, odd)


def pack_kernel(counts, *refs):
    ins, outs = refs[: sum(counts)], refs[sum(counts) :]
    taken = 0
    for count, o_ref in zip(counts, outs):
        first = 0
        for part in ins[taken : taken + count]:
            o_ref[:, pl.ds(first, part.shape[1])] = part[...]
            first += part.shape[1]
        taken += count


def pack(*lists):
    cut = lambda e: e if not isinstance(e, tuple) else e[0]
    shape = lambda e: e.shape if not isinstance(e, tuple) else (e[0].shape[0], e[2])
    at = lambda e: 0 if not isinstance(e, tuple) else e[1] // e[2]
    entries = [e for group in lists for e in group]
    return pl.pallas_call(
        functools.partial(pack_kernel, [len(group) for group in lists]),
        grid=(1,),
        in_specs=[pl.BlockSpec(shape(e), lambda i, e=e: (0, at(e))) for e in entries],
        out_specs=[
            pl.BlockSpec((shape(group[0])[0], sum(shape(e)[1] for e in group)), lambda i: (0, 0))
            for group in lists
        ],
        out_shape=[
            jax.ShapeDtypeStruct((shape(group[0])[0], sum(shape(e)[1] for e in group)), BF)
            for group in lists
        ],
        name="pack",
    )(*[cut(e) for e in entries])


def gather_column(piece, late=None):
    per_mode = lax.axis_size("dp")
    got = [swap(piece, 2 * j) for j in range(1, per_mode // 2)]
    return jnp.stack([piece] + (got if late is None else tied(got, late)))


def gather_rest(column, widths, late=None):
    per_mode, modes = lax.axis_size("dp"), lax.axis_size("mode")
    got = [swap(column, per_mode * j) for j in range(1, modes)]
    if late is not None:
        got = tied(got, late)
    plane = jnp.stack([column] + got)
    plane = plane.reshape((-1,) + column.shape[1:])
    placed = place(plane, swap(plane, 1), widths, device_number())
    return [a.reshape(-1, a.shape[2]) for a in placed]


def take_kernel(parts, me, *refs):
    ins, (keep_ref, send_ref) = refs[:parts], refs[parts:]
    first = 0
    for in_ref in ins:
        at = pl.ds(first, in_ref.shape[2])
        first += in_ref.shape[2]
        for t in range(keep_ref.shape[0]):
            keep_ref[t, :, at] = in_ref[jnp.bitwise_xor(2 * t, me[0])]
            send_ref[t, :, at] = in_ref[jnp.bitwise_xor(2 * t + 1, me[0])]


def take(parts):
    count, rows = parts[0].shape[:2]
    width = sum(part.shape[2] for part in parts)
    half = jax.ShapeDtypeStruct((count // 2, rows, width), parts[0].dtype)

    def whole(shape):
        return pl.BlockSpec(shape, lambda i, me: (0, 0, 0))

    return pl.pallas_call(
        functools.partial(take_kernel, len(parts)),
        grid_spec=pltpu.PrefetchScalarGridSpec(
            num_scalar_prefetch=1,
            grid=(1,),
            in_specs=[whole(part.shape) for part in parts],
            out_specs=[whole(half.shape)] * 2,
        ),
        out_shape=[half, half],
        compiler_params=pltpu.CompilerParams(vmem_limit_bytes=48 * 2**20),
        cost_estimate=BRIEF,
        name="take",
    )(device_number(), *parts)


def add_up(parts):
    return functools.reduce(jnp.add, [part.astype(F32) for part in parts])


def scatter_pairs(parts):
    count = lax.axis_size(ALL)
    parts = [part.reshape(count, part.shape[0] // count, part.shape[1]) for part in parts]
    keep, send = take(parts)
    return add_up([keep, swap(send, 1)]).astype(BF)


def scatter_plane(pair):
    per_mode, modes = lax.axis_size("dp"), lax.axis_size("mode")
    plane = pair.reshape((modes, per_mode // 2) + pair.shape[1:])
    return add_up([plane[0]] + [swap(plane[j], per_mode * j) for j in range(1, modes)]).astype(BF)


def scatter_column(column):
    per_mode = lax.axis_size("dp")
    return add_up([column[0]] + [swap(column[j], 2 * j) for j in range(1, per_mode // 2)])


def later(lens, tokens):
    return lens - jnp.array([tokens, 0], jnp.int32)


def tied(first, second):
    return lax.optimization_barrier((first, second))[0]


def lanes_of(*vectors):
    columns_ = jnp.stack(vectors, axis=1)
    return jnp.pad(columns_, ((0, 0), (0, 128 - len(vectors))))


def on_device(
    rows,
    memory,
    cotangent,
    mode_ids,
    target_lengths,
    encoder_lengths,
    self_q,
    self_k,
    self_v,
    self_o,
    self_gain,
    cross_q,
    cross_k,
    cross_v,
    cross_o,
    cross_gain,
    ffn_gain,
    ffn_gate,
    ffn_up,
    ffn_down,
):
    devices = lax.axis_size(ALL)
    per_mode = lax.axis_size("dp")
    here = lax.axis_index(ALL)
    width = rows.shape[2]
    ff = ffn_gate.shape[2]
    index = jnp.arange(devices, dtype=jnp.int32)
    same = mode_ids[:, None] == mode_ids[None, :]
    earlier = index[None, :] < index[:, None]
    rank = jnp.sum(jnp.where(same & earlier, 1, 0), axis=1).astype(jnp.int32)
    target = mode_ids * per_mode + rank
    source = jnp.sum(
        jnp.where(target[:, None] == index[None, :], index[:, None], 0), axis=0
    ).astype(jnp.int32)
    live_len = jnp.sum(jnp.where(index == here, target_lengths, 0))
    memory_len = jnp.sum(jnp.where(index == here, encoder_lengths, 0))
    lens = jnp.stack([live_len, memory_len]).astype(jnp.int32)
    tokens, memory_row, incoming = rows[0], memory[0], cotangent[0]
    length = tokens.shape[0]
    half = length // 2
    key_count = memory_row.shape[0]
    valid = (jnp.arange(length, dtype=jnp.int32) < live_len)[:, None]
    grad_low = jnp.where(valid, incoming, jnp.zeros_like(incoming))

    group_pairs = HEADS // 4
    part = group_pairs * PAIR

    def of_group(g):
        return tuple((a, g * part, part) for a in (self_q, self_k, self_v))

    own_piece, rest_piece = pack(
        of_group(0) + of_group(1) + (lanes_of(self_gain, cross_gain, ffn_gain),),
        (self_o, cross_q, cross_k, cross_v, cross_o),
    )
    column = gather_column(own_piece)
    own_0, own_1, gain_columns = gather_rest(column, (3 * part, 3 * part, 128))
    crossing = lax.all_gather(rest_piece, ALL, axis=0, tiled=True)

    def weight(array, i, wide=width):
        return (array, (width, wide), (0, i))

    h1, qkv, gains = by_tokens(
        enter_kernel,
        length,
        [(tokens, 0)],
        [(a, a.shape, (0, 0)) for a in (own_0, own_1, gain_columns)],
        [(width, BF), (6 * part, BF), (None, F32)],
        "enter",
    )
    all_gains = (gains, gains.shape, (0, 0))
    pairs = HEADS // 2

    def of_pair(i):
        return lambda g: (g // group_pairs) * 3 * group_pairs + i * group_pairs + g % group_pairs

    grad_dealt = grad_low.reshape(2, devices, -1, width).swapaxes(0, 1)
    grad_spread = to_all(tied(grad_dealt, h1))

    wgu = lax.all_gather(
        jnp.concatenate([ffn_gate[0], ffn_up[0]], axis=1), "dp", axis=0, tiled=True
    )
    wd = lax.all_gather(ffn_down[0], "dp", axis=0, tiled=True)

    mixed, log_self = attend_forward(
        (qkv, of_pair(0), 0),
        (qkv, of_pair(1)),
        (qkv, of_pair(2)),
        lens,
        True,
        0,
        length,
        length,
        pairs,
    )
    wo, cq, ckv, co = (
        crossing[:, i * width : j * width] for i, j in ((0, 1), (1, 2), (2, 4), (4, 5))
    )

    def forward_middle(c):
        first = c * (half // QB)
        return by_tokens(
            middle_kernel,
            half,
            [(tokens, first), (mixed, first)],
            [all_gains, weight(wo, 0), weight(cq, 0)],
            [(width, F32), (width, BF), (width, BF)],
            "middle",
        )

    def forward_cross(c, query):
        return attend_forward(
            (query, 0, 0),
            (cross_kv, 0),
            (cross_kv, pairs),
            later(lens, c * half),
            False,
            0,
            half,
            key_count,
            pairs,
        )

    def forward_outer(x1, cross_mixed):
        return by_tokens(
            outer_kernel,
            half,
            [(x1, 0), (cross_mixed, 0)],
            [all_gains, weight(co, 0)],
            [(width, F32), (width, BF)],
            "outer",
        )

    x1_a, h2_a, query_a = forward_middle(0)
    cross_kv = nn(memory_row, ckv).astype(BF)
    cross_a, log_cross_a = forward_cross(0, query_a)
    x2_a, h3_a = forward_outer(x1_a, cross_a)
    spread_a = to_all(dealt(tied(h3_a, grad_spread)))
    grad_parts = to_mode(grad_spread, source)
    x1_b, h2_b, query_b = forward_middle(1)
    query_b = tied(query_b, h3_a)
    cross_b, log_cross_b = forward_cross(1, query_b)
    cross_b, grad_parts = lax.optimization_barrier((cross_b, grad_parts))
    x2_b, h3_b = forward_outer(x1_b, cross_b)
    routed_a = to_mode(tied(spread_a, cross_b), source)
    spread_b = to_all(dealt(h3_b))

    modes = len(routed_a)
    fed_a = feed(0, tied(routed_a, h3_b), grad_parts, wgu, wd, ())
    y_a, dh_a, kept_a = fed_a[:modes], fed_a[modes : 2 * modes], fed_a[2 * modes :]
    back_a = put_back(swap_modes(dh_a), source)
    routed_b = to_mode(tied(spread_b, dh_a[0]), source)
    routed_b, back_a = lax.optimization_barrier((routed_b, back_a))
    home_a = to_all(back_a)
    fed_b = feed(1, routed_b, grad_parts, wgu, wd, y_a + kept_a)
    home_a = home_a.reshape(half, width)
    y, dh_b = fed_b[:modes], fed_b[modes : 2 * modes]
    hidden, dgu, routed_h, routed_grad = fed_b[2 * modes :]
    back_b = swap_modes(dh_b)
    grad_wd = weight_grad(tied(hidden, home_a), routed_grad, 512)
    back_b = put_back(tied(back_b, grad_wd), source)
    grad_wgu = weight_grad(routed_h, tied(dgu, back_b), 256)
    sum_wgu = lax.psum_scatter(grad_wgu, "dp", scatter_dimension=0, tiled=True)
    sum_wd = lax.psum_scatter(grad_wd, "dp", scatter_dimension=0, tiled=True)
    home_b = to_all(back_b).reshape(half, width)
    home_a = tied(home_a, grad_wgu)
    y_mode = swap_modes(tied(y, back_b))

    def back_outer(c, dh, x2):
        return by_tokens(
            outer_back_kernel,
            half,
            [(dh, 0), (x2, 0), (grad_low, c * (half // QB))],
            [all_gains, weight(co, 0)],
            [(width, BF), (width, F32), (width, BF), (None, F32)],
            "outer_back",
        )

    def back_middle(c, dq, x1, dx2, kept):
        return by_tokens(
            middle_back_kernel,
            half,
            [(dq, 0), (x1, 0), (dx2, 0)],
            [all_gains, weight(cq, 0), weight(wo, 0)],
            [(width, F32), (width, BF), (width, BF), (None, F32)],
            "middle_back",
            c,
            kept,
        )

    def back_cross(c, query, mixed, grad, lse, carried):
        return attend_backward(
            (query, 0, 0),
            (cross_kv, 0),
            (cross_kv, pairs),
            (mixed, 0),
            (grad, 0),
            lse,
            later(lens, c * half),
            False,
            0,
            half,
            key_count,
            pairs,
            carried,
            c == 1,
        )

    def back_self(grad):
        return attend_backward(
            (qkv, of_pair(0), 0),
            (qkv, of_pair(1)),
            (qkv, of_pair(2)),
            (mixed, 0),
            (grad, 0),
            log_self,
            lens,
            True,
            0,
            length,
            length,
            pairs,
            None,
            True,
        )

    d2_a, dx2_a, do2_a, dgain_ffn_a = back_outer(0, home_a, x2_a)
    dcq_a, dck_a, dcv_a = back_cross(0, query_a, cross_a, do2_a, log_cross_a, None)
    *halves, dgain_cross_a = back_middle(0, dcq_a, x1_a, dx2_a, ())
    home_b, y_mode = lax.optimization_barrier((tied(home_b, halves), y_mode))
    d2_b, dx2_b, do2_b, dgain_ffn_b = back_outer(1, home_b, x2_b)
    y_put, do2_b = lax.optimization_barrier((put_back(y_mode, source), do2_b))
    y_home = to_all(y_put)
    dcq_b, dck, dcv = back_cross(1, query_b, cross_b, do2_b, log_cross_b, (dck_a, dcv_a))
    dx1, d1, do1, dgain_cross_b = back_middle(1, dcq_b, x1_b, dx2_b, halves)
    cross_pair = scatter_pairs(
        [
            (tn(h2_a, dcq_a) + tn(h2_b, dcq_b)).astype(BF),
            tn(memory_row, dck).astype(BF),
            tn(memory_row, dcv).astype(BF),
            (tn(cross_a, d2_a) + tn(cross_b, d2_b)).astype(BF),
            tn(mixed, d1).astype(BF),
        ]
    )
    do1, cross_pair = lax.optimization_barrier((do1, cross_pair))
    cross_plane = scatter_plane(cross_pair)
    grads = back_self(do1)
    grads, cross_plane, y_home, sum_wgu, sum_wd = lax.optimization_barrier(
        (grads, cross_plane, y_home, sum_wgu, sum_wd)
    )
    cross_sum = scatter_column(cross_plane)
    own_pair = scatter_pairs([tn(h1, d).astype(BF) for d in grads])
    own_plane = scatter_plane(own_pair)
    grads, dck, dcv = tied((grads, dck, dcv), own_pair)
    y_home = tied(y_home, own_plane)
    grad_tokens, dgain_self = by_tokens(
        enter_back_kernel,
        length,
        [(tokens, 0), (dx1, 0)] + [(d, 0) for d in grads],
        [all_gains] + [weight(own, i, part) for i in range(3) for own in (own_0, own_1)],
        [(width, BF), (None, F32)],
        "enter_back",
    )
    gain_grads = jnp.stack(
        [dgain_self[0], dgain_cross_a[0] + dgain_cross_b[0], dgain_ffn_a[0] + dgain_ffn_b[0]]
    )
    own_plane, gain_grads = lax.optimization_barrier((own_plane, gain_grads))
    own_sum = scatter_column(own_plane)
    gain_grads = gain_grads.reshape(3, devices, -1).swapaxes(0, 1)
    gain_sums = jnp.sum(to_all(gain_grads), axis=0)
    grad_memory = (nt(dck, ckv[:, :width]) + nt(dcv, ckv[:, width:])).astype(BF)
    y = y_home.swapaxes(0, 1).reshape(length, width)
    result = jnp.where(valid, jnp.concatenate([x2_a, x2_b]) + y.astype(F32), 0.0).astype(BF)

    def block(value, i):
        return value[:, i * width : (i + 1) * width]

    return (
        result[None],
        grad_tokens[None],
        grad_memory[None],
        block(own_sum, 0),
        block(own_sum, 1),
        block(own_sum, 2),
        block(cross_sum, 4),
        gain_sums[0],
        block(cross_sum, 0),
        block(cross_sum, 1),
        block(cross_sum, 2),
        block(cross_sum, 3),
        gain_sums[1],
        gain_sums[2],
        sum_wgu[:, :ff].astype(F32)[None],
        sum_wgu[:, ff:].astype(F32)[None],
        sum_wd.astype(F32)[None],
    )


def solution(mesh):
    rows = P(ALL, None, None)
    weight = P(ALL, None)
    gain = P(ALL)
    feeding = P("mode", "dp", None)
    return jax.shard_map(
        on_device,
        mesh=mesh,
        in_specs=(
            (rows,) * 3
            + (P(),) * 3
            + (weight,) * 4
            + (gain,)
            + (weight,) * 4
            + (gain,) * 2
            + (feeding,) * 3
        ),
        out_specs=(
            (rows,) * 3
            + (weight,) * 4
            + (gain,)
            + (weight,) * 4
            + (gain,) * 2
            + (feeding,) * 3
        ),
        check_vma=False,
    )
```

```python
import functools

import jax
import jax.numpy as jnp
from jax import lax
from jax.experimental import pallas as pl
from jax.experimental.pallas import tpu as pltpu
from jax.sharding import PartitionSpec as P

HEADS = 12
HEAD_DIM = 64
PAIR = 2 * HEAD_DIM
EPS = 1e-06
NEG = -1e30
SCALE = HEAD_DIM ** -0.5
QB = 256
AB = 512
ALL = ("mode", "dp")
BF = jnp.bfloat16
F32 = jnp.float32
VMEM = 56 * 2**20
BRIEF = pl.CostEstimate(flops=10**6, bytes_accessed=10**4, transcendentals=0)


def nt(left, right):
    return lax.dot_general(left, right, (((1,), (1,)), ((), ())), preferred_element_type=F32)


def nn(left, right):
    return jnp.dot(left, right, preferred_element_type=F32)


def tn(left, right):
    return lax.dot_general(left, right, (((0,), (0,)), ((), ())), preferred_element_type=F32)


def head_lanes(value, h):
    lane = lax.broadcasted_iota(jnp.int32, value.shape, 1)
    return jnp.where((lane >= HEAD_DIM) == (h == 1), value, jnp.zeros_like(value))


def masks(causal, key_count, qb, limit):
    if causal:
        parts = []
        if qb:
            parts.append((0, qb * AB, None))
        row = lax.broadcasted_iota(jnp.int32, (AB, AB), 0)
        col = lax.broadcasted_iota(jnp.int32, (AB, AB), 1)
        parts.append((qb * AB, AB, row <= col))
        return parts
    row = lax.broadcasted_iota(jnp.int32, (key_count, AB), 0)
    return [(0, key_count, row < limit)]


def attend_fwd_kernel(causal, lens, q_ref, k_ref, v_ref, o_ref, lse_ref):
    live, limit = lens[0], lens[1]
    length, key_count = q_ref.shape[0], k_ref.shape[0]
    block = min(AB, length)
    first_head = lax.broadcasted_iota(jnp.int32, (1, PAIR), 1) < HEAD_DIM
    for start in range(0, length, block):
        at = pl.ds(start, block)

        @pl.when(start < live)
        def _(start=start, at=at):
            query = q_ref[at, :] * jnp.asarray(SCALE, BF)
            if causal:
                row = lax.broadcasted_iota(jnp.int32, (block, block), 0)
                col = lax.broadcasted_iota(jnp.int32, (block, block), 1)
                parts = [(0, start, None)] if start else []
                parts.append((start, block, col <= row))
            else:
                col = lax.broadcasted_iota(jnp.int32, (block, key_count), 1)
                parts = [(0, key_count, col < limit)]
            outs, logs = [], []
            for h in range(2):
                mine = head_lanes(query, h)
                scores = []
                for first, count, mask in parts:
                    s = nt(mine, k_ref[pl.ds(first, count), :])
                    scores.append(s if mask is None else jnp.where(mask, s, NEG))
                top = functools.reduce(
                    jnp.maximum, [jnp.max(s, axis=1, keepdims=True) for s in scores]
                )
                total, mixed = 0.0, 0.0
                for (first, count, _), s in zip(parts, scores):
                    p = jnp.exp(s - top)
                    total = total + jnp.sum(p, axis=1, keepdims=True)
                    mixed = mixed + nn(p.astype(BF), v_ref[pl.ds(first, count), :])
                outs.append(mixed / total)
                logs.append(top + jnp.log(total))
            o_ref[at, :] = jnp.where(first_head, outs[0], outs[1]).astype(BF)
            rows = jnp.swapaxes(jnp.where(first_head, logs[0], logs[1]), 0, 1)
            lse_ref[0, pl.ds(0, 1), at] = rows[0:1]
            lse_ref[0, pl.ds(1, 1), at] = rows[HEAD_DIM : HEAD_DIM + 1]

        @pl.when(start >= live)
        def _(at=at):
            o_ref[at, :] = jnp.zeros((block, PAIR), BF)
            lse_ref[0, pl.ds(0, 2), at] = jnp.zeros((2, block), F32)


def attend_bwd_kernel(causal, start, carried, lens, *refs):
    q_ref, k_ref, v_ref, o_ref, do_ref, lse_ref = refs[:6]
    more, (dq_ref, dk_ref, dv_ref, kt, dk, dv) = refs[6:-6], refs[-6:]
    live, limit = lens[0], lens[1]
    length, key_count = q_ref.shape[0], k_ref.shape[0]
    kt[...] = jnp.swapaxes(k_ref[...].astype(F32), 0, 1).astype(BF)
    if carried < key_count:
        fresh = pl.ds(carried, key_count - carried)
        dk[fresh, :] = jnp.zeros((key_count - carried, PAIR), F32)
        dv[fresh, :] = jnp.zeros((key_count - carried, PAIR), F32)
    if carried:
        dk[pl.ds(0, carried), :] = more[0][...]
        dv[pl.ds(0, carried), :] = more[1][...]
    for block in range(length // AB):
        at = pl.ds(block * AB, AB)
        qb = start // AB + block

        @pl.when(qb * AB < live)
        def _(qb=qb, at=at):
            query = q_ref[at, :] * jnp.asarray(SCALE, BF)
            grad = do_ref[at, :]
            inner = jnp.swapaxes(o_ref[at, :].astype(F32) * grad.astype(F32), 0, 1)
            parts = masks(causal, key_count, qb, limit)
            sums = [[0.0, 0.0] for _ in parts]
            outs = []
            for h in range(2):
                mine = head_lanes(query, h)
                grad_mine = head_lanes(grad, h)
                lse = lse_ref[0, pl.ds(h, 1), at]
                delta = jnp.sum(inner[h * HEAD_DIM : (h + 1) * HEAD_DIM], axis=0, keepdims=True)
                grad_query = 0.0
                for i, (first, count, mask) in enumerate(parts):
                    keys = pl.ds(first, count)
                    p = jnp.exp(nt(k_ref[keys, :], mine) - lse)
                    if mask is not None:
                        p = jnp.where(mask, p, 0.0)
                    dp = nt(v_ref[keys, :], grad_mine)
                    ds = (p * (dp - delta)).astype(BF)
                    sums[i][0] = sums[i][0] + nn(ds, mine)
                    sums[i][1] = sums[i][1] + nn(p.astype(BF), grad_mine)
                    grad_query = grad_query + nn(kt[pl.ds(h * HEAD_DIM, HEAD_DIM), keys], ds)
                outs.append(grad_query * SCALE)
            for (first, count, _), (sum_k, sum_v) in zip(parts, sums):
                dk[pl.ds(first, count), :] += sum_k
                dv[pl.ds(first, count), :] += sum_v
            dq_ref[at, :] = jnp.swapaxes(jnp.concatenate(outs, axis=0), 0, 1).astype(BF)

        @pl.when(qb * AB >= live)
        def _(at=at):
            dq_ref[at, :] = jnp.zeros((AB, PAIR), BF)

    dk_ref[...] = dk[...].astype(dk_ref.dtype)
    dv_ref[...] = dv[...].astype(dv_ref.dtype)


def columns(rows, first, row_block=0):
    at = first if callable(first) else lambda g: first + g
    return pl.BlockSpec((rows, PAIR), lambda g, lens: (row_block, at(g)))


def attend_forward(query, keys, values, lens, causal, length, key_count, pairs):
    (qa, q0, rows), (ka, k0), (va, v0) = query, keys, values
    return pl.pallas_call(
        functools.partial(attend_fwd_kernel, causal),
        grid_spec=pltpu.PrefetchScalarGridSpec(
            num_scalar_prefetch=1,
            grid=(pairs,),
            in_specs=[
                columns(length, q0, rows),
                columns(key_count, k0),
                columns(key_count, v0),
            ],
            out_specs=[
                columns(length, 0),
                pl.BlockSpec((1, 2, length), lambda g, lens: (g, 0, 0)),
            ],
        ),
        out_shape=[
            jax.ShapeDtypeStruct((length, pairs * PAIR), BF),
            jax.ShapeDtypeStruct((pairs, 2, length), F32),
        ],
        compiler_params=pltpu.CompilerParams(vmem_limit_bytes=24 * 2**20),
        cost_estimate=BRIEF,
        name="attend_causal" if causal else "attend_memory",
    )(lens, qa, ka, va)


def attend_backward(
    query, keys, values, mixed, grad, lse, lens, causal, start, length, key_count, pairs, carried, last
):
    (qa, q0, rows), (ka, k0), (va, v0) = query, keys, values
    had = carried[0].shape[0] if carried else 0
    kept = BF if last else F32
    return pl.pallas_call(
        functools.partial(attend_bwd_kernel, causal, start, had),
        grid_spec=pltpu.PrefetchScalarGridSpec(
            num_scalar_prefetch=1,
            grid=(pairs,),
            in_specs=[
                columns(length, q0, rows),
                columns(key_count, k0),
                columns(key_count, v0),
                columns(length, mixed[1]),
                columns(length, grad[1]),
                pl.BlockSpec((1, 2, length), lambda g, lens: (mixed[1] + g, 0, 0)),
            ]
            + [columns(had, 0)] * (2 if carried else 0),
            out_specs=[columns(length, 0), columns(key_count, 0), columns(key_count, 0)],
            scratch_shapes=[
                pltpu.VMEM((PAIR, key_count), BF),
                pltpu.VMEM((key_count, PAIR), F32),
                pltpu.VMEM((key_count, PAIR), F32),
            ],
        ),
        out_shape=[
            jax.ShapeDtypeStruct((length, pairs * PAIR), BF),
            jax.ShapeDtypeStruct((key_count, pairs * PAIR), kept),
            jax.ShapeDtypeStruct((key_count, pairs * PAIR), kept),
        ],
        compiler_params=pltpu.CompilerParams(vmem_limit_bytes=32 * 2**20),
        cost_estimate=BRIEF,
        name="attend_causal_back" if causal else "attend_memory_back",
    )(lens, qa, ka, va, mixed[0], grad[0], lse, *(carried or ()))


def normed(value, gain):
    scale = lax.rsqrt(jnp.mean(value * value, axis=-1, keepdims=True) + EPS)
    return value * scale * gain


def norm_back(value, gain, grad):
    scale = lax.rsqrt(jnp.mean(value * value, axis=-1, keepdims=True) + EPS)
    unit = value * scale
    scaled = grad * gain
    inner = jnp.mean(scaled * unit, axis=-1, keepdims=True)
    return scale * (scaled - unit * inner), jnp.sum(grad * unit, axis=0, keepdims=True)


def enter_kernel(x_ref, w0_ref, w1_ref, columns_ref, h_ref, qkv_ref, gain_ref):
    rows = jnp.swapaxes(columns_ref[...].astype(F32), 0, 1)
    gain_ref[...] = rows[:8]
    h = normed(x_ref[...].astype(F32), rows[0:1]).astype(BF)
    h_ref[...] = h
    wide = w0_ref.shape[1]
    qkv_ref[:, pl.ds(0, wide)] = nn(h, w0_ref[...]).astype(BF)
    qkv_ref[:, pl.ds(wide, wide)] = nn(h, w1_ref[...]).astype(BF)


def product_kernel(x_ref, w_ref, o_ref):
    o_ref[...] = nn(x_ref[...], w_ref[...]).astype(BF)


def middle_kernel(x_ref, o_ref, gain_ref, wo_ref, cq_ref, x1_ref, h_ref, q_ref):
    x1 = x_ref[...].astype(F32) + nn(o_ref[...], wo_ref[...])
    h = normed(x1, gain_ref[1:2]).astype(BF)
    x1_ref[...] = x1
    h_ref[...] = h
    q_ref[...] = nn(h, cq_ref[...]).astype(BF)


def outer_kernel(x1_ref, o_ref, gain_ref, co_ref, x2_ref, h_ref):
    x2 = x1_ref[...] + nn(o_ref[...], co_ref[...])
    x2_ref[...] = x2
    h_ref[...] = normed(x2, gain_ref[2:3]).astype(BF)


def add_gain(step, ref, value):
    @pl.when(step == 0)
    def _():
        ref[...] = jnp.zeros_like(ref)

    ref[0:1, :] += value


def outer_back_kernel(dh_ref, x2_ref, g_ref, gain_ref, co_ref, d_ref, dx_ref, do_ref, dgain_ref):
    dx, dgain = norm_back(x2_ref[...], gain_ref[2:3], dh_ref[...].astype(F32))
    dx = g_ref[...].astype(F32) + dx
    d = dx.astype(BF)
    dx_ref[...] = dx
    d_ref[...] = d
    do_ref[...] = nt(d, co_ref[...]).astype(BF)
    add_gain(pl.program_id(0), dgain_ref, dgain)


def middle_back_kernel(
    dq_ref, x1_ref, dx2_ref, gain_ref, cq_ref, wo_ref, dx_ref, d_ref, do_ref, dgain_ref
):
    dx, dgain = norm_back(x1_ref[...], gain_ref[1:2], nt(dq_ref[...], cq_ref[...]))
    dx = dx2_ref[...] + dx
    d = dx.astype(BF)
    dx_ref[...] = dx
    d_ref[...] = d
    do_ref[...] = nt(d, wo_ref[...]).astype(BF)
    add_gain(pl.program_id(0), dgain_ref, dgain)


def enter_back_kernel(x_ref, dx1_ref, *refs):
    grads, gain_ref, weights, (out_ref, dgain_ref) = refs[:3], refs[3], refs[4:10], refs[10:]
    dh = 0.0
    for i, grad in enumerate(grads):
        for g in range(2):
            w = weights[2 * i + g]
            at = pl.ds(g * w.shape[1], w.shape[1])
            dh = dh + nt(grad[:, at], w[...])
    dx, dgain = norm_back(x_ref[...].astype(F32), gain_ref[0:1], dh)
    out_ref[...] = (dx1_ref[...] + dx).astype(BF)
    add_gain(pl.program_id(0), dgain_ref, dgain)


def by_tokens(kernel, tokens, blocked, whole, outs, name, c=0, kept=None):
    width = blocked[0][0].shape[1]
    steps = tokens // QB
    full = tokens if kept is None else 2 * tokens

    def rows(n, first):
        return pl.BlockSpec((QB, n), lambda i, first=first: (first + i, 0))

    def fixed(shape, index):
        return pl.BlockSpec(shape, lambda i, index=index: index)

    kept = kept or ()
    inputs = len(blocked) + len(whole)

    def run(*refs):
        kernel(*refs[:inputs], *refs[inputs + len(kept) :])

    return pl.pallas_call(
        run,
        grid=(steps,),
        in_specs=[rows(a.shape[1], first) for a, first in blocked]
        + [fixed(shape, index) for _, shape, index in whole]
        + [pl.BlockSpec(memory_space=pl.ANY)] * len(kept),
        out_specs=[
            fixed((8, width), (0, 0)) if n is None else rows(n, c * steps) for n, _ in outs
        ],
        out_shape=[
            jax.ShapeDtypeStruct((8, width) if n is None else (full, n), dtype)
            for n, dtype in outs
        ],
        input_output_aliases={inputs + i: i for i in range(len(kept))},
        compiler_params=pltpu.CompilerParams(vmem_limit_bytes=24 * 2**20),
        cost_estimate=BRIEF,
        name=name,
    )(*[a for a, _ in blocked], *[a for a, _, _ in whole], *kept)


def weight_grad_kernel(*refs):
    *ins, o_ref = refs
    total = tn(ins[0][...], ins[1][...])
    for i in range(2, len(ins), 2):
        total = total + tn(ins[i][...], ins[i + 1][...])
    o_ref[...] = total.astype(BF)


def weight_grad(pairs, columns_at_once):
    rows, width = pairs[0][0].shape[1], pairs[0][1].shape[1]
    specs = []
    for x, grad in pairs:
        specs.append(pl.BlockSpec((x.shape[0], columns_at_once), lambda i: (0, i)))
        specs.append(pl.BlockSpec(grad.shape, lambda i: (0, 0)))
    return pl.pallas_call(
        weight_grad_kernel,
        grid=(rows // columns_at_once,),
        in_specs=specs,
        out_specs=pl.BlockSpec((columns_at_once, width), lambda i: (i, 0)),
        out_shape=jax.ShapeDtypeStruct((rows, width), BF),
        compiler_params=pltpu.CompilerParams(
            vmem_limit_bytes=(40 if width > 768 else 24) * 2**20
        ),
        cost_estimate=BRIEF,
        name="weight_grad",
    )(*[a for pair in pairs for a in pair])


GELU_A = 0.7978845608028654
GELU_B = 0.044715


def feed_kernel(groups, ff, step, *refs):
    h_refs, g_refs, (gu_ref, down_ref) = refs[:groups], refs[groups : 2 * groups], refs[2 * groups : 2 * groups + 2]
    outs = refs[-2 * groups - 4 :]
    y_refs, dh_refs, (hid_ref, dgu_ref, h_ref, g_ref) = outs[:groups], outs[groups:-4], outs[-4:]
    part = h_refs[0].shape[0]
    for j in range(groups):
        h_ref[pl.ds(j * part, part), :] = h_refs[j][...]
        g_ref[pl.ds(j * part, part), :] = g_refs[j][0]
    y, dh = 0.0, 0.0
    for c in range(0, ff, step):
        wg = gu_ref[:, pl.ds(c, step)]
        wu = gu_ref[:, pl.ds(ff + c, step)]
        wd = down_ref[pl.ds(c, step), :]
        gate, up, dhid = nn(h_ref[...], wg), nn(h_ref[...], wu), nt(g_ref[...], wd)
        square = gate * gate
        th = jnp.tanh(gate * (GELU_A + (GELU_A * GELU_B) * square))
        half = 0.5 + 0.5 * th
        act = gate * half
        slope = half + (0.5 * gate) * (1.0 - th * th) * (
            GELU_A + (3.0 * GELU_A * GELU_B) * square
        )
        hidden = (act * up).astype(BF)
        dgate = (dhid * up * slope).astype(BF)
        dup = (dhid * act).astype(BF)
        hid_ref[:, pl.ds(c, step)] = hidden
        dgu_ref[:, pl.ds(c, step)] = dgate
        dgu_ref[:, pl.ds(ff + c, step)] = dup
        y = y + nn(hidden, wd)
        dh = dh + nt(dgate, wg) + nt(dup, wu)
    for j in range(groups):
        y_refs[j][0] = y[j * part : (j + 1) * part].astype(BF)
        dh_refs[j][...] = dh[j * part : (j + 1) * part].astype(BF)


def feed(c, h_parts, g_parts, wgu, wd, kept):
    groups = len(h_parts)
    part, width = h_parts[0].shape
    ff = wd.shape[0]
    tokens = groups * part

    def whole(a):
        return pl.BlockSpec(a.shape, lambda i: (0,) * a.ndim)

    def halves(n):
        return pl.BlockSpec((tokens, n), lambda i: (c, 0))

    wide = (ff, 2 * ff, width, width)
    of_half = pl.BlockSpec((1, part, width), lambda i: (c, 0, 0))
    made = [0 + i for i in range(groups)] + [2 * groups + i for i in range(len(wide))]
    return pl.pallas_call(
        functools.partial(feed_kernel, groups, ff, 512),
        grid=(1,),
        in_specs=[whole(h) for h in h_parts]
        + [of_half] * groups
        + [whole(wgu), whole(wd)]
        + [pl.BlockSpec(memory_space=pl.ANY)] * len(kept),
        out_specs=[of_half] * groups
        + [whole(h) for h in h_parts]
        + [halves(n) for n in wide],
        out_shape=[jax.ShapeDtypeStruct((2, part, width), BF)] * groups
        + [jax.ShapeDtypeStruct((part, width), BF)] * groups
        + [jax.ShapeDtypeStruct((2 * tokens, n), BF) for n in wide],
        input_output_aliases={2 * groups + 2 + i: made[i] for i in range(len(kept))},
        compiler_params=pltpu.CompilerParams(vmem_limit_bytes=VMEM),
        cost_estimate=BRIEF,
        name="feed",
    )(*h_parts, *g_parts, wgu, wd, *kept)


def pick_kernel(modes, halves, source, mode, x_ref, *o_refs):
    per_mode = x_ref.shape[0] // modes
    for j in range(modes):
        first = jnp.bitwise_xor(mode[0], j) * per_mode

        def move(r, carry, j=j, first=first):
            row = source[first + r]
            if halves:
                for c in range(halves):
                    o_refs[j][c, r] = x_ref[row, c]
            else:
                o_refs[j][r] = x_ref[row]
            return carry

        lax.fori_loop(0, per_mode, move, 0)


def put_kernel(modes, halves, source, mode, *refs):
    o_ref = refs[-1]
    per_mode = o_ref.shape[0] // modes
    for j in range(modes):
        first = jnp.bitwise_xor(mode[0], j) * per_mode

        def move(r, carry, j=j, first=first):
            row = source[first + r]
            if halves:
                for c in range(halves):
                    o_ref[row, c] = refs[j][c, r]
            else:
                o_ref[row] = refs[j][r]
            return carry

        lax.fori_loop(0, per_mode, move, 0)


def mode_number():
    return lax.axis_index("mode").astype(jnp.int32)[None]


def by_rows(kernel, source, ins, outs, name):
    def whole(shape):
        return pl.BlockSpec(shape, lambda i, source, mode: (0,) * len(shape))

    return pl.pallas_call(
        kernel,
        grid_spec=pltpu.PrefetchScalarGridSpec(
            num_scalar_prefetch=2,
            grid=(1,),
            in_specs=[whole(a.shape) for a in ins],
            out_specs=[whole(shape) for shape in outs],
        ),
        out_shape=[jax.ShapeDtypeStruct(shape, BF) for shape in outs],
        compiler_params=pltpu.CompilerParams(vmem_limit_bytes=16 * 2**20),
        cost_estimate=pl.CostEstimate(
            flops=0, bytes_accessed=4 * sum(a.size for a in ins), transcendentals=0
        ),
        name=name,
    )(source, mode_number(), *ins)


def to_mode(spread, source):
    per_mode, modes = lax.axis_size("dp"), lax.axis_size("mode")
    piece = spread.shape[-2:]
    if spread.ndim == 4:
        outs = [(spread.shape[1], per_mode) + piece] * modes
    else:
        outs = [(per_mode,) + piece] * modes
    parts = by_rows(
        functools.partial(pick_kernel, modes, spread.shape[1] if spread.ndim == 4 else 0),
        source,
        [spread],
        outs,
        "pick",
    )
    got = [parts[0]] + [swap(parts[j], per_mode * j) for j in range(1, modes)]
    if spread.ndim == 4:
        return [part.reshape(part.shape[0], -1, part.shape[-1]) for part in got]
    return [part.reshape(-1, part.shape[-1]) for part in got]


def swap_modes(parts):
    per_mode = lax.axis_size("dp")
    lead = parts[0].shape[:-2]
    parts = [part.reshape(lead + (per_mode, -1, part.shape[-1])) for part in parts]
    return [parts[0]] + [swap(parts[j], per_mode * j) for j in range(1, len(parts))]


def put_back(parts, source):
    halves = parts[0].shape[0] if parts[0].ndim == 4 else 0
    shape = (lax.axis_size(ALL),) + ((halves,) if halves else ()) + parts[0].shape[-2:]
    return by_rows(
        functools.partial(put_kernel, len(parts), halves), source, parts, [shape], "put"
    )[0]


def dealt(value):
    count = lax.axis_size(ALL)
    return value.reshape(count, -1, value.shape[-1])


def to_all(value):
    return lax.all_to_all(value, ALL, 0, 0, tiled=True)


def swap(value, j):
    count = lax.axis_size(ALL)
    return lax.ppermute(value, ALL, [(i, i ^ j) for i in range(count)])


def device_number():
    return lax.axis_index(ALL).astype(jnp.int32)[None]


def place_kernel(me, even_ref, odd_ref, *o_refs):
    first = 0
    for o_ref in o_refs:
        at = pl.ds(first, o_ref.shape[2])
        first += o_ref.shape[2]
        for t in range(even_ref.shape[0]):
            o_ref[jnp.bitwise_xor(2 * t, me[0])] = even_ref[t, :, at]
            o_ref[jnp.bitwise_xor(2 * t + 1, me[0])] = odd_ref[t, :, at]


def place(even, odd, widths, number):
    count, rows, width = even.shape
    shapes = [(2 * count, rows, w) for w in widths]

    def whole(shape):
        return pl.BlockSpec(shape, lambda i, me: (0, 0, 0))

    return pl.pallas_call(
        place_kernel,
        grid_spec=pltpu.PrefetchScalarGridSpec(
            num_scalar_prefetch=1,
            grid=(1,),
            in_specs=[whole(even.shape)] * 2,
            out_specs=[whole(shape) for shape in shapes],
        ),
        out_shape=[jax.ShapeDtypeStruct(shape, even.dtype) for shape in shapes],
        compiler_params=pltpu.CompilerParams(vmem_limit_bytes=28 * 2**20),
        cost_estimate=BRIEF,
        name="place",
    )(number, even, odd)


def pack_kernel(counts, *refs):
    ins, outs = refs[: sum(counts)], refs[sum(counts) :]
    taken = 0
    for count, o_ref in zip(counts, outs):
        first = 0
        for part in ins[taken : taken + count]:
            o_ref[:, pl.ds(first, part.shape[1])] = part[...]
            first += part.shape[1]
        taken += count


def pack(*lists):
    cut = lambda e: e if not isinstance(e, tuple) else e[0]
    shape = lambda e: e.shape if not isinstance(e, tuple) else (e[0].shape[0], e[2])
    at = lambda e: 0 if not isinstance(e, tuple) else e[1] // e[2]
    entries = [e for group in lists for e in group]
    return pl.pallas_call(
        functools.partial(pack_kernel, [len(group) for group in lists]),
        grid=(1,),
        in_specs=[pl.BlockSpec(shape(e), lambda i, e=e: (0, at(e))) for e in entries],
        out_specs=[
            pl.BlockSpec((shape(group[0])[0], sum(shape(e)[1] for e in group)), lambda i: (0, 0))
            for group in lists
        ],
        out_shape=[
            jax.ShapeDtypeStruct((shape(group[0])[0], sum(shape(e)[1] for e in group)), BF)
            for group in lists
        ],
        name="pack",
    )(*[cut(e) for e in entries])


def gather_column(piece, late=None):
    per_mode = lax.axis_size("dp")
    got = [swap(piece, 2 * j) for j in range(1, per_mode // 2)]
    return jnp.stack([piece] + (got if late is None else tied(got, late)))


def gather_rest(column, widths, late=None):
    per_mode, modes = lax.axis_size("dp"), lax.axis_size("mode")
    got = [swap(column, per_mode * j) for j in range(1, modes)]
    if late is not None:
        got = tied(got, late)
    plane = jnp.stack([column] + got)
    plane = plane.reshape((-1,) + column.shape[1:])
    placed = place(plane, swap(plane, 1), widths, device_number())
    return [a.reshape(-1, a.shape[2]) for a in placed]


def take_kernel(parts, me, *refs):
    ins, (keep_ref, send_ref) = refs[:parts], refs[parts:]
    first = 0
    for in_ref in ins:
        at = pl.ds(first, in_ref.shape[2])
        first += in_ref.shape[2]
        for t in range(keep_ref.shape[0]):
            keep_ref[t, :, at] = in_ref[jnp.bitwise_xor(2 * t, me[0])]
            send_ref[t, :, at] = in_ref[jnp.bitwise_xor(2 * t + 1, me[0])]


def take(parts):
    count, rows = parts[0].shape[:2]
    width = sum(part.shape[2] for part in parts)
    half = jax.ShapeDtypeStruct((count // 2, rows, width), parts[0].dtype)

    def whole(shape):
        return pl.BlockSpec(shape, lambda i, me: (0, 0, 0))

    return pl.pallas_call(
        functools.partial(take_kernel, len(parts)),
        grid_spec=pltpu.PrefetchScalarGridSpec(
            num_scalar_prefetch=1,
            grid=(1,),
            in_specs=[whole(part.shape) for part in parts],
            out_specs=[whole(half.shape)] * 2,
        ),
        out_shape=[half, half],
        compiler_params=pltpu.CompilerParams(vmem_limit_bytes=48 * 2**20),
        cost_estimate=BRIEF,
        name="take",
    )(device_number(), *parts)


def add_up(parts):
    return functools.reduce(jnp.add, [part.astype(F32) for part in parts])


def scatter_pairs(parts):
    count = lax.axis_size(ALL)
    parts = [part.reshape(count, part.shape[0] // count, part.shape[1]) for part in parts]
    keep, send = take(parts)
    return add_up([keep, swap(send, 1)]).astype(BF)


def scatter_plane(pair):
    per_mode, modes = lax.axis_size("dp"), lax.axis_size("mode")
    plane = pair.reshape((modes, per_mode // 2) + pair.shape[1:])
    return add_up([plane[0]] + [swap(plane[j], per_mode * j) for j in range(1, modes)]).astype(BF)


def scatter_column(column):
    per_mode = lax.axis_size("dp")
    return add_up([column[0]] + [swap(column[j], 2 * j) for j in range(1, per_mode // 2)])


def later(lens, tokens):
    return lens - jnp.array([tokens, 0], jnp.int32)


def tied(first, second):
    return lax.optimization_barrier((first, second))[0]


def lanes_of(*vectors):
    columns_ = jnp.stack(vectors, axis=1)
    return jnp.pad(columns_, ((0, 0), (0, 128 - len(vectors))))


def on_device(
    rows,
    memory,
    cotangent,
    mode_ids,
    target_lengths,
    encoder_lengths,
    self_q,
    self_k,
    self_v,
    self_o,
    self_gain,
    cross_q,
    cross_k,
    cross_v,
    cross_o,
    cross_gain,
    ffn_gain,
    ffn_gate,
    ffn_up,
    ffn_down,
):
    devices = lax.axis_size(ALL)
    per_mode = lax.axis_size("dp")
    here = lax.axis_index(ALL)
    width = rows.shape[2]
    ff = ffn_gate.shape[2]
    index = jnp.arange(devices, dtype=jnp.int32)
    same = mode_ids[:, None] == mode_ids[None, :]
    earlier = index[None, :] < index[:, None]
    rank = jnp.sum(jnp.where(same & earlier, 1, 0), axis=1).astype(jnp.int32)
    target = mode_ids * per_mode + rank
    source = jnp.sum(
        jnp.where(target[:, None] == index[None, :], index[:, None], 0), axis=0
    ).astype(jnp.int32)
    live_len = jnp.sum(jnp.where(index == here, target_lengths, 0))
    memory_len = jnp.sum(jnp.where(index == here, encoder_lengths, 0))
    lens = jnp.stack([live_len, memory_len]).astype(jnp.int32)
    tokens, memory_row, incoming = rows[0], memory[0], cotangent[0]
    length = tokens.shape[0]
    half = length // 2
    key_count = memory_row.shape[0]
    valid = (jnp.arange(length, dtype=jnp.int32) < live_len)[:, None]
    grad_low = jnp.where(valid, incoming, jnp.zeros_like(incoming))

    group_pairs = HEADS // 4
    part = group_pairs * PAIR

    def of_group(g):
        return tuple((a, g * part, part) for a in (self_q, self_k, self_v))

    own_piece, rest_piece = pack(
        of_group(0) + of_group(1) + (lanes_of(self_gain, cross_gain, ffn_gain),),
        (self_o, cross_q, cross_k, cross_v, cross_o),
    )
    column = gather_column(own_piece)
    own_0, own_1, gain_columns = gather_rest(column, (3 * part, 3 * part, 128))
    crossing = lax.all_gather(rest_piece, ALL, axis=0, tiled=True)

    def weight(array, i, wide=width):
        return (array, (width, wide), (0, i))

    h1, qkv, gains = by_tokens(
        enter_kernel,
        length,
        [(tokens, 0)],
        [(a, a.shape, (0, 0)) for a in (own_0, own_1, gain_columns)],
        [(width, BF), (6 * part, BF), (None, F32)],
        "enter",
    )
    all_gains = (gains, gains.shape, (0, 0))
    pairs = HEADS // 2

    def of_pair(i):
        return lambda g: (g // group_pairs) * 3 * group_pairs + i * group_pairs + g % group_pairs

    grad_dealt = grad_low.reshape(2, devices, -1, width).swapaxes(0, 1)
    grad_spread = to_all(grad_dealt)

    wgu = lax.all_gather(
        jnp.concatenate([ffn_gate[0], ffn_up[0]], axis=1), "dp", axis=0, tiled=True
    )
    wd = lax.all_gather(ffn_down[0], "dp", axis=0, tiled=True)

    mixed, log_self = attend_forward(
        (qkv, of_pair(0), 0),
        (qkv, of_pair(1)),
        (qkv, of_pair(2)),
        lens,
        True,
        length,
        length,
        pairs,
    )
    wo, cq, ckv, co = (
        crossing[:, i * width : j * width] for i, j in ((0, 1), (1, 2), (2, 4), (4, 5))
    )

    def forward_middle(c):
        first = c * (half // QB)
        return by_tokens(
            middle_kernel,
            half,
            [(tokens, first), (mixed, first)],
            [all_gains, weight(wo, 0), weight(cq, 0)],
            [(width, F32), (width, BF), (width, BF)],
            "middle",
        )

    def forward_cross(c, query):
        return attend_forward(
            (query, 0, 0),
            (cross_kv, 0),
            (cross_kv, pairs),
            later(lens, c * half),
            False,
            half,
            key_count,
            pairs,
        )

    def forward_outer(x1, cross_mixed):
        return by_tokens(
            outer_kernel,
            half,
            [(x1, 0), (cross_mixed, 0)],
            [all_gains, weight(co, 0)],
            [(width, F32), (width, BF)],
            "outer",
        )

    x1_a, h2_a, query_a = forward_middle(0)
    (cross_kv,) = by_tokens(
        product_kernel,
        key_count,
        [(memory_row, 0)],
        [(ckv, ckv.shape, (0, 0))],
        [(2 * width, BF)],
        "memory",
    )
    cross_a, log_cross_a = forward_cross(0, query_a)
    x2_a, h3_a = forward_outer(x1_a, cross_a)
    spread_a = to_all(dealt(tied(h3_a, grad_spread)))
    grad_parts = to_mode(grad_spread, source)
    x1_b, h2_b, query_b = forward_middle(1)
    query_b = tied(query_b, h3_a)
    cross_b, log_cross_b = forward_cross(1, query_b)
    cross_b, grad_parts = lax.optimization_barrier((cross_b, grad_parts))
    x2_b, h3_b = forward_outer(x1_b, cross_b)
    routed_a = to_mode(tied(spread_a, cross_b), source)
    spread_b = to_all(dealt(h3_b))

    modes = len(routed_a)
    routed_b = to_mode(spread_b, source)
    fed_a = feed(0, tied(routed_a, routed_b), grad_parts, wgu, wd, ())
    y_a, dh_a, kept_a = fed_a[:modes], fed_a[modes : 2 * modes], fed_a[2 * modes :]
    back_a = put_back(swap_modes(dh_a), source)
    routed_b, back_a = lax.optimization_barrier((routed_b, back_a))
    home_a = to_all(back_a).reshape(half, width)
    fed_b = feed(1, routed_b, grad_parts, wgu, wd, y_a + kept_a)
    y, dh_b = fed_b[:modes], fed_b[modes : 2 * modes]
    hidden, dgu, routed_h, routed_grad = fed_b[2 * modes :]
    back_b = swap_modes(dh_b)
    grad_wd = weight_grad([(tied(hidden, home_a), routed_grad)], 512)
    grad_wgu = weight_grad([(routed_h, dgu)], 256)
    back_b = put_back(tied(back_b, (grad_wd, grad_wgu)), source)
    sum_wgu = lax.psum_scatter(grad_wgu, "dp", scatter_dimension=0, tiled=True)
    sum_wd = lax.psum_scatter(grad_wd, "dp", scatter_dimension=0, tiled=True)
    home_b = to_all(back_b).reshape(half, width)
    home_a = tied(home_a, back_b)
    y_mode = swap_modes(tied(y, back_b))

    def back_outer(c, dh, x2):
        return by_tokens(
            outer_back_kernel,
            half,
            [(dh, 0), (x2, 0), (grad_low, c * (half // QB))],
            [all_gains, weight(co, 0)],
            [(width, BF), (width, F32), (width, BF), (None, F32)],
            "outer_back",
        )

    def back_middle(c, dq, x1, dx2, kept):
        return by_tokens(
            middle_back_kernel,
            half,
            [(dq, 0), (x1, 0), (dx2, 0)],
            [all_gains, weight(cq, 0), weight(wo, 0)],
            [(width, F32), (width, BF), (width, BF), (None, F32)],
            "middle_back",
            c,
            kept,
        )

    def back_cross(c, query, mixed, grad, lse, carried):
        return attend_backward(
            (query, 0, 0),
            (cross_kv, 0),
            (cross_kv, pairs),
            (mixed, 0),
            (grad, 0),
            lse,
            later(lens, c * half),
            False,
            0,
            half,
            key_count,
            pairs,
            carried,
            c == 1,
        )

    def back_self(grad):
        return attend_backward(
            (qkv, of_pair(0), 0),
            (qkv, of_pair(1)),
            (qkv, of_pair(2)),
            (mixed, 0),
            (grad, 0),
            log_self,
            lens,
            True,
            0,
            length,
            length,
            pairs,
            None,
            True,
        )

    d2_a, dx2_a, do2_a, dgain_ffn_a = back_outer(0, home_a, x2_a)
    dcq_a, dck_a, dcv_a = back_cross(0, query_a, cross_a, do2_a, log_cross_a, None)
    *halves, dgain_cross_a = back_middle(0, dcq_a, x1_a, dx2_a, ())
    home_b, y_mode = lax.optimization_barrier((tied(home_b, halves), y_mode))
    d2_b, dx2_b, do2_b, dgain_ffn_b = back_outer(1, home_b, x2_b)
    y_put, do2_b = lax.optimization_barrier((put_back(y_mode, source), do2_b))
    y_home = to_all(y_put)
    dcq_b, dck, dcv = back_cross(1, query_b, cross_b, do2_b, log_cross_b, (dck_a, dcv_a))
    dx1, d1, do1, dgain_cross_b = back_middle(1, dcq_b, x1_b, dx2_b, halves)
    cross_pair = scatter_pairs(
        [
            weight_grad([(h2_a, dcq_a), (h2_b, dcq_b)], 256),
            weight_grad([(memory_row, dck)], 256),
            weight_grad([(memory_row, dcv)], 256),
            weight_grad([(cross_a, d2_a), (cross_b, d2_b)], 256),
            weight_grad([(mixed, d1)], 256),
        ]
    )
    do1, cross_pair = lax.optimization_barrier((do1, cross_pair))
    cross_plane = scatter_plane(cross_pair)
    grads = back_self(do1)
    grads, cross_plane, y_home, sum_wgu, sum_wd = lax.optimization_barrier(
        (grads, cross_plane, y_home, sum_wgu, sum_wd)
    )
    cross_sum = scatter_column(cross_plane)
    own_pair = scatter_pairs([tn(h1, d).astype(BF) for d in grads])
    own_plane = scatter_plane(own_pair)
    grads, dck, dcv = tied((grads, dck, dcv), own_pair)
    y_home = tied(y_home, own_plane)
    grad_tokens, dgain_self = by_tokens(
        enter_back_kernel,
        length,
        [(tokens, 0), (dx1, 0)] + [(d, 0) for d in grads],
        [all_gains] + [weight(own, i, part) for i in range(3) for own in (own_0, own_1)],
        [(width, BF), (None, F32)],
        "enter_back",
    )
    gain_grads = jnp.stack(
        [dgain_self[0], dgain_cross_a[0] + dgain_cross_b[0], dgain_ffn_a[0] + dgain_ffn_b[0]]
    )
    own_plane, gain_grads = lax.optimization_barrier((own_plane, gain_grads))
    own_sum = scatter_column(own_plane)
    gain_grads = gain_grads.reshape(3, devices, -1).swapaxes(0, 1)
    gain_sums = jnp.sum(to_all(gain_grads), axis=0)
    grad_memory = (nt(dck, ckv[:, :width]) + nt(dcv, ckv[:, width:])).astype(BF)
    y = y_home.swapaxes(0, 1).reshape(length, width)
    result = jnp.where(valid, jnp.concatenate([x2_a, x2_b]) + y.astype(F32), 0.0).astype(BF)

    def block(value, i):
        return value[:, i * width : (i + 1) * width]

    return (
        result[None],
        grad_tokens[None],
        grad_memory[None],
        block(own_sum, 0),
        block(own_sum, 1),
        block(own_sum, 2),
        block(cross_sum, 4),
        gain_sums[0],
        block(cross_sum, 0),
        block(cross_sum, 1),
        block(cross_sum, 2),
        block(cross_sum, 3),
        gain_sums[1],
        gain_sums[2],
        sum_wgu[:, :ff].astype(F32)[None],
        sum_wgu[:, ff:].astype(F32)[None],
        sum_wd.astype(F32)[None],
    )


def solution(mesh):
    rows = P(ALL, None, None)
    weight = P(ALL, None)
    gain = P(ALL)
    feeding = P("mode", "dp", None)
    return jax.shard_map(
        on_device,
        mesh=mesh,
        in_specs=(
            (rows,) * 3
            + (P(),) * 3
            + (weight,) * 4
            + (gain,)
            + (weight,) * 4
            + (gain,) * 2
            + (feeding,) * 3
        ),
        out_specs=(
            (rows,) * 3
            + (weight,) * 4
            + (gain,)
            + (weight,) * 4
            + (gain,) * 2
            + (feeding,) * 3
        ),
        check_vma=False,
    )
```

```python
import functools

import jax
import jax.numpy as jnp
from jax import lax
from jax.experimental import pallas as pl
from jax.experimental.pallas import tpu as pltpu
from jax.sharding import PartitionSpec as P

HEADS = 12
HEAD_DIM = 64
PAIR = 2 * HEAD_DIM
EPS = 1e-06
NEG = -1e30
SCALE = HEAD_DIM ** -0.5
QB = 256
AB = 512
ALL = ("mode", "dp")
BF = jnp.bfloat16
F32 = jnp.float32
VMEM = 56 * 2**20
BRIEF = pl.CostEstimate(flops=10**6, bytes_accessed=10**4, transcendentals=0)


def nt(left, right):
    return lax.dot_general(left, right, (((1,), (1,)), ((), ())), preferred_element_type=F32)


def nn(left, right):
    return jnp.dot(left, right, preferred_element_type=F32)


def tn(left, right):
    return lax.dot_general(left, right, (((0,), (0,)), ((), ())), preferred_element_type=F32)


def head_lanes(value, h):
    lane = lax.broadcasted_iota(jnp.int32, value.shape, 1)
    return jnp.where((lane >= HEAD_DIM) == (h == 1), value, jnp.zeros_like(value))


def masks(causal, key_count, qb, limit):
    if causal:
        parts = []
        if qb:
            parts.append((0, qb * AB, None))
        row = lax.broadcasted_iota(jnp.int32, (AB, AB), 0)
        col = lax.broadcasted_iota(jnp.int32, (AB, AB), 1)
        parts.append((qb * AB, AB, row <= col))
        return parts
    row = lax.broadcasted_iota(jnp.int32, (key_count, AB), 0)
    return [(0, key_count, row < limit)]


def attend_fwd_kernel(causal, lens, q_ref, k_ref, v_ref, o_ref, lse_ref):
    live, limit = lens[0], lens[1]
    length, key_count = q_ref.shape[0], k_ref.shape[0]
    block = min(AB, length)
    first_head = lax.broadcasted_iota(jnp.int32, (1, PAIR), 1) < HEAD_DIM
    for start in range(0, length, block):
        at = pl.ds(start, block)

        @pl.when(start < live)
        def _(start=start, at=at):
            query = q_ref[at, :] * jnp.asarray(SCALE, BF)
            if causal:
                row = lax.broadcasted_iota(jnp.int32, (block, block), 0)
                col = lax.broadcasted_iota(jnp.int32, (block, block), 1)
                parts = [(0, start, None)] if start else []
                parts.append((start, block, col <= row))
            else:
                col = lax.broadcasted_iota(jnp.int32, (block, key_count), 1)
                parts = [(0, key_count, col < limit)]
            outs, logs = [], []
            for h in range(2):
                mine = head_lanes(query, h)
                scores = []
                for first, count, mask in parts:
                    s = nt(mine, k_ref[pl.ds(first, count), :])
                    scores.append(s if mask is None else jnp.where(mask, s, NEG))
                top = functools.reduce(
                    jnp.maximum, [jnp.max(s, axis=1, keepdims=True) for s in scores]
                )
                total, mixed = 0.0, 0.0
                for (first, count, _), s in zip(parts, scores):
                    p = jnp.exp(s - top)
                    total = total + jnp.sum(p, axis=1, keepdims=True)
                    mixed = mixed + nn(p.astype(BF), v_ref[pl.ds(first, count), :])
                outs.append(mixed / total)
                logs.append(top + jnp.log(total))
            o_ref[at, :] = jnp.where(first_head, outs[0], outs[1]).astype(BF)
            rows = jnp.swapaxes(jnp.where(first_head, logs[0], logs[1]), 0, 1)
            lse_ref[0, pl.ds(0, 1), at] = rows[0:1]
            lse_ref[0, pl.ds(1, 1), at] = rows[HEAD_DIM : HEAD_DIM + 1]

        @pl.when(start >= live)
        def _(at=at):
            o_ref[at, :] = jnp.zeros((block, PAIR), BF)
            lse_ref[0, pl.ds(0, 2), at] = jnp.zeros((2, block), F32)


def attend_bwd_kernel(causal, start, carried, lens, *refs):
    q_ref, k_ref, v_ref, o_ref, do_ref, lse_ref = refs[:6]
    more, (dq_ref, dk_ref, dv_ref, kt, dk, dv) = refs[6:-6], refs[-6:]
    live, limit = lens[0], lens[1]
    length, key_count = q_ref.shape[0], k_ref.shape[0]
    kt[...] = jnp.swapaxes(k_ref[...].astype(F32), 0, 1).astype(BF)
    if carried < key_count:
        fresh = pl.ds(carried, key_count - carried)
        dk[fresh, :] = jnp.zeros((key_count - carried, PAIR), F32)
        dv[fresh, :] = jnp.zeros((key_count - carried, PAIR), F32)
    if carried:
        dk[pl.ds(0, carried), :] = more[0][...]
        dv[pl.ds(0, carried), :] = more[1][...]
    for block in range(length // AB):
        at = pl.ds(block * AB, AB)
        qb = start // AB + block

        @pl.when(qb * AB < live)
        def _(qb=qb, at=at):
            query = q_ref[at, :] * jnp.asarray(SCALE, BF)
            grad = do_ref[at, :]
            inner = jnp.swapaxes(o_ref[at, :].astype(F32) * grad.astype(F32), 0, 1)
            parts = masks(causal, key_count, qb, limit)
            sums = [[0.0, 0.0] for _ in parts]
            outs = []
            for h in range(2):
                mine = head_lanes(query, h)
                grad_mine = head_lanes(grad, h)
                lse = lse_ref[0, pl.ds(h, 1), at]
                delta = jnp.sum(inner[h * HEAD_DIM : (h + 1) * HEAD_DIM], axis=0, keepdims=True)
                grad_query = 0.0
                for i, (first, count, mask) in enumerate(parts):
                    keys = pl.ds(first, count)
                    p = jnp.exp(nt(k_ref[keys, :], mine) - lse)
                    if mask is not None:
                        p = jnp.where(mask, p, 0.0)
                    dp = nt(v_ref[keys, :], grad_mine)
                    ds = (p * (dp - delta)).astype(BF)
                    sums[i][0] = sums[i][0] + nn(ds, mine)
                    sums[i][1] = sums[i][1] + nn(p.astype(BF), grad_mine)
                    grad_query = grad_query + nn(kt[pl.ds(h * HEAD_DIM, HEAD_DIM), keys], ds)
                outs.append(grad_query * SCALE)
            for (first, count, _), (sum_k, sum_v) in zip(parts, sums):
                dk[pl.ds(first, count), :] += sum_k
                dv[pl.ds(first, count), :] += sum_v
            dq_ref[at, :] = jnp.swapaxes(jnp.concatenate(outs, axis=0), 0, 1).astype(BF)

        @pl.when(qb * AB >= live)
        def _(at=at):
            dq_ref[at, :] = jnp.zeros((AB, PAIR), BF)

    dk_ref[...] = dk[...].astype(dk_ref.dtype)
    dv_ref[...] = dv[...].astype(dv_ref.dtype)


def columns(rows, first, row_block=0):
    at = first if callable(first) else lambda g: first + g
    return pl.BlockSpec((rows, PAIR), lambda g, lens: (row_block, at(g)))


def attend_forward(query, keys, values, lens, causal, length, key_count, pairs):
    (qa, q0, rows), (ka, k0), (va, v0) = query, keys, values
    return pl.pallas_call(
        functools.partial(attend_fwd_kernel, causal),
        grid_spec=pltpu.PrefetchScalarGridSpec(
            num_scalar_prefetch=1,
            grid=(pairs,),
            in_specs=[
                columns(length, q0, rows),
                columns(key_count, k0),
                columns(key_count, v0),
            ],
            out_specs=[
                columns(length, 0),
                pl.BlockSpec((1, 2, length), lambda g, lens: (g, 0, 0)),
            ],
        ),
        out_shape=[
            jax.ShapeDtypeStruct((length, pairs * PAIR), BF),
            jax.ShapeDtypeStruct((pairs, 2, length), F32),
        ],
        compiler_params=pltpu.CompilerParams(vmem_limit_bytes=41943040),
        cost_estimate=BRIEF,
        name="attend_causal" if causal else "attend_memory",
    )(lens, qa, ka, va)


def attend_backward(
    query, keys, values, mixed, grad, lse, lens, causal, start, length, key_count, pairs, carried, last
):
    (qa, q0, rows), (ka, k0), (va, v0) = query, keys, values
    had = carried[0].shape[0] if carried else 0
    kept = BF if last else F32
    return pl.pallas_call(
        functools.partial(attend_bwd_kernel, causal, start, had),
        grid_spec=pltpu.PrefetchScalarGridSpec(
            num_scalar_prefetch=1,
            grid=(pairs,),
            in_specs=[
                columns(length, q0, rows),
                columns(key_count, k0),
                columns(key_count, v0),
                columns(length, mixed[1]),
                columns(length, grad[1]),
                pl.BlockSpec((1, 2, length), lambda g, lens: (mixed[1] + g, 0, 0)),
            ]
            + [columns(had, 0)] * (2 if carried else 0),
            out_specs=[columns(length, 0), columns(key_count, 0), columns(key_count, 0)],
            scratch_shapes=[
                pltpu.VMEM((PAIR, key_count), BF),
                pltpu.VMEM((key_count, PAIR), F32),
                pltpu.VMEM((key_count, PAIR), F32),
            ],
        ),
        out_shape=[
            jax.ShapeDtypeStruct((length, pairs * PAIR), BF),
            jax.ShapeDtypeStruct((key_count, pairs * PAIR), kept),
            jax.ShapeDtypeStruct((key_count, pairs * PAIR), kept),
        ],
        compiler_params=pltpu.CompilerParams(vmem_limit_bytes=50331648),
        cost_estimate=BRIEF,
        name="attend_causal_back" if causal else "attend_memory_back",
    )(lens, qa, ka, va, mixed[0], grad[0], lse, *(carried or ()))


def normed(value, gain):
    scale = lax.rsqrt(jnp.mean(value * value, axis=-1, keepdims=True) + EPS)
    return value * scale * gain


def norm_back(value, gain, grad):
    scale = lax.rsqrt(jnp.mean(value * value, axis=-1, keepdims=True) + EPS)
    unit = value * scale
    scaled = grad * gain
    inner = jnp.mean(scaled * unit, axis=-1, keepdims=True)
    return scale * (scaled - unit * inner), jnp.sum(grad * unit, axis=0, keepdims=True)


def enter_kernel(x_ref, w0_ref, w1_ref, columns_ref, h_ref, qkv_ref, gain_ref):
    rows = jnp.swapaxes(columns_ref[...].astype(F32), 0, 1)
    gain_ref[...] = rows[:8]
    h = normed(x_ref[...].astype(F32), rows[0:1]).astype(BF)
    h_ref[...] = h
    wide = w0_ref.shape[1]
    qkv_ref[:, pl.ds(0, wide)] = nn(h, w0_ref[...]).astype(BF)
    qkv_ref[:, pl.ds(wide, wide)] = nn(h, w1_ref[...]).astype(BF)


def product_kernel(x_ref, w_ref, o_ref):
    o_ref[...] = nn(x_ref[...], w_ref[...]).astype(BF)


def middle_kernel(x_ref, o_ref, gain_ref, wo_ref, cq_ref, x1_ref, h_ref, q_ref):
    x1 = x_ref[...].astype(F32) + nn(o_ref[...], wo_ref[...])
    h = normed(x1, gain_ref[1:2]).astype(BF)
    x1_ref[...] = x1
    h_ref[...] = h
    q_ref[...] = nn(h, cq_ref[...]).astype(BF)


def outer_kernel(x1_ref, o_ref, gain_ref, co_ref, x2_ref, h_ref):
    x2 = x1_ref[...] + nn(o_ref[...], co_ref[...])
    x2_ref[...] = x2
    h_ref[...] = normed(x2, gain_ref[2:3]).astype(BF)


def add_gain(step, ref, value):
    @pl.when(step == 0)
    def _():
        ref[...] = jnp.zeros_like(ref)

    ref[0:1, :] += value


def outer_back_kernel(dh_ref, x2_ref, g_ref, gain_ref, co_ref, d_ref, dx_ref, do_ref, dgain_ref):
    dx, dgain = norm_back(x2_ref[...], gain_ref[2:3], dh_ref[...].astype(F32))
    dx = g_ref[...].astype(F32) + dx
    d = dx.astype(BF)
    dx_ref[...] = dx
    d_ref[...] = d
    do_ref[...] = nt(d, co_ref[...]).astype(BF)
    add_gain(pl.program_id(0), dgain_ref, dgain)


def middle_back_kernel(
    dq_ref, x1_ref, dx2_ref, gain_ref, cq_ref, wo_ref, dx_ref, d_ref, do_ref, dgain_ref
):
    dx, dgain = norm_back(x1_ref[...], gain_ref[1:2], nt(dq_ref[...], cq_ref[...]))
    dx = dx2_ref[...] + dx
    d = dx.astype(BF)
    dx_ref[...] = dx
    d_ref[...] = d
    do_ref[...] = nt(d, wo_ref[...]).astype(BF)
    add_gain(pl.program_id(0), dgain_ref, dgain)


def enter_back_kernel(x_ref, dx1_ref, *refs):
    grads, gain_ref, weights, (out_ref, dgain_ref) = refs[:3], refs[3], refs[4:10], refs[10:]
    dh = 0.0
    for i, grad in enumerate(grads):
        for g in range(2):
            w = weights[2 * i + g]
            at = pl.ds(g * w.shape[1], w.shape[1])
            dh = dh + nt(grad[:, at], w[...])
    dx, dgain = norm_back(x_ref[...].astype(F32), gain_ref[0:1], dh)
    out_ref[...] = (dx1_ref[...] + dx).astype(BF)
    add_gain(pl.program_id(0), dgain_ref, dgain)


def by_tokens(kernel, tokens, blocked, whole, outs, name, c=0, kept=None):
    width = blocked[0][0].shape[1]
    steps = tokens // QB
    full = tokens if kept is None else 2 * tokens

    def rows(n, first):
        return pl.BlockSpec((QB, n), lambda i, first=first: (first + i, 0))

    def fixed(shape, index):
        return pl.BlockSpec(shape, lambda i, index=index: index)

    kept = kept or ()
    inputs = len(blocked) + len(whole)

    def run(*refs):
        kernel(*refs[:inputs], *refs[inputs + len(kept) :])

    return pl.pallas_call(
        run,
        grid=(steps,),
        in_specs=[rows(a.shape[1], first) for a, first in blocked]
        + [fixed(shape, index) for _, shape, index in whole]
        + [pl.BlockSpec(memory_space=pl.ANY)] * len(kept),
        out_specs=[
            fixed((8, width), (0, 0)) if n is None else rows(n, c * steps) for n, _ in outs
        ],
        out_shape=[
            jax.ShapeDtypeStruct((8, width) if n is None else (full, n), dtype)
            for n, dtype in outs
        ],
        input_output_aliases={inputs + i: i for i in range(len(kept))},
        compiler_params=pltpu.CompilerParams(vmem_limit_bytes=25165824),
        cost_estimate=BRIEF,
        name=name,
    )(*[a for a, _ in blocked], *[a for a, _, _ in whole], *kept)


def weight_grad_kernel(*refs):
    *ins, o_ref = refs
    total = tn(ins[0][...], ins[1][...])
    for i in range(2, len(ins), 2):
        total = total + tn(ins[i][...], ins[i + 1][...])
    o_ref[...] = total.astype(BF)


def weight_grad(pairs, columns_at_once):
    rows, width = pairs[0][0].shape[1], pairs[0][1].shape[1]
    specs = []
    for x, grad in pairs:
        specs.append(pl.BlockSpec((x.shape[0], columns_at_once), lambda i: (0, i)))
        specs.append(pl.BlockSpec(grad.shape, lambda i: (0, 0)))
    return pl.pallas_call(
        weight_grad_kernel,
        grid=(rows // columns_at_once,),
        in_specs=specs,
        out_specs=pl.BlockSpec((columns_at_once, width), lambda i: (i, 0)),
        out_shape=jax.ShapeDtypeStruct((rows, width), BF),
        compiler_params=pltpu.CompilerParams(
            vmem_limit_bytes=41943040 if width > 768 or rows > 768 else 25165824
        ),
        cost_estimate=BRIEF,
        name="weight_grad",
    )(*[a for pair in pairs for a in pair])


GELU_A = 0.7978845608028654
GELU_B = 0.044715


def feed_kernel(groups, ff, step, *refs):
    h_refs, g_refs, (gu_ref, down_ref) = refs[:groups], refs[groups : 2 * groups], refs[2 * groups : 2 * groups + 2]
    outs = refs[-2 * groups - 4 :]
    y_refs, dh_refs, (hid_ref, dgu_ref, h_ref, g_ref) = outs[:groups], outs[groups:-4], outs[-4:]
    part = h_refs[0].shape[0]
    for j in range(groups):
        h_ref[pl.ds(j * part, part), :] = h_refs[j][...]
        g_ref[pl.ds(j * part, part), :] = g_refs[j][0]
    y, dh = 0.0, 0.0
    for c in range(0, ff, step):
        wg = gu_ref[:, pl.ds(c, step)]
        wu = gu_ref[:, pl.ds(ff + c, step)]
        wd = down_ref[pl.ds(c, step), :]
        gate, up, dhid = nn(h_ref[...], wg), nn(h_ref[...], wu), nt(g_ref[...], wd)
        square = gate * gate
        th = jnp.tanh(gate * (GELU_A + (GELU_A * GELU_B) * square))
        half = 0.5 + 0.5 * th
        act = gate * half
        slope = half + (0.5 * gate) * (1.0 - th * th) * (
            GELU_A + (3.0 * GELU_A * GELU_B) * square
        )
        hidden = (act * up).astype(BF)
        dgate = (dhid * up * slope).astype(BF)
        dup = (dhid * act).astype(BF)
        hid_ref[:, pl.ds(c, step)] = hidden
        dgu_ref[:, pl.ds(c, step)] = dgate
        dgu_ref[:, pl.ds(ff + c, step)] = dup
        y = y + nn(hidden, wd)
        dh = dh + nt(dgate, wg) + nt(dup, wu)
    for j in range(groups):
        y_refs[j][0] = y[j * part : (j + 1) * part].astype(BF)
        dh_refs[j][...] = dh[j * part : (j + 1) * part].astype(BF)


def feed(c, h_parts, g_parts, wgu, wd, kept):
    groups = len(h_parts)
    part, width = h_parts[0].shape
    ff = wd.shape[0]
    tokens = groups * part

    def whole(a):
        return pl.BlockSpec(a.shape, lambda i: (0,) * a.ndim)

    def halves(n):
        return pl.BlockSpec((tokens, n), lambda i: (c, 0))

    wide = (ff, 2 * ff, width, width)
    of_half = pl.BlockSpec((1, part, width), lambda i: (c, 0, 0))
    made = [0 + i for i in range(groups)] + [2 * groups + i for i in range(len(wide))]
    return pl.pallas_call(
        functools.partial(feed_kernel, groups, ff, 512),
        grid=(1,),
        in_specs=[whole(h) for h in h_parts]
        + [of_half] * groups
        + [whole(wgu), whole(wd)]
        + [pl.BlockSpec(memory_space=pl.ANY)] * len(kept),
        out_specs=[of_half] * groups
        + [whole(h) for h in h_parts]
        + [halves(n) for n in wide],
        out_shape=[jax.ShapeDtypeStruct((2, part, width), BF)] * groups
        + [jax.ShapeDtypeStruct((part, width), BF)] * groups
        + [jax.ShapeDtypeStruct((2 * tokens, n), BF) for n in wide],
        input_output_aliases={2 * groups + 2 + i: made[i] for i in range(len(kept))},
        compiler_params=pltpu.CompilerParams(vmem_limit_bytes=58720256),
        cost_estimate=BRIEF,
        name="feed",
    )(*h_parts, *g_parts, wgu, wd, *kept)


def pick_kernel(modes, halves, source, mode, x_ref, *o_refs):
    per_mode = x_ref.shape[0] // modes
    for j in range(modes):
        first = jnp.bitwise_xor(mode[0], j) * per_mode

        def move(r, carry, j=j, first=first):
            row = source[first + r]
            if halves:
                for c in range(halves):
                    o_refs[j][c, r] = x_ref[row, c]
            else:
                o_refs[j][r] = x_ref[row]
            return carry

        lax.fori_loop(0, per_mode, move, 0)


def put_kernel(modes, halves, source, mode, *refs):
    o_ref = refs[-1]
    per_mode = o_ref.shape[0] // modes
    for j in range(modes):
        first = jnp.bitwise_xor(mode[0], j) * per_mode

        def move(r, carry, j=j, first=first):
            row = source[first + r]
            if halves:
                for c in range(halves):
                    o_ref[row, c] = refs[j][c, r]
            else:
                o_ref[row] = refs[j][r]
            return carry

        lax.fori_loop(0, per_mode, move, 0)


def mode_number():
    return lax.axis_index("mode").astype(jnp.int32)[None]


def by_rows(kernel, source, ins, outs, name):
    def whole(shape):
        return pl.BlockSpec(shape, lambda i, source, mode: (0,) * len(shape))

    return pl.pallas_call(
        kernel,
        grid_spec=pltpu.PrefetchScalarGridSpec(
            num_scalar_prefetch=2,
            grid=(1,),
            in_specs=[whole(a.shape) for a in ins],
            out_specs=[whole(shape) for shape in outs],
        ),
        out_shape=[jax.ShapeDtypeStruct(shape, BF) for shape in outs],
        compiler_params=pltpu.CompilerParams(vmem_limit_bytes=16777216),
        cost_estimate=pl.CostEstimate(
            flops=0, bytes_accessed=4 * sum(a.size for a in ins), transcendentals=0
        ),
        name=name,
    )(source, mode_number(), *ins)


def to_mode(spread, source):
    per_mode, modes = lax.axis_size("dp"), lax.axis_size("mode")
    piece = spread.shape[-2:]
    if spread.ndim == 4:
        outs = [(spread.shape[1], per_mode) + piece] * modes
    else:
        outs = [(per_mode,) + piece] * modes
    parts = by_rows(
        functools.partial(pick_kernel, modes, spread.shape[1] if spread.ndim == 4 else 0),
        source,
        [spread],
        outs,
        "pick",
    )
    got = [parts[0]] + [swap(parts[j], per_mode * j) for j in range(1, modes)]
    if spread.ndim == 4:
        return [part.reshape(part.shape[0], -1, part.shape[-1]) for part in got]
    return [part.reshape(-1, part.shape[-1]) for part in got]


def swap_modes(parts):
    per_mode = lax.axis_size("dp")
    lead = parts[0].shape[:-2]
    parts = [part.reshape(lead + (per_mode, -1, part.shape[-1])) for part in parts]
    return [parts[0]] + [swap(parts[j], per_mode * j) for j in range(1, len(parts))]


def put_back(parts, source):
    halves = parts[0].shape[0] if parts[0].ndim == 4 else 0
    shape = (lax.axis_size(ALL),) + ((halves,) if halves else ()) + parts[0].shape[-2:]
    return by_rows(
        functools.partial(put_kernel, len(parts), halves), source, parts, [shape], "put"
    )[0]


def dealt(value):
    count = lax.axis_size(ALL)
    return value.reshape(count, -1, value.shape[-1])


def to_all(value):
    return lax.all_to_all(value, ALL, 0, 0, tiled=True)


def swap(value, j):
    count = lax.axis_size(ALL)
    return lax.ppermute(value, ALL, [(i, i ^ j) for i in range(count)])


def device_number():
    return lax.axis_index(ALL).astype(jnp.int32)[None]


def place_kernel(me, even_ref, odd_ref, *o_refs):
    first = 0
    for o_ref in o_refs:
        at = pl.ds(first, o_ref.shape[2])
        first += o_ref.shape[2]
        for t in range(even_ref.shape[0]):
            o_ref[jnp.bitwise_xor(2 * t, me[0])] = even_ref[t, :, at]
            o_ref[jnp.bitwise_xor(2 * t + 1, me[0])] = odd_ref[t, :, at]


def place(even, odd, widths, number):
    count, rows, width = even.shape
    shapes = [(2 * count, rows, w) for w in widths]

    def whole(shape):
        return pl.BlockSpec(shape, lambda i, me: (0, 0, 0))

    return pl.pallas_call(
        place_kernel,
        grid_spec=pltpu.PrefetchScalarGridSpec(
            num_scalar_prefetch=1,
            grid=(1,),
            in_specs=[whole(even.shape)] * 2,
            out_specs=[whole(shape) for shape in shapes],
        ),
        out_shape=[jax.ShapeDtypeStruct(shape, even.dtype) for shape in shapes],
        compiler_params=pltpu.CompilerParams(vmem_limit_bytes=29360128),
        cost_estimate=BRIEF,
        name="place",
    )(number, even, odd)


def pack_kernel(counts, *refs):
    ins, outs = refs[: sum(counts)], refs[sum(counts) :]
    taken = 0
    for count, o_ref in zip(counts, outs):
        first = 0
        for part in ins[taken : taken + count]:
            o_ref[:, pl.ds(first, part.shape[1])] = part[...]
            first += part.shape[1]
        taken += count


def pack(*lists):
    cut = lambda e: e if not isinstance(e, tuple) else e[0]
    shape = lambda e: e.shape if not isinstance(e, tuple) else (e[0].shape[0], e[2])
    at = lambda e: 0 if not isinstance(e, tuple) else e[1] // e[2]
    entries = [e for group in lists for e in group]
    return pl.pallas_call(
        functools.partial(pack_kernel, [len(group) for group in lists]),
        grid=(1,),
        in_specs=[pl.BlockSpec(shape(e), lambda i, e=e: (0, at(e))) for e in entries],
        out_specs=[
            pl.BlockSpec((shape(group[0])[0], sum(shape(e)[1] for e in group)), lambda i: (0, 0))
            for group in lists
        ],
        out_shape=[
            jax.ShapeDtypeStruct((shape(group[0])[0], sum(shape(e)[1] for e in group)), BF)
            for group in lists
        ],
        name="pack",
    )(*[cut(e) for e in entries])


def gather_column(piece, late=None):
    per_mode = lax.axis_size("dp")
    got = [swap(piece, 2 * j) for j in range(1, per_mode // 2)]
    return jnp.stack([piece] + (got if late is None else tied(got, late)))


def gather_rest(column, widths, late=None):
    per_mode, modes = lax.axis_size("dp"), lax.axis_size("mode")
    got = [swap(column, per_mode * j) for j in range(1, modes)]
    if late is not None:
        got = tied(got, late)
    plane = jnp.stack([column] + got)
    plane = plane.reshape((-1,) + column.shape[1:])
    placed = place(plane, swap(plane, 1), widths, device_number())
    return [a.reshape(-1, a.shape[2]) for a in placed]


def take_kernel(parts, me, *refs):
    ins, (keep_ref, send_ref) = refs[:parts], refs[parts:]
    first = 0
    for in_ref in ins:
        at = pl.ds(first, in_ref.shape[2])
        first += in_ref.shape[2]
        for t in range(keep_ref.shape[0]):
            keep_ref[t, :, at] = in_ref[jnp.bitwise_xor(2 * t, me[0])]
            send_ref[t, :, at] = in_ref[jnp.bitwise_xor(2 * t + 1, me[0])]


def take(parts):
    count, rows = parts[0].shape[:2]
    width = sum(part.shape[2] for part in parts)
    half = jax.ShapeDtypeStruct((count // 2, rows, width), parts[0].dtype)

    def whole(shape):
        return pl.BlockSpec(shape, lambda i, me: (0, 0, 0))

    return pl.pallas_call(
        functools.partial(take_kernel, len(parts)),
        grid_spec=pltpu.PrefetchScalarGridSpec(
            num_scalar_prefetch=1,
            grid=(1,),
            in_specs=[whole(part.shape) for part in parts],
            out_specs=[whole(half.shape)] * 2,
        ),
        out_shape=[half, half],
        compiler_params=pltpu.CompilerParams(vmem_limit_bytes=50331648),
        cost_estimate=BRIEF,
        name="take",
    )(device_number(), *parts)


def add_up(parts):
    return functools.reduce(jnp.add, [part.astype(F32) for part in parts])


def scatter_pairs(parts):
    count = lax.axis_size(ALL)
    parts = [part.reshape(count, part.shape[0] // count, part.shape[1]) for part in parts]
    keep, send = take(parts)
    return add_up([keep, swap(send, 1)]).astype(BF)


def scatter_plane(pair):
    per_mode, modes = lax.axis_size("dp"), lax.axis_size("mode")
    plane = pair.reshape((modes, per_mode // 2) + pair.shape[1:])
    return add_up([plane[0]] + [swap(plane[j], per_mode * j) for j in range(1, modes)]).astype(BF)


def scatter_column(column):
    per_mode = lax.axis_size("dp")
    return add_up([column[0]] + [swap(column[j], 2 * j) for j in range(1, per_mode // 2)])


def later(lens, tokens):
    return lens - jnp.array([tokens, 0], jnp.int32)


def tied(first, second):
    return lax.optimization_barrier((first, second))[0]


def lanes_of(*vectors):
    columns_ = jnp.stack(vectors, axis=1)
    return jnp.pad(columns_, ((0, 0), (0, 128 - len(vectors))))


def on_device(
    rows,
    memory,
    cotangent,
    mode_ids,
    target_lengths,
    encoder_lengths,
    self_q,
    self_k,
    self_v,
    self_o,
    self_gain,
    cross_q,
    cross_k,
    cross_v,
    cross_o,
    cross_gain,
    ffn_gain,
    ffn_gate,
    ffn_up,
    ffn_down,
):
    devices = lax.axis_size(ALL)
    per_mode = lax.axis_size("dp")
    here = lax.axis_index(ALL)
    width = rows.shape[2]
    ff = ffn_gate.shape[2]
    index = jnp.arange(devices, dtype=jnp.int32)
    same = mode_ids[:, None] == mode_ids[None, :]
    earlier = index[None, :] < index[:, None]
    rank = jnp.sum(jnp.where(same & earlier, 1, 0), axis=1).astype(jnp.int32)
    target = mode_ids * per_mode + rank
    source = jnp.sum(
        jnp.where(target[:, None] == index[None, :], index[:, None], 0), axis=0
    ).astype(jnp.int32)
    live_len = jnp.sum(jnp.where(index == here, target_lengths, 0))
    memory_len = jnp.sum(jnp.where(index == here, encoder_lengths, 0))
    lens = jnp.stack([live_len, memory_len]).astype(jnp.int32)
    tokens, memory_row, incoming = rows[0], memory[0], cotangent[0]
    length = tokens.shape[0]
    half = length // 2
    key_count = memory_row.shape[0]
    valid = (jnp.arange(length, dtype=jnp.int32) < live_len)[:, None]
    grad_low = jnp.where(valid, incoming, jnp.zeros_like(incoming))

    group_pairs = HEADS // 4
    part = group_pairs * PAIR

    def of_group(g):
        return tuple((a, g * part, part) for a in (self_q, self_k, self_v))

    own_piece, rest_piece = pack(
        of_group(0) + of_group(1) + (lanes_of(self_gain, cross_gain, ffn_gain),),
        (self_o, cross_q, cross_k, cross_v, cross_o),
    )
    column = gather_column(own_piece)
    own_0, own_1, gain_columns = gather_rest(column, (3 * part, 3 * part, 128))
    crossing = lax.all_gather(rest_piece, ALL, axis=0, tiled=True)

    def weight(array, i, wide=width):
        return (array, (width, wide), (0, i))

    h1, qkv, gains = by_tokens(
        enter_kernel,
        length,
        [(tokens, 0)],
        [(a, a.shape, (0, 0)) for a in (own_0, own_1, gain_columns)],
        [(width, BF), (6 * part, BF), (None, F32)],
        "enter",
    )
    all_gains = (gains, gains.shape, (0, 0))
    pairs = HEADS // 2

    def of_pair(i):
        return lambda g: (g // group_pairs) * 3 * group_pairs + i * group_pairs + g % group_pairs

    grad_dealt = grad_low.reshape(2, devices, -1, width).swapaxes(0, 1)
    grad_spread = to_all(grad_dealt)

    wgu = lax.all_gather(
        jnp.concatenate([ffn_gate[0], ffn_up[0]], axis=1), "dp", axis=0, tiled=True
    )
    wd = lax.all_gather(ffn_down[0], "dp", axis=0, tiled=True)

    mixed, log_self = attend_forward(
        (qkv, of_pair(0), 0),
        (qkv, of_pair(1)),
        (qkv, of_pair(2)),
        lens,
        True,
        length,
        length,
        pairs,
    )
    wo, cq, ckv, co = (
        crossing[:, i * width : j * width] for i, j in ((0, 1), (1, 2), (2, 4), (4, 5))
    )

    def forward_middle(c):
        first = c * (half // QB)
        return by_tokens(
            middle_kernel,
            half,
            [(tokens, first), (mixed, first)],
            [all_gains, weight(wo, 0), weight(cq, 0)],
            [(width, F32), (width, BF), (width, BF)],
            "middle",
        )

    def forward_cross(c, query):
        return attend_forward(
            (query, 0, 0),
            (cross_kv, 0),
            (cross_kv, pairs),
            later(lens, c * half),
            False,
            half,
            key_count,
            pairs,
        )

    def forward_outer(x1, cross_mixed):
        return by_tokens(
            outer_kernel,
            half,
            [(x1, 0), (cross_mixed, 0)],
            [all_gains, weight(co, 0)],
            [(width, F32), (width, BF)],
            "outer",
        )

    x1_a, h2_a, query_a = forward_middle(0)
    (cross_kv,) = by_tokens(
        product_kernel,
        key_count,
        [(memory_row, 0)],
        [(ckv, ckv.shape, (0, 0))],
        [(2 * width, BF)],
        "memory",
    )
    cross_a, log_cross_a = forward_cross(0, query_a)
    x2_a, h3_a = forward_outer(x1_a, cross_a)
    spread_a = to_all(dealt(tied(h3_a, grad_spread)))
    grad_parts = to_mode(grad_spread, source)
    x1_b, h2_b, query_b = forward_middle(1)
    query_b = tied(query_b, h3_a)
    cross_b, log_cross_b = forward_cross(1, query_b)
    cross_b, grad_parts = lax.optimization_barrier((cross_b, grad_parts))
    x2_b, h3_b = forward_outer(x1_b, cross_b)
    routed_a = to_mode(tied(spread_a, cross_b), source)
    spread_b = to_all(dealt(h3_b))

    modes = len(routed_a)
    routed_b = to_mode(spread_b, source)
    fed_a = feed(0, tied(routed_a, routed_b), grad_parts, wgu, wd, ())
    y_a, dh_a, kept_a = fed_a[:modes], fed_a[modes : 2 * modes], fed_a[2 * modes :]
    back_a = put_back(swap_modes(dh_a), source)
    routed_b, back_a = lax.optimization_barrier((routed_b, back_a))
    home_a = to_all(back_a).reshape(half, width)
    fed_b = feed(1, routed_b, grad_parts, wgu, wd, y_a + kept_a)
    y, dh_b = fed_b[:modes], fed_b[modes : 2 * modes]
    hidden, dgu, routed_h, routed_grad = fed_b[2 * modes :]
    back_b = swap_modes(dh_b)
    grad_wd = weight_grad([(tied(hidden, home_a), routed_grad)], 512)
    grad_wgu = weight_grad([(routed_h, dgu)], 256)
    grad_wgu, back_b = lax.optimization_barrier((tied(grad_wgu, grad_wd), back_b))
    back_b = put_back(back_b, source)
    sum_wgu = lax.psum_scatter(grad_wgu, "dp", scatter_dimension=0, tiled=True)
    sum_wd = lax.psum_scatter(grad_wd, "dp", scatter_dimension=0, tiled=True)
    home_b = to_all(back_b).reshape(half, width)
    home_a = tied(home_a, back_b)
    y_mode = swap_modes(tied(y, back_b))

    def back_outer(c, dh, x2):
        return by_tokens(
            outer_back_kernel,
            half,
            [(dh, 0), (x2, 0), (grad_low, c * (half // QB))],
            [all_gains, weight(co, 0)],
            [(width, BF), (width, F32), (width, BF), (None, F32)],
            "outer_back",
        )

    def back_middle(c, dq, x1, dx2, kept):
        return by_tokens(
            middle_back_kernel,
            half,
            [(dq, 0), (x1, 0), (dx2, 0)],
            [all_gains, weight(cq, 0), weight(wo, 0)],
            [(width, F32), (width, BF), (width, BF), (None, F32)],
            "middle_back",
            c,
            kept,
        )

    def back_cross(c, query, mixed, grad, lse, carried):
        return attend_backward(
            (query, 0, 0),
            (cross_kv, 0),
            (cross_kv, pairs),
            (mixed, 0),
            (grad, 0),
            lse,
            later(lens, c * half),
            False,
            0,
            half,
            key_count,
            pairs,
            carried,
            c == 1,
        )

    def back_self(grad):
        return attend_backward(
            (qkv, of_pair(0), 0),
            (qkv, of_pair(1)),
            (qkv, of_pair(2)),
            (mixed, 0),
            (grad, 0),
            log_self,
            lens,
            True,
            0,
            length,
            length,
            pairs,
            None,
            True,
        )

    d2_a, dx2_a, do2_a, dgain_ffn_a = back_outer(0, home_a, x2_a)
    dcq_a, dck_a, dcv_a = back_cross(0, query_a, cross_a, do2_a, log_cross_a, None)
    *halves, dgain_cross_a = back_middle(0, dcq_a, x1_a, dx2_a, ())
    home_b, y_mode = lax.optimization_barrier((tied(home_b, halves), y_mode))
    d2_b, dx2_b, do2_b, dgain_ffn_b = back_outer(1, home_b, x2_b)
    y_put, do2_b = lax.optimization_barrier((put_back(y_mode, source), do2_b))
    y_home = to_all(y_put)
    dcq_b, dck, dcv = back_cross(1, query_b, cross_b, do2_b, log_cross_b, (dck_a, dcv_a))
    dx1, d1, do1, dgain_cross_b = back_middle(1, dcq_b, x1_b, dx2_b, halves)
    cross_pair = scatter_pairs(
        [
            weight_grad([(h2_a, dcq_a), (h2_b, dcq_b)], 256),
            weight_grad([(memory_row, dck)], 256),
            weight_grad([(memory_row, dcv)], 256),
            weight_grad([(cross_a, d2_a), (cross_b, d2_b)], 256),
            weight_grad([(mixed, d1)], 256),
        ]
    )
    do1, cross_pair = lax.optimization_barrier((do1, cross_pair))
    cross_plane = scatter_plane(cross_pair)
    grads = back_self(do1)
    grads, cross_plane, y_home, sum_wgu, sum_wd = lax.optimization_barrier(
        (grads, cross_plane, y_home, sum_wgu, sum_wd)
    )
    cross_sum = scatter_column(cross_plane)
    own_pair = scatter_pairs([tn(h1, d).astype(BF) for d in grads])
    own_plane = scatter_plane(own_pair)
    grads, dck, dcv = tied((grads, dck, dcv), own_pair)
    y_home = tied(y_home, own_plane)
    grad_tokens, dgain_self = by_tokens(
        enter_back_kernel,
        length,
        [(tokens, 0), (dx1, 0)] + [(d, 0) for d in grads],
        [all_gains] + [weight(own, i, part) for i in range(3) for own in (own_0, own_1)],
        [(width, BF), (None, F32)],
        "enter_back",
    )
    gain_grads = jnp.stack(
        [dgain_self[0], dgain_cross_a[0] + dgain_cross_b[0], dgain_ffn_a[0] + dgain_ffn_b[0]]
    )
    own_plane, gain_grads = lax.optimization_barrier((own_plane, gain_grads))
    own_sum = scatter_column(own_plane)
    gain_grads = gain_grads.reshape(3, devices, -1).swapaxes(0, 1)
    gain_sums = jnp.sum(to_all(gain_grads), axis=0)
    grad_memory = (nt(dck, ckv[:, :width]) + nt(dcv, ckv[:, width:])).astype(BF)
    y = y_home.swapaxes(0, 1).reshape(length, width)
    result = jnp.where(valid, jnp.concatenate([x2_a, x2_b]) + y.astype(F32), 0.0).astype(BF)

    def block(value, i):
        return value[:, i * width : (i + 1) * width]

    return (
        result[None],
        grad_tokens[None],
        grad_memory[None],
        block(own_sum, 0),
        block(own_sum, 1),
        block(own_sum, 2),
        block(cross_sum, 4),
        gain_sums[0],
        block(cross_sum, 0),
        block(cross_sum, 1),
        block(cross_sum, 2),
        block(cross_sum, 3),
        gain_sums[1],
        gain_sums[2],
        sum_wgu[:, :ff].astype(F32)[None],
        sum_wgu[:, ff:].astype(F32)[None],
        sum_wd.astype(F32)[None],
    )


def solution(mesh):
    rows = P(ALL, None, None)
    weight = P(ALL, None)
    gain = P(ALL)
    feeding = P("mode", "dp", None)
    return jax.shard_map(
        on_device,
        mesh=mesh,
        in_specs=(
            (rows,) * 3
            + (P(),) * 3
            + (weight,) * 4
            + (gain,)
            + (weight,) * 4
            + (gain,) * 2
            + (feeding,) * 3
        ),
        out_specs=(
            (rows,) * 3
            + (weight,) * 4
            + (gain,)
            + (weight,) * 4
            + (gain,) * 2
            + (feeding,) * 3
        ),
        check_vma=False,
    )
```

```python
import functools

import jax
import jax.numpy as jnp
from jax import lax
from jax.experimental import pallas as pl
from jax.experimental.pallas import tpu as pltpu
from jax.sharding import PartitionSpec as P

HEADS = 12
HEAD_DIM = 64
PAIR = 2 * HEAD_DIM
EPS = 1e-06
NEG = -1e30
SCALE = HEAD_DIM ** -0.5
QB = 256
AB = 512
FS = 512
ALL = ("mode", "dp")
BF = jnp.bfloat16
F32 = jnp.float32
VMEM = 56 * 2**20
BRIEF = pl.CostEstimate(flops=10**6, bytes_accessed=10**4, transcendentals=0)


def nt(left, right):
    return lax.dot_general(left, right, (((1,), (1,)), ((), ())), preferred_element_type=F32)


def nn(left, right):
    return jnp.dot(left, right, preferred_element_type=F32)


def tn(left, right):
    return lax.dot_general(left, right, (((0,), (0,)), ((), ())), preferred_element_type=F32)


def head_lanes(value, h):
    lane = lax.broadcasted_iota(jnp.int32, value.shape, 1)
    return jnp.where((lane >= HEAD_DIM) == (h == 1), value, jnp.zeros_like(value))


def masks(causal, key_count, qb, limit):
    if causal:
        parts = []
        if qb:
            parts.append((0, qb * AB, None))
        row = lax.broadcasted_iota(jnp.int32, (AB, AB), 0)
        col = lax.broadcasted_iota(jnp.int32, (AB, AB), 1)
        parts.append((qb * AB, AB, row <= col))
        return parts
    row = lax.broadcasted_iota(jnp.int32, (key_count, AB), 0)
    return [(0, key_count, row < limit)]


def attend_fwd_kernel(causal, lens, q_ref, k_ref, v_ref, o_ref, lse_ref):
    live, limit = lens[0], lens[1]
    length, key_count = q_ref.shape[0], k_ref.shape[0]
    block = min(AB, length)
    first_head = lax.broadcasted_iota(jnp.int32, (1, PAIR), 1) < HEAD_DIM
    for start in range(0, length, block):
        at = pl.ds(start, block)

        @pl.when(start < live)
        def _(start=start, at=at):
            query = q_ref[at, :] * jnp.asarray(SCALE, BF)
            if causal:
                row = lax.broadcasted_iota(jnp.int32, (block, block), 0)
                col = lax.broadcasted_iota(jnp.int32, (block, block), 1)
                parts = [(0, start, None)] if start else []
                parts.append((start, block, col <= row))
            else:
                col = lax.broadcasted_iota(jnp.int32, (block, key_count), 1)
                parts = [(0, key_count, col < limit)]
            outs, logs = [], []
            for h in range(2):
                mine = head_lanes(query, h)
                scores = []
                for first, count, mask in parts:
                    s = nt(mine, k_ref[pl.ds(first, count), :])
                    scores.append(s if mask is None else jnp.where(mask, s, NEG))
                top = functools.reduce(
                    jnp.maximum, [jnp.max(s, axis=1, keepdims=True) for s in scores]
                )
                total, mixed = 0.0, 0.0
                for (first, count, _), s in zip(parts, scores):
                    p = jnp.exp(s - top)
                    total = total + jnp.sum(p, axis=1, keepdims=True)
                    mixed = mixed + nn(p.astype(BF), v_ref[pl.ds(first, count), :])
                outs.append(mixed / total)
                logs.append(top + jnp.log(total))
            o_ref[at, :] = jnp.where(first_head, outs[0], outs[1]).astype(BF)
            rows = jnp.swapaxes(jnp.where(first_head, logs[0], logs[1]), 0, 1)
            lse_ref[0, pl.ds(0, 1), at] = rows[0:1]
            lse_ref[0, pl.ds(1, 1), at] = rows[HEAD_DIM : HEAD_DIM + 1]

        @pl.when(start >= live)
        def _(at=at):
            o_ref[at, :] = jnp.zeros((block, PAIR), BF)
            lse_ref[0, pl.ds(0, 2), at] = jnp.zeros((2, block), F32)


def attend_bwd_kernel(causal, start, carried, lens, *refs):
    q_ref, k_ref, v_ref, o_ref, do_ref, lse_ref = refs[:6]
    more, (dq_ref, dk_ref, dv_ref, kt, dk, dv) = refs[6:-6], refs[-6:]
    live, limit = lens[0], lens[1]
    length, key_count = q_ref.shape[0], k_ref.shape[0]
    kt[...] = jnp.swapaxes(k_ref[...].astype(F32), 0, 1).astype(BF)
    if carried < key_count:
        fresh = pl.ds(carried, key_count - carried)
        dk[fresh, :] = jnp.zeros((key_count - carried, PAIR), F32)
        dv[fresh, :] = jnp.zeros((key_count - carried, PAIR), F32)
    if carried:
        dk[pl.ds(0, carried), :] = more[0][...]
        dv[pl.ds(0, carried), :] = more[1][...]
    for block in range(length // AB):
        at = pl.ds(block * AB, AB)
        qb = start // AB + block

        @pl.when(qb * AB < live)
        def _(qb=qb, at=at):
            query = q_ref[at, :] * jnp.asarray(SCALE, BF)
            grad = do_ref[at, :]
            inner = jnp.swapaxes(o_ref[at, :].astype(F32) * grad.astype(F32), 0, 1)
            parts = masks(causal, key_count, qb, limit)
            sums = [[0.0, 0.0] for _ in parts]
            outs = []
            for h in range(2):
                mine = head_lanes(query, h)
                grad_mine = head_lanes(grad, h)
                lse = lse_ref[0, pl.ds(h, 1), at]
                delta = jnp.sum(inner[h * HEAD_DIM : (h + 1) * HEAD_DIM], axis=0, keepdims=True)
                grad_query = 0.0
                for i, (first, count, mask) in enumerate(parts):
                    keys = pl.ds(first, count)
                    p = jnp.exp(nt(k_ref[keys, :], mine) - lse)
                    if mask is not None:
                        p = jnp.where(mask, p, 0.0)
                    dp = nt(v_ref[keys, :], grad_mine)
                    ds = (p * (dp - delta)).astype(BF)
                    sums[i][0] = sums[i][0] + nn(ds, mine)
                    sums[i][1] = sums[i][1] + nn(p.astype(BF), grad_mine)
                    grad_query = grad_query + nn(kt[pl.ds(h * HEAD_DIM, HEAD_DIM), keys], ds)
                outs.append(grad_query * SCALE)
            for (first, count, _), (sum_k, sum_v) in zip(parts, sums):
                dk[pl.ds(first, count), :] += sum_k
                dv[pl.ds(first, count), :] += sum_v
            dq_ref[at, :] = jnp.swapaxes(jnp.concatenate(outs, axis=0), 0, 1).astype(BF)

        @pl.when(qb * AB >= live)
        def _(at=at):
            dq_ref[at, :] = jnp.zeros((AB, PAIR), BF)

    dk_ref[...] = dk[...].astype(dk_ref.dtype)
    dv_ref[...] = dv[...].astype(dv_ref.dtype)


def columns(rows, first, row_block=0):
    at = first if callable(first) else lambda g: first + g
    return pl.BlockSpec((rows, PAIR), lambda g, lens: (row_block, at(g)))


def attend_forward(query, keys, values, lens, causal, length, key_count, pairs):
    (qa, q0, rows), (ka, k0), (va, v0) = query, keys, values
    return pl.pallas_call(
        functools.partial(attend_fwd_kernel, causal),
        grid_spec=pltpu.PrefetchScalarGridSpec(
            num_scalar_prefetch=1,
            grid=(pairs,),
            in_specs=[
                columns(length, q0, rows),
                columns(key_count, k0),
                columns(key_count, v0),
            ],
            out_specs=[
                columns(length, 0),
                pl.BlockSpec((1, 2, length), lambda g, lens: (g, 0, 0)),
            ],
        ),
        out_shape=[
            jax.ShapeDtypeStruct((length, pairs * PAIR), BF),
            jax.ShapeDtypeStruct((pairs, 2, length), F32),
        ],
        compiler_params=pltpu.CompilerParams(vmem_limit_bytes=41943040),
        cost_estimate=BRIEF,
        name="attend_causal" if causal else "attend_memory",
    )(lens, qa, ka, va)


def attend_backward(
    query, keys, values, mixed, grad, lse, lens, causal, start, length, key_count, pairs, carried, last
):
    (qa, q0, rows), (ka, k0), (va, v0) = query, keys, values
    had = carried[0].shape[0] if carried else 0
    kept = BF if last else F32
    return pl.pallas_call(
        functools.partial(attend_bwd_kernel, causal, start, had),
        grid_spec=pltpu.PrefetchScalarGridSpec(
            num_scalar_prefetch=1,
            grid=(pairs,),
            in_specs=[
                columns(length, q0, rows),
                columns(key_count, k0),
                columns(key_count, v0),
                columns(length, mixed[1]),
                columns(length, grad[1]),
                pl.BlockSpec((1, 2, length), lambda g, lens: (mixed[1] + g, 0, 0)),
            ]
            + [columns(had, 0)] * (2 if carried else 0),
            out_specs=[columns(length, 0), columns(key_count, 0), columns(key_count, 0)],
            scratch_shapes=[
                pltpu.VMEM((PAIR, key_count), BF),
                pltpu.VMEM((key_count, PAIR), F32),
                pltpu.VMEM((key_count, PAIR), F32),
            ],
        ),
        out_shape=[
            jax.ShapeDtypeStruct((length, pairs * PAIR), BF),
            jax.ShapeDtypeStruct((key_count, pairs * PAIR), kept),
            jax.ShapeDtypeStruct((key_count, pairs * PAIR), kept),
        ],
        compiler_params=pltpu.CompilerParams(vmem_limit_bytes=50331648),
        cost_estimate=BRIEF,
        name="attend_causal_back" if causal else "attend_memory_back",
    )(lens, qa, ka, va, mixed[0], grad[0], lse, *(carried or ()))


def normed(value, gain):
    scale = lax.rsqrt(jnp.mean(value * value, axis=-1, keepdims=True) + EPS)
    return value * scale * gain


def norm_back(value, gain, grad):
    scale = lax.rsqrt(jnp.mean(value * value, axis=-1, keepdims=True) + EPS)
    unit = value * scale
    scaled = grad * gain
    inner = jnp.mean(scaled * unit, axis=-1, keepdims=True)
    return scale * (scaled - unit * inner), jnp.sum(grad * unit, axis=0, keepdims=True)


def enter_kernel(x_ref, w0_ref, w1_ref, columns_ref, h_ref, qkv_ref, gain_ref):
    rows = jnp.swapaxes(columns_ref[...].astype(F32), 0, 1)
    gain_ref[...] = rows[:8]
    h = normed(x_ref[...].astype(F32), rows[0:1]).astype(BF)
    h_ref[...] = h
    wide = w0_ref.shape[1]
    qkv_ref[:, pl.ds(0, wide)] = nn(h, w0_ref[...]).astype(BF)
    qkv_ref[:, pl.ds(wide, wide)] = nn(h, w1_ref[...]).astype(BF)


def product_kernel(x_ref, w_ref, o_ref):
    o_ref[...] = nn(x_ref[...], w_ref[...]).astype(BF)


def middle_kernel(x_ref, o_ref, gain_ref, wo_ref, cq_ref, x1_ref, h_ref, q_ref):
    x1 = x_ref[...].astype(F32) + nn(o_ref[...], wo_ref[...])
    h = normed(x1, gain_ref[1:2]).astype(BF)
    x1_ref[...] = x1
    h_ref[...] = h
    q_ref[...] = nn(h, cq_ref[...]).astype(BF)


def outer_kernel(x1_ref, o_ref, gain_ref, co_ref, x2_ref, h_ref):
    x2 = x1_ref[...] + nn(o_ref[...], co_ref[...])
    x2_ref[...] = x2
    h_ref[...] = normed(x2, gain_ref[2:3]).astype(BF)


def add_gain(step, ref, value):
    @pl.when(step == 0)
    def _():
        ref[...] = jnp.zeros_like(ref)

    ref[0:1, :] += value


def outer_back_kernel(dh_ref, x2_ref, g_ref, gain_ref, co_ref, d_ref, dx_ref, do_ref, dgain_ref):
    dx, dgain = norm_back(x2_ref[...], gain_ref[2:3], dh_ref[...].astype(F32))
    dx = g_ref[...].astype(F32) + dx
    d = dx.astype(BF)
    dx_ref[...] = dx
    d_ref[...] = d
    do_ref[...] = nt(d, co_ref[...]).astype(BF)
    add_gain(pl.program_id(0), dgain_ref, dgain)


def middle_back_kernel(
    dq_ref, x1_ref, dx2_ref, gain_ref, cq_ref, wo_ref, dx_ref, d_ref, do_ref, dgain_ref
):
    dx, dgain = norm_back(x1_ref[...], gain_ref[1:2], nt(dq_ref[...], cq_ref[...]))
    dx = dx2_ref[...] + dx
    d = dx.astype(BF)
    dx_ref[...] = dx
    d_ref[...] = d
    do_ref[...] = nt(d, wo_ref[...]).astype(BF)
    add_gain(pl.program_id(0), dgain_ref, dgain)


def enter_back_kernel(x_ref, dx1_ref, *refs):
    grads, gain_ref, weights, (out_ref, dgain_ref) = refs[:3], refs[3], refs[4:10], refs[10:]
    dh = 0.0
    for i, grad in enumerate(grads):
        for g in range(2):
            w = weights[2 * i + g]
            at = pl.ds(g * w.shape[1], w.shape[1])
            dh = dh + nt(grad[:, at], w[...])
    dx, dgain = norm_back(x_ref[...].astype(F32), gain_ref[0:1], dh)
    out_ref[...] = (dx1_ref[...] + dx).astype(BF)
    add_gain(pl.program_id(0), dgain_ref, dgain)


def by_tokens(kernel, tokens, blocked, whole, outs, name, c=0, kept=None):
    width = blocked[0][0].shape[1]
    steps = tokens // QB
    full = tokens if kept is None else 2 * tokens

    def rows(n, first):
        return pl.BlockSpec((QB, n), lambda i, first=first: (first + i, 0))

    def fixed(shape, index):
        return pl.BlockSpec(shape, lambda i, index=index: index)

    kept = kept or ()
    inputs = len(blocked) + len(whole)

    def run(*refs):
        kernel(*refs[:inputs], *refs[inputs + len(kept) :])

    return pl.pallas_call(
        run,
        grid=(steps,),
        in_specs=[rows(a.shape[1], first) for a, first in blocked]
        + [fixed(shape, index) for _, shape, index in whole]
        + [pl.BlockSpec(memory_space=pl.ANY)] * len(kept),
        out_specs=[
            fixed((8, width), (0, 0)) if n is None else rows(n, c * steps) for n, _ in outs
        ],
        out_shape=[
            jax.ShapeDtypeStruct((8, width) if n is None else (full, n), dtype)
            for n, dtype in outs
        ],
        input_output_aliases={inputs + i: i for i in range(len(kept))},
        compiler_params=pltpu.CompilerParams(vmem_limit_bytes=25165824),
        cost_estimate=BRIEF,
        name=name,
    )(*[a for a, _ in blocked], *[a for a, _, _ in whole], *kept)


def weight_grad_kernel(*refs):
    *ins, o_ref = refs
    total = tn(ins[0][...], ins[1][...])
    for i in range(2, len(ins), 2):
        total = total + tn(ins[i][...], ins[i + 1][...])
    o_ref[...] = total.astype(BF)


def weight_grad(pairs, columns_at_once):
    rows, width = pairs[0][0].shape[1], pairs[0][1].shape[1]
    specs = []
    for x, grad in pairs:
        specs.append(pl.BlockSpec((x.shape[0], columns_at_once), lambda i: (0, i)))
        specs.append(pl.BlockSpec(grad.shape, lambda i: (0, 0)))
    return pl.pallas_call(
        weight_grad_kernel,
        grid=(rows // columns_at_once,),
        in_specs=specs,
        out_specs=pl.BlockSpec((columns_at_once, width), lambda i: (i, 0)),
        out_shape=jax.ShapeDtypeStruct((rows, width), BF),
        compiler_params=pltpu.CompilerParams(
            vmem_limit_bytes=41943040 if width > 768 or rows > 768 else 25165824
        ),
        cost_estimate=BRIEF,
        name="weight_grad",
    )(*[a for pair in pairs for a in pair])


GELU_A = 0.7978845608028654
GELU_B = 0.044715


def feed_kernel(groups, *refs):
    h_refs, g_refs, (gu_ref, down_ref) = refs[:groups], refs[groups : 2 * groups], refs[2 * groups : 2 * groups + 2]
    outs, (y_sum, dh_sum) = refs[-2 * groups - 6 : -2], refs[-2:]
    y_refs, dh_refs, (hid_ref, dgu_ref, h_ref, g_ref) = outs[:groups], outs[groups:-4], outs[-4:]
    part = h_refs[0].shape[0]
    step = down_ref.shape[0]

    @pl.when(pl.program_id(0) == 0)
    def _():
        for j in range(groups):
            h_ref[pl.ds(j * part, part), :] = h_refs[j][...]
            g_ref[pl.ds(j * part, part), :] = g_refs[j][0]
        y_sum[...] = jnp.zeros_like(y_sum)
        dh_sum[...] = jnp.zeros_like(dh_sum)

    wg, wu, wd = gu_ref[:, pl.ds(0, step)], gu_ref[:, pl.ds(step, step)], down_ref[...]
    gate, up, dhid = nn(h_ref[...], wg), nn(h_ref[...], wu), nt(g_ref[...], wd)
    square = gate * gate
    th = jnp.tanh(gate * (GELU_A + (GELU_A * GELU_B) * square))
    half = 0.5 + 0.5 * th
    act = gate * half
    slope = half + (0.5 * gate) * (1.0 - th * th) * (GELU_A + (3.0 * GELU_A * GELU_B) * square)
    hidden = (act * up).astype(BF)
    dgate = (dhid * up * slope).astype(BF)
    dup = (dhid * act).astype(BF)
    hid_ref[...] = hidden
    dgu_ref[:, pl.ds(0, step)] = dgate
    dgu_ref[:, pl.ds(step, step)] = dup
    y_sum[...] += nn(hidden, wd)
    dh_sum[...] += nt(dgate, wg) + nt(dup, wu)

    @pl.when(pl.program_id(0) == pl.num_programs(0) - 1)
    def _():
        for j in range(groups):
            at = pl.ds(j * part, part)
            y_refs[j][0] = y_sum[at, :].astype(BF)
            dh_refs[j][...] = dh_sum[at, :].astype(BF)


def feed(c, h_parts, g_parts, wgu, wd, kept):
    groups = len(h_parts)
    part, width = h_parts[0].shape
    ff = wd.shape[0]
    tokens = groups * part

    def whole(a):
        return pl.BlockSpec(a.shape, lambda i: (0,) * a.ndim)

    def halves(n, columns_at_once):
        if columns_at_once == n:
            return pl.BlockSpec((tokens, n), lambda i: (c, 0))
        return pl.BlockSpec((tokens, columns_at_once), lambda i: (c, i))

    wide = ((ff, FS), (2 * ff, 2 * FS), (width, width), (width, width))
    of_half = pl.BlockSpec((1, part, width), lambda i: (c, 0, 0))
    made = [0 + i for i in range(groups)] + [2 * groups + i for i in range(len(wide))]
    return pl.pallas_call(
        functools.partial(feed_kernel, groups),
        grid=(ff // FS,),
        in_specs=[whole(h) for h in h_parts]
        + [of_half] * groups
        + [
            pl.BlockSpec((width, 2 * FS), lambda i: (0, i)),
            pl.BlockSpec((FS, width), lambda i: (i, 0)),
        ]
        + [pl.BlockSpec(memory_space=pl.ANY)] * len(kept),
        out_specs=[of_half] * groups
        + [whole(h) for h in h_parts]
        + [halves(*n) for n in wide],
        out_shape=[jax.ShapeDtypeStruct((2, part, width), BF)] * groups
        + [jax.ShapeDtypeStruct((part, width), BF)] * groups
        + [jax.ShapeDtypeStruct((2 * tokens, n), BF) for n, _ in wide],
        scratch_shapes=[pltpu.VMEM((tokens, width), F32)] * 2,
        input_output_aliases={2 * groups + 2 + i: made[i] for i in range(len(kept))},
        compiler_params=pltpu.CompilerParams(vmem_limit_bytes=VMEM),
        cost_estimate=BRIEF,
        name="feed",
    )(*h_parts, *g_parts, wgu, wd, *kept)


def pick_kernel(modes, halves, source, mode, x_ref, *o_refs):
    per_mode = x_ref.shape[0] // modes
    for j in range(modes):
        first = jnp.bitwise_xor(mode[0], j) * per_mode

        def move(r, carry, j=j, first=first):
            row = source[first + r]
            if halves:
                for c in range(halves):
                    o_refs[j][c, r] = x_ref[row, c]
            else:
                o_refs[j][r] = x_ref[row]
            return carry

        lax.fori_loop(0, per_mode, move, 0)


def put_kernel(modes, halves, source, mode, *refs):
    o_ref = refs[-1]
    per_mode = o_ref.shape[0] // modes
    for j in range(modes):
        first = jnp.bitwise_xor(mode[0], j) * per_mode

        def move(r, carry, j=j, first=first):
            row = source[first + r]
            if halves:
                for c in range(halves):
                    o_ref[row, c] = refs[j][c, r]
            else:
                o_ref[row] = refs[j][r]
            return carry

        lax.fori_loop(0, per_mode, move, 0)


def mode_number():
    return lax.axis_index("mode").astype(jnp.int32)[None]


def by_rows(kernel, source, ins, outs, name):
    def whole(shape):
        return pl.BlockSpec(shape, lambda i, source, mode: (0,) * len(shape))

    return pl.pallas_call(
        kernel,
        grid_spec=pltpu.PrefetchScalarGridSpec(
            num_scalar_prefetch=2,
            grid=(1,),
            in_specs=[whole(a.shape) for a in ins],
            out_specs=[whole(shape) for shape in outs],
        ),
        out_shape=[jax.ShapeDtypeStruct(shape, BF) for shape in outs],
        compiler_params=pltpu.CompilerParams(vmem_limit_bytes=16777216),
        cost_estimate=pl.CostEstimate(
            flops=0, bytes_accessed=4 * sum(a.size for a in ins), transcendentals=0
        ),
        name=name,
    )(source, mode_number(), *ins)


def to_mode(spread, source):
    per_mode, modes = lax.axis_size("dp"), lax.axis_size("mode")
    piece = spread.shape[-2:]
    if spread.ndim == 4:
        outs = [(spread.shape[1], per_mode) + piece] * modes
    else:
        outs = [(per_mode,) + piece] * modes
    parts = by_rows(
        functools.partial(pick_kernel, modes, spread.shape[1] if spread.ndim == 4 else 0),
        source,
        [spread],
        outs,
        "pick",
    )
    got = [parts[0]] + [swap(parts[j], per_mode * j) for j in range(1, modes)]
    if spread.ndim == 4:
        return [part.reshape(part.shape[0], -1, part.shape[-1]) for part in got]
    return [part.reshape(-1, part.shape[-1]) for part in got]


def swap_modes(parts):
    per_mode = lax.axis_size("dp")
    lead = parts[0].shape[:-2]
    parts = [part.reshape(lead + (per_mode, -1, part.shape[-1])) for part in parts]
    return [parts[0]] + [swap(parts[j], per_mode * j) for j in range(1, len(parts))]


def put_back(parts, source):
    halves = parts[0].shape[0] if parts[0].ndim == 4 else 0
    shape = (lax.axis_size(ALL),) + ((halves,) if halves else ()) + parts[0].shape[-2:]
    return by_rows(
        functools.partial(put_kernel, len(parts), halves), source, parts, [shape], "put"
    )[0]


def dealt(value):
    count = lax.axis_size(ALL)
    return value.reshape(count, -1, value.shape[-1])


def to_all(value):
    return lax.all_to_all(value, ALL, 0, 0, tiled=True)


def swap(value, j):
    count = lax.axis_size(ALL)
    return lax.ppermute(value, ALL, [(i, i ^ j) for i in range(count)])


def device_number():
    return lax.axis_index(ALL).astype(jnp.int32)[None]


def place_kernel(me, even_ref, odd_ref, *o_refs):
    first = 0
    for o_ref in o_refs:
        at = pl.ds(first, o_ref.shape[2])
        first += o_ref.shape[2]
        for t in range(even_ref.shape[0]):
            o_ref[jnp.bitwise_xor(2 * t, me[0])] = even_ref[t, :, at]
            o_ref[jnp.bitwise_xor(2 * t + 1, me[0])] = odd_ref[t, :, at]


def place(even, odd, widths, number):
    count, rows, width = even.shape
    shapes = [(2 * count, rows, w) for w in widths]

    def whole(shape):
        return pl.BlockSpec(shape, lambda i, me: (0, 0, 0))

    return pl.pallas_call(
        place_kernel,
        grid_spec=pltpu.PrefetchScalarGridSpec(
            num_scalar_prefetch=1,
            grid=(1,),
            in_specs=[whole(even.shape)] * 2,
            out_specs=[whole(shape) for shape in shapes],
        ),
        out_shape=[jax.ShapeDtypeStruct(shape, even.dtype) for shape in shapes],
        compiler_params=pltpu.CompilerParams(vmem_limit_bytes=29360128),
        cost_estimate=BRIEF,
        name="place",
    )(number, even, odd)


def pack_kernel(counts, *refs):
    ins, outs = refs[: sum(counts)], refs[sum(counts) :]
    taken = 0
    for count, o_ref in zip(counts, outs):
        first = 0
        for part in ins[taken : taken + count]:
            o_ref[:, pl.ds(first, part.shape[1])] = part[...]
            first += part.shape[1]
        taken += count


def pack(*lists):
    cut = lambda e: e if not isinstance(e, tuple) else e[0]
    shape = lambda e: e.shape if not isinstance(e, tuple) else (e[0].shape[0], e[2])
    at = lambda e: 0 if not isinstance(e, tuple) else e[1] // e[2]
    entries = [e for group in lists for e in group]
    return pl.pallas_call(
        functools.partial(pack_kernel, [len(group) for group in lists]),
        grid=(1,),
        in_specs=[pl.BlockSpec(shape(e), lambda i, e=e: (0, at(e))) for e in entries],
        out_specs=[
            pl.BlockSpec((shape(group[0])[0], sum(shape(e)[1] for e in group)), lambda i: (0, 0))
            for group in lists
        ],
        out_shape=[
            jax.ShapeDtypeStruct((shape(group[0])[0], sum(shape(e)[1] for e in group)), BF)
            for group in lists
        ],
        name="pack",
    )(*[cut(e) for e in entries])


def gather_column(piece, late=None):
    per_mode = lax.axis_size("dp")
    got = [swap(piece, 2 * j) for j in range(1, per_mode // 2)]
    return jnp.stack([piece] + (got if late is None else tied(got, late)))


def gather_rest(column, widths, late=None):
    per_mode, modes = lax.axis_size("dp"), lax.axis_size("mode")
    got = [swap(column, per_mode * j) for j in range(1, modes)]
    if late is not None:
        got = tied(got, late)
    plane = jnp.stack([column] + got)
    plane = plane.reshape((-1,) + column.shape[1:])
    placed = place(plane, swap(plane, 1), widths, device_number())
    return [a.reshape(-1, a.shape[2]) for a in placed]


def take_kernel(parts, me, *refs):
    ins, (keep_ref, send_ref) = refs[:parts], refs[parts:]
    first = 0
    for in_ref in ins:
        at = pl.ds(first, in_ref.shape[2])
        first += in_ref.shape[2]
        for t in range(keep_ref.shape[0]):
            keep_ref[t, :, at] = in_ref[jnp.bitwise_xor(2 * t, me[0])]
            send_ref[t, :, at] = in_ref[jnp.bitwise_xor(2 * t + 1, me[0])]


def take(parts):
    count, rows = parts[0].shape[:2]
    width = sum(part.shape[2] for part in parts)
    half = jax.ShapeDtypeStruct((count // 2, rows, width), parts[0].dtype)

    def whole(shape):
        return pl.BlockSpec(shape, lambda i, me: (0, 0, 0))

    return pl.pallas_call(
        functools.partial(take_kernel, len(parts)),
        grid_spec=pltpu.PrefetchScalarGridSpec(
            num_scalar_prefetch=1,
            grid=(1,),
            in_specs=[whole(part.shape) for part in parts],
            out_specs=[whole(half.shape)] * 2,
        ),
        out_shape=[half, half],
        compiler_params=pltpu.CompilerParams(vmem_limit_bytes=50331648),
        cost_estimate=BRIEF,
        name="take",
    )(device_number(), *parts)


def add_up(parts):
    return functools.reduce(jnp.add, [part.astype(F32) for part in parts])


def scatter_pairs(parts):
    count = lax.axis_size(ALL)
    parts = [part.reshape(count, part.shape[0] // count, part.shape[1]) for part in parts]
    keep, send = take(parts)
    return add_up([keep, swap(send, 1)]).astype(BF)


def scatter_plane(pair):
    per_mode, modes = lax.axis_size("dp"), lax.axis_size("mode")
    plane = pair.reshape((modes, per_mode // 2) + pair.shape[1:])
    return add_up([plane[0]] + [swap(plane[j], per_mode * j) for j in range(1, modes)]).astype(BF)


def scatter_column(column):
    per_mode = lax.axis_size("dp")
    return add_up([column[0]] + [swap(column[j], 2 * j) for j in range(1, per_mode // 2)])


def later(lens, tokens):
    return lens - jnp.array([tokens, 0], jnp.int32)


def tied(first, second):
    return lax.optimization_barrier((first, second))[0]


def lanes_of(*vectors):
    columns_ = jnp.stack(vectors, axis=1)
    return jnp.pad(columns_, ((0, 0), (0, 128 - len(vectors))))


def on_device(
    rows,
    memory,
    cotangent,
    mode_ids,
    target_lengths,
    encoder_lengths,
    self_q,
    self_k,
    self_v,
    self_o,
    self_gain,
    cross_q,
    cross_k,
    cross_v,
    cross_o,
    cross_gain,
    ffn_gain,
    ffn_gate,
    ffn_up,
    ffn_down,
):
    devices = lax.axis_size(ALL)
    per_mode = lax.axis_size("dp")
    here = lax.axis_index(ALL)
    width = rows.shape[2]
    ff = ffn_gate.shape[2]
    index = jnp.arange(devices, dtype=jnp.int32)
    same = mode_ids[:, None] == mode_ids[None, :]
    earlier = index[None, :] < index[:, None]
    rank = jnp.sum(jnp.where(same & earlier, 1, 0), axis=1).astype(jnp.int32)
    target = mode_ids * per_mode + rank
    source = jnp.sum(
        jnp.where(target[:, None] == index[None, :], index[:, None], 0), axis=0
    ).astype(jnp.int32)
    live_len = jnp.sum(jnp.where(index == here, target_lengths, 0))
    memory_len = jnp.sum(jnp.where(index == here, encoder_lengths, 0))
    lens = jnp.stack([live_len, memory_len]).astype(jnp.int32)
    tokens, memory_row, incoming = rows[0], memory[0], cotangent[0]
    length = tokens.shape[0]
    half = length // 2
    key_count = memory_row.shape[0]
    valid = (jnp.arange(length, dtype=jnp.int32) < live_len)[:, None]
    grad_low = jnp.where(valid, incoming, jnp.zeros_like(incoming))

    group_pairs = HEADS // 4
    part = group_pairs * PAIR

    def of_group(g):
        return tuple((a, g * part, part) for a in (self_q, self_k, self_v))

    own_piece, rest_piece = pack(
        of_group(0) + of_group(1) + (lanes_of(self_gain, cross_gain, ffn_gain),),
        (self_o, cross_q, cross_k, cross_v, cross_o),
    )
    column = gather_column(own_piece)
    own_0, own_1, gain_columns = gather_rest(column, (3 * part, 3 * part, 128))
    crossing = lax.all_gather(rest_piece, ALL, axis=0, tiled=True)

    def weight(array, i, wide=width):
        return (array, (width, wide), (0, i))

    h1, qkv, gains = by_tokens(
        enter_kernel,
        length,
        [(tokens, 0)],
        [(a, a.shape, (0, 0)) for a in (own_0, own_1, gain_columns)],
        [(width, BF), (6 * part, BF), (None, F32)],
        "enter",
    )
    all_gains = (gains, gains.shape, (0, 0))
    pairs = HEADS // 2

    def of_pair(i):
        return lambda g: (g // group_pairs) * 3 * group_pairs + i * group_pairs + g % group_pairs

    grad_dealt = grad_low.reshape(2, devices, -1, width).swapaxes(0, 1)
    grad_spread = to_all(grad_dealt)

    wgu = lax.all_gather(
        jnp.concatenate(
            [a[0][:, i : i + FS] for i in range(0, ff, FS) for a in (ffn_gate, ffn_up)], axis=1
        ),
        "dp",
        axis=0,
        tiled=True,
    )
    wd = lax.all_gather(ffn_down[0], "dp", axis=0, tiled=True)

    mixed, log_self = attend_forward(
        (qkv, of_pair(0), 0),
        (qkv, of_pair(1)),
        (qkv, of_pair(2)),
        lens,
        True,
        length,
        length,
        pairs,
    )
    wo, cq, ckv, co = (
        crossing[:, i * width : j * width] for i, j in ((0, 1), (1, 2), (2, 4), (4, 5))
    )

    def forward_middle(c):
        first = c * (half // QB)
        return by_tokens(
            middle_kernel,
            half,
            [(tokens, first), (mixed, first)],
            [all_gains, weight(wo, 0), weight(cq, 0)],
            [(width, F32), (width, BF), (width, BF)],
            "middle",
        )

    def forward_cross(c, query):
        return attend_forward(
            (query, 0, 0),
            (cross_kv, 0),
            (cross_kv, pairs),
            later(lens, c * half),
            False,
            half,
            key_count,
            pairs,
        )

    def forward_outer(x1, cross_mixed):
        return by_tokens(
            outer_kernel,
            half,
            [(x1, 0), (cross_mixed, 0)],
            [all_gains, weight(co, 0)],
            [(width, F32), (width, BF)],
            "outer",
        )

    x1_a, h2_a, query_a = forward_middle(0)
    (cross_kv,) = by_tokens(
        product_kernel,
        key_count,
        [(memory_row, 0)],
        [(ckv, ckv.shape, (0, 0))],
        [(2 * width, BF)],
        "memory",
    )
    cross_a, log_cross_a = forward_cross(0, query_a)
    x2_a, h3_a = forward_outer(x1_a, cross_a)
    spread_a = to_all(dealt(tied(h3_a, grad_spread)))
    grad_parts = to_mode(grad_spread, source)
    x1_b, h2_b, query_b = forward_middle(1)
    query_b = tied(query_b, h3_a)
    cross_b, log_cross_b = forward_cross(1, query_b)
    cross_b, grad_parts = lax.optimization_barrier((cross_b, grad_parts))
    x2_b, h3_b = forward_outer(x1_b, cross_b)
    routed_a = to_mode(tied(spread_a, cross_b), source)
    spread_b = to_all(dealt(h3_b))

    modes = len(routed_a)
    routed_b = to_mode(spread_b, source)
    fed_a = feed(0, tied(routed_a, routed_b), grad_parts, wgu, wd, ())
    y_a, dh_a, kept_a = fed_a[:modes], fed_a[modes : 2 * modes], fed_a[2 * modes :]
    back_a = put_back(swap_modes(dh_a), source)
    routed_b, back_a = lax.optimization_barrier((routed_b, back_a))
    home_a = to_all(back_a).reshape(half, width)
    fed_b = feed(1, routed_b, grad_parts, wgu, wd, y_a + kept_a)
    y, dh_b = fed_b[:modes], fed_b[modes : 2 * modes]
    hidden, dgu, routed_h, routed_grad = fed_b[2 * modes :]
    back_b = swap_modes(dh_b)
    grad_wd = weight_grad([(tied(hidden, home_a), routed_grad)], 512)
    grad_wgu = weight_grad([(routed_h, dgu)], 256)
    grad_wgu, back_b = lax.optimization_barrier((tied(grad_wgu, grad_wd), back_b))
    back_b = put_back(back_b, source)
    sum_wgu = lax.psum_scatter(grad_wgu, "dp", scatter_dimension=0, tiled=True)
    sum_wd = lax.psum_scatter(grad_wd, "dp", scatter_dimension=0, tiled=True)
    home_b = to_all(back_b).reshape(half, width)
    home_a = tied(home_a, back_b)
    y_mode = swap_modes(tied(y, back_b))

    def back_outer(c, dh, x2):
        return by_tokens(
            outer_back_kernel,
            half,
            [(dh, 0), (x2, 0), (grad_low, c * (half // QB))],
            [all_gains, weight(co, 0)],
            [(width, BF), (width, F32), (width, BF), (None, F32)],
            "outer_back",
        )

    def back_middle(c, dq, x1, dx2, kept):
        return by_tokens(
            middle_back_kernel,
            half,
            [(dq, 0), (x1, 0), (dx2, 0)],
            [all_gains, weight(cq, 0), weight(wo, 0)],
            [(width, F32), (width, BF), (width, BF), (None, F32)],
            "middle_back",
            c,
            kept,
        )

    def back_cross(c, query, mixed, grad, lse, carried):
        return attend_backward(
            (query, 0, 0),
            (cross_kv, 0),
            (cross_kv, pairs),
            (mixed, 0),
            (grad, 0),
            lse,
            later(lens, c * half),
            False,
            0,
            half,
            key_count,
            pairs,
            carried,
            c == 1,
        )

    def back_self(grad):
        return attend_backward(
            (qkv, of_pair(0), 0),
            (qkv, of_pair(1)),
            (qkv, of_pair(2)),
            (mixed, 0),
            (grad, 0),
            log_self,
            lens,
            True,
            0,
            length,
            length,
            pairs,
            None,
            True,
        )

    d2_a, dx2_a, do2_a, dgain_ffn_a = back_outer(0, home_a, x2_a)
    dcq_a, dck_a, dcv_a = back_cross(0, query_a, cross_a, do2_a, log_cross_a, None)
    *halves, dgain_cross_a = back_middle(0, dcq_a, x1_a, dx2_a, ())
    home_b, y_mode = lax.optimization_barrier((tied(home_b, halves), y_mode))
    d2_b, dx2_b, do2_b, dgain_ffn_b = back_outer(1, home_b, x2_b)
    y_put, do2_b = lax.optimization_barrier((put_back(y_mode, source), do2_b))
    y_home = to_all(y_put)
    dcq_b, dck, dcv = back_cross(1, query_b, cross_b, do2_b, log_cross_b, (dck_a, dcv_a))
    dx1, d1, do1, dgain_cross_b = back_middle(1, dcq_b, x1_b, dx2_b, halves)
    cross_pair = scatter_pairs(
        [
            weight_grad([(h2_a, dcq_a), (h2_b, dcq_b)], 256),
            weight_grad([(memory_row, dck)], 256),
            weight_grad([(memory_row, dcv)], 256),
            weight_grad([(cross_a, d2_a), (cross_b, d2_b)], 256),
            weight_grad([(mixed, d1)], 256),
        ]
    )
    do1, cross_pair = lax.optimization_barrier((do1, cross_pair))
    cross_plane = scatter_plane(cross_pair)
    grads = back_self(do1)
    grads, cross_plane, y_home, sum_wgu, sum_wd = lax.optimization_barrier(
        (grads, cross_plane, y_home, sum_wgu, sum_wd)
    )
    cross_sum = scatter_column(cross_plane)
    own_pair = scatter_pairs([tn(h1, d).astype(BF) for d in grads])
    own_plane = scatter_plane(own_pair)
    grads, dck, dcv = tied((grads, dck, dcv), own_pair)
    y_home = tied(y_home, own_plane)
    grad_tokens, dgain_self = by_tokens(
        enter_back_kernel,
        length,
        [(tokens, 0), (dx1, 0)] + [(d, 0) for d in grads],
        [all_gains] + [weight(own, i, part) for i in range(3) for own in (own_0, own_1)],
        [(width, BF), (None, F32)],
        "enter_back",
    )
    gain_grads = jnp.stack(
        [dgain_self[0], dgain_cross_a[0] + dgain_cross_b[0], dgain_ffn_a[0] + dgain_ffn_b[0]]
    )
    own_plane, gain_grads = lax.optimization_barrier((own_plane, gain_grads))
    own_sum = scatter_column(own_plane)
    gain_grads = gain_grads.reshape(3, devices, -1).swapaxes(0, 1)
    gain_sums = jnp.sum(to_all(gain_grads), axis=0)
    grad_memory = (nt(dck, ckv[:, :width]) + nt(dcv, ckv[:, width:])).astype(BF)
    y = y_home.swapaxes(0, 1).reshape(length, width)
    result = jnp.where(valid, jnp.concatenate([x2_a, x2_b]) + y.astype(F32), 0.0).astype(BF)

    def turns(which):
        picked = [sum_wgu[:, i : i + FS] for i in range(which * FS, 2 * ff, 2 * FS)]
        return jnp.concatenate(picked, axis=1).astype(F32)[None]

    def block(value, i):
        return value[:, i * width : (i + 1) * width]

    return (
        result[None],
        grad_tokens[None],
        grad_memory[None],
        block(own_sum, 0),
        block(own_sum, 1),
        block(own_sum, 2),
        block(cross_sum, 4),
        gain_sums[0],
        block(cross_sum, 0),
        block(cross_sum, 1),
        block(cross_sum, 2),
        block(cross_sum, 3),
        gain_sums[1],
        gain_sums[2],
        turns(0),
        turns(1),
        sum_wd.astype(F32)[None],
    )


def solution(mesh):
    rows = P(ALL, None, None)
    weight = P(ALL, None)
    gain = P(ALL)
    feeding = P("mode", "dp", None)
    return jax.shard_map(
        on_device,
        mesh=mesh,
        in_specs=(
            (rows,) * 3
            + (P(),) * 3
            + (weight,) * 4
            + (gain,)
            + (weight,) * 4
            + (gain,) * 2
            + (feeding,) * 3
        ),
        out_specs=(
            (rows,) * 3
            + (weight,) * 4
            + (gain,)
            + (weight,) * 4
            + (gain,) * 2
            + (feeding,) * 3
        ),
        check_vma=False,
    )
```

```python
import functools

import jax
import jax.numpy as jnp
from jax import lax
from jax.experimental import pallas as pl
from jax.experimental.pallas import tpu as pltpu
from jax.sharding import PartitionSpec as P

HEADS = 12
HEAD_DIM = 64
PAIR = 2 * HEAD_DIM
EPS = 1e-06
NEG = -1e30
SCALE = HEAD_DIM ** -0.5
QB = 256
AB = 512
FS = 512
ALL = ("mode", "dp")
BF = jnp.bfloat16
F32 = jnp.float32
VMEM = 56 * 2**20
BRIEF = pl.CostEstimate(flops=10**6, bytes_accessed=10**4, transcendentals=0)


def nt(left, right):
    return lax.dot_general(left, right, (((1,), (1,)), ((), ())), preferred_element_type=F32)


def nn(left, right):
    return jnp.dot(left, right, preferred_element_type=F32)


def tn(left, right):
    return lax.dot_general(left, right, (((0,), (0,)), ((), ())), preferred_element_type=F32)


def head_lanes(value, h):
    lane = lax.broadcasted_iota(jnp.int32, value.shape, 1)
    return jnp.where((lane >= HEAD_DIM) == (h == 1), value, jnp.zeros_like(value))


def masks(causal, key_count, qb, limit):
    if causal:
        parts = []
        if qb:
            parts.append((0, qb * AB, None))
        row = lax.broadcasted_iota(jnp.int32, (AB, AB), 0)
        col = lax.broadcasted_iota(jnp.int32, (AB, AB), 1)
        parts.append((qb * AB, AB, row <= col))
        return parts
    row = lax.broadcasted_iota(jnp.int32, (key_count, AB), 0)
    return [(0, key_count, row < limit)]


def attend_fwd_kernel(causal, lens, q_ref, k_ref, v_ref, o_ref, lse_ref):
    live, limit = lens[0], lens[1]
    length, key_count = q_ref.shape[0], k_ref.shape[0]
    block = min(AB, length)
    first_head = lax.broadcasted_iota(jnp.int32, (1, PAIR), 1) < HEAD_DIM
    for start in range(0, length, block):
        at = pl.ds(start, block)

        @pl.when(start < live)
        def _(start=start, at=at):
            query = q_ref[at, :] * jnp.asarray(SCALE, BF)
            if causal:
                row = lax.broadcasted_iota(jnp.int32, (block, block), 0)
                col = lax.broadcasted_iota(jnp.int32, (block, block), 1)
                parts = [(0, start, None)] if start else []
                parts.append((start, block, col <= row))
            else:
                col = lax.broadcasted_iota(jnp.int32, (block, key_count), 1)
                parts = [(0, key_count, col < limit)]
            outs, logs = [], []
            for h in range(2):
                mine = head_lanes(query, h)
                scores = []
                for first, count, mask in parts:
                    s = nt(mine, k_ref[pl.ds(first, count), :])
                    scores.append(s if mask is None else jnp.where(mask, s, NEG))
                top = functools.reduce(
                    jnp.maximum, [jnp.max(s, axis=1, keepdims=True) for s in scores]
                )
                total, mixed = 0.0, 0.0
                for (first, count, _), s in zip(parts, scores):
                    p = jnp.exp(s - top)
                    total = total + jnp.sum(p, axis=1, keepdims=True)
                    mixed = mixed + nn(p.astype(BF), v_ref[pl.ds(first, count), :])
                outs.append(mixed / total)
                logs.append(top + jnp.log(total))
            o_ref[at, :] = jnp.where(first_head, outs[0], outs[1]).astype(BF)
            rows = jnp.swapaxes(jnp.where(first_head, logs[0], logs[1]), 0, 1)
            lse_ref[0, pl.ds(0, 1), at] = rows[0:1]
            lse_ref[0, pl.ds(1, 1), at] = rows[HEAD_DIM : HEAD_DIM + 1]

        @pl.when(start >= live)
        def _(at=at):
            o_ref[at, :] = jnp.zeros((block, PAIR), BF)
            lse_ref[0, pl.ds(0, 2), at] = jnp.zeros((2, block), F32)


def attend_bwd_kernel(causal, start, carried, lens, *refs):
    q_ref, k_ref, v_ref, o_ref, do_ref, lse_ref = refs[:6]
    more, (dq_ref, dk_ref, dv_ref, kt, dk, dv) = refs[6:-6], refs[-6:]
    live, limit = lens[0], lens[1]
    length, key_count = q_ref.shape[0], k_ref.shape[0]
    kt[...] = jnp.swapaxes(k_ref[...].astype(F32), 0, 1).astype(BF)
    if carried < key_count:
        fresh = pl.ds(carried, key_count - carried)
        dk[fresh, :] = jnp.zeros((key_count - carried, PAIR), F32)
        dv[fresh, :] = jnp.zeros((key_count - carried, PAIR), F32)
    if carried:
        dk[pl.ds(0, carried), :] = more[0][...]
        dv[pl.ds(0, carried), :] = more[1][...]
    for block in range(length // AB):
        at = pl.ds(block * AB, AB)
        qb = start // AB + block

        @pl.when(qb * AB < live)
        def _(qb=qb, at=at):
            query = q_ref[at, :] * jnp.asarray(SCALE, BF)
            grad = do_ref[at, :]
            inner = jnp.swapaxes(o_ref[at, :].astype(F32) * grad.astype(F32), 0, 1)
            parts = masks(causal, key_count, qb, limit)
            sums = [[0.0, 0.0] for _ in parts]
            outs = []
            for h in range(2):
                mine = head_lanes(query, h)
                grad_mine = head_lanes(grad, h)
                lse = lse_ref[0, pl.ds(h, 1), at]
                delta = jnp.sum(inner[h * HEAD_DIM : (h + 1) * HEAD_DIM], axis=0, keepdims=True)
                grad_query = 0.0
                for i, (first, count, mask) in enumerate(parts):
                    keys = pl.ds(first, count)
                    p = jnp.exp(nt(k_ref[keys, :], mine) - lse)
                    if mask is not None:
                        p = jnp.where(mask, p, 0.0)
                    dp = nt(v_ref[keys, :], grad_mine)
                    ds = (p * (dp - delta)).astype(BF)
                    sums[i][0] = sums[i][0] + nn(ds, mine)
                    sums[i][1] = sums[i][1] + nn(p.astype(BF), grad_mine)
                    grad_query = grad_query + nn(kt[pl.ds(h * HEAD_DIM, HEAD_DIM), keys], ds)
                outs.append(grad_query * SCALE)
            for (first, count, _), (sum_k, sum_v) in zip(parts, sums):
                dk[pl.ds(first, count), :] += sum_k
                dv[pl.ds(first, count), :] += sum_v
            dq_ref[at, :] = jnp.swapaxes(jnp.concatenate(outs, axis=0), 0, 1).astype(BF)

        @pl.when(qb * AB >= live)
        def _(at=at):
            dq_ref[at, :] = jnp.zeros((AB, PAIR), BF)

    dk_ref[...] = dk[...].astype(dk_ref.dtype)
    dv_ref[...] = dv[...].astype(dv_ref.dtype)


def columns(rows, first, row_block=0):
    at = first if callable(first) else lambda g: first + g
    return pl.BlockSpec((rows, PAIR), lambda g, lens: (row_block, at(g)))


def attend_forward(query, keys, values, lens, causal, length, key_count, pairs):
    (qa, q0, rows), (ka, k0), (va, v0) = query, keys, values
    return pl.pallas_call(
        functools.partial(attend_fwd_kernel, causal),
        grid_spec=pltpu.PrefetchScalarGridSpec(
            num_scalar_prefetch=1,
            grid=(pairs,),
            in_specs=[
                columns(length, q0, rows),
                columns(key_count, k0),
                columns(key_count, v0),
            ],
            out_specs=[
                columns(length, 0),
                pl.BlockSpec((1, 2, length), lambda g, lens: (g, 0, 0)),
            ],
        ),
        out_shape=[
            jax.ShapeDtypeStruct((length, pairs * PAIR), BF),
            jax.ShapeDtypeStruct((pairs, 2, length), F32),
        ],
        compiler_params=pltpu.CompilerParams(vmem_limit_bytes=41943040),
        cost_estimate=BRIEF,
        name="attend_causal" if causal else "attend_memory",
    )(lens, qa, ka, va)


def attend_backward(
    query, keys, values, mixed, grad, lse, lens, causal, start, length, key_count, pairs, carried, last
):
    (qa, q0, rows), (ka, k0), (va, v0) = query, keys, values
    had = carried[0].shape[0] if carried else 0
    kept = BF if last else F32
    return pl.pallas_call(
        functools.partial(attend_bwd_kernel, causal, start, had),
        grid_spec=pltpu.PrefetchScalarGridSpec(
            num_scalar_prefetch=1,
            grid=(pairs,),
            in_specs=[
                columns(length, q0, rows),
                columns(key_count, k0),
                columns(key_count, v0),
                columns(length, mixed[1]),
                columns(length, grad[1]),
                pl.BlockSpec((1, 2, length), lambda g, lens: (mixed[1] + g, 0, 0)),
            ]
            + [columns(had, 0)] * (2 if carried else 0),
            out_specs=[columns(length, 0), columns(key_count, 0), columns(key_count, 0)],
            scratch_shapes=[
                pltpu.VMEM((PAIR, key_count), BF),
                pltpu.VMEM((key_count, PAIR), F32),
                pltpu.VMEM((key_count, PAIR), F32),
            ],
        ),
        out_shape=[
            jax.ShapeDtypeStruct((length, pairs * PAIR), BF),
            jax.ShapeDtypeStruct((key_count, pairs * PAIR), kept),
            jax.ShapeDtypeStruct((key_count, pairs * PAIR), kept),
        ],
        compiler_params=pltpu.CompilerParams(vmem_limit_bytes=50331648),
        cost_estimate=BRIEF,
        name="attend_causal_back" if causal else "attend_memory_back",
    )(lens, qa, ka, va, mixed[0], grad[0], lse, *(carried or ()))


def normed(value, gain):
    scale = lax.rsqrt(jnp.mean(value * value, axis=-1, keepdims=True) + EPS)
    return value * scale * gain


def norm_back(value, gain, grad):
    scale = lax.rsqrt(jnp.mean(value * value, axis=-1, keepdims=True) + EPS)
    unit = value * scale
    scaled = grad * gain
    inner = jnp.mean(scaled * unit, axis=-1, keepdims=True)
    return scale * (scaled - unit * inner), jnp.sum(grad * unit, axis=0, keepdims=True)


def enter_kernel(x_ref, w0_ref, w1_ref, columns_ref, h_ref, qkv_ref, gain_ref):
    rows = jnp.swapaxes(columns_ref[...].astype(F32), 0, 1)
    gain_ref[...] = rows[:8]
    h = normed(x_ref[...].astype(F32), rows[0:1]).astype(BF)
    h_ref[...] = h
    wide = w0_ref.shape[1]
    qkv_ref[:, pl.ds(0, wide)] = nn(h, w0_ref[...]).astype(BF)
    qkv_ref[:, pl.ds(wide, wide)] = nn(h, w1_ref[...]).astype(BF)


def product_kernel(x_ref, w_ref, o_ref):
    o_ref[...] = nn(x_ref[...], w_ref[...]).astype(BF)


def middle_kernel(x_ref, o_ref, gain_ref, wo_ref, cq_ref, x1_ref, h_ref, q_ref):
    x1 = x_ref[...].astype(F32) + nn(o_ref[...], wo_ref[...])
    h = normed(x1, gain_ref[1:2]).astype(BF)
    x1_ref[...] = x1
    h_ref[...] = h
    q_ref[...] = nn(h, cq_ref[...]).astype(BF)


def outer_kernel(x1_ref, o_ref, gain_ref, co_ref, x2_ref, h_ref):
    x2 = x1_ref[...] + nn(o_ref[...], co_ref[...])
    x2_ref[...] = x2
    h_ref[...] = normed(x2, gain_ref[2:3]).astype(BF)


def add_gain(step, ref, value):
    @pl.when(step == 0)
    def _():
        ref[...] = jnp.zeros_like(ref)

    ref[0:1, :] += value


def outer_back_kernel(dh_ref, x2_ref, g_ref, gain_ref, co_ref, d_ref, dx_ref, do_ref, dgain_ref):
    dx, dgain = norm_back(x2_ref[...], gain_ref[2:3], dh_ref[...].astype(F32))
    dx = g_ref[...].astype(F32) + dx
    d = dx.astype(BF)
    dx_ref[...] = dx
    d_ref[...] = d
    do_ref[...] = nt(d, co_ref[...]).astype(BF)
    add_gain(pl.program_id(0), dgain_ref, dgain)


def middle_back_kernel(
    dq_ref, x1_ref, dx2_ref, gain_ref, cq_ref, wo_ref, dx_ref, d_ref, do_ref, dgain_ref
):
    dx, dgain = norm_back(x1_ref[...], gain_ref[1:2], nt(dq_ref[...], cq_ref[...]))
    dx = dx2_ref[...] + dx
    d = dx.astype(BF)
    dx_ref[...] = dx
    d_ref[...] = d
    do_ref[...] = nt(d, wo_ref[...]).astype(BF)
    add_gain(pl.program_id(0), dgain_ref, dgain)


def enter_back_kernel(x_ref, dx1_ref, *refs):
    grads, gain_ref, weights, (out_ref, dgain_ref) = refs[:3], refs[3], refs[4:10], refs[10:]
    dh = 0.0
    for i, grad in enumerate(grads):
        for g in range(2):
            w = weights[2 * i + g]
            at = pl.ds(g * w.shape[1], w.shape[1])
            dh = dh + nt(grad[:, at], w[...])
    dx, dgain = norm_back(x_ref[...].astype(F32), gain_ref[0:1], dh)
    out_ref[...] = (dx1_ref[...] + dx).astype(BF)
    add_gain(pl.program_id(0), dgain_ref, dgain)


def by_tokens(kernel, tokens, blocked, whole, outs, name, c=0, kept=None):
    width = blocked[0][0].shape[1]
    steps = tokens // QB
    full = tokens if kept is None else 2 * tokens

    def rows(n, first):
        return pl.BlockSpec((QB, n), lambda i, first=first: (first + i, 0))

    def fixed(shape, index):
        return pl.BlockSpec(shape, lambda i, index=index: index)

    kept = kept or ()
    inputs = len(blocked) + len(whole)

    def run(*refs):
        kernel(*refs[:inputs], *refs[inputs + len(kept) :])

    return pl.pallas_call(
        run,
        grid=(steps,),
        in_specs=[rows(a.shape[1], first) for a, first in blocked]
        + [fixed(shape, index) for _, shape, index in whole]
        + [pl.BlockSpec(memory_space=pl.ANY)] * len(kept),
        out_specs=[
            fixed((8, width), (0, 0)) if n is None else rows(n, c * steps) for n, _ in outs
        ],
        out_shape=[
            jax.ShapeDtypeStruct((8, width) if n is None else (full, n), dtype)
            for n, dtype in outs
        ],
        input_output_aliases={inputs + i: i for i in range(len(kept))},
        compiler_params=pltpu.CompilerParams(vmem_limit_bytes=25165824),
        cost_estimate=BRIEF,
        name=name,
    )(*[a for a, _ in blocked], *[a for a, _, _ in whole], *kept)


def weight_grad_kernel(*refs):
    *ins, o_ref = refs
    total = tn(ins[0][...], ins[1][...])
    for i in range(2, len(ins), 2):
        total = total + tn(ins[i][...], ins[i + 1][...])
    o_ref[...] = total.astype(BF)


def weight_grad(pairs, columns_at_once):
    rows, width = pairs[0][0].shape[1], pairs[0][1].shape[1]
    specs = []
    for x, grad in pairs:
        specs.append(pl.BlockSpec((x.shape[0], columns_at_once), lambda i: (0, i)))
        specs.append(pl.BlockSpec(grad.shape, lambda i: (0, 0)))
    return pl.pallas_call(
        weight_grad_kernel,
        grid=(rows // columns_at_once,),
        in_specs=specs,
        out_specs=pl.BlockSpec((columns_at_once, width), lambda i: (i, 0)),
        out_shape=jax.ShapeDtypeStruct((rows, width), BF),
        compiler_params=pltpu.CompilerParams(
            vmem_limit_bytes=41943040 if width > 768 or rows > 768 else 25165824
        ),
        cost_estimate=BRIEF,
        name="weight_grad",
    )(*[a for pair in pairs for a in pair])


GELU_A = 0.7978845608028654
GELU_B = 0.044715


def feed_kernel(groups, *refs):
    h_refs, g_refs, (gu_ref, down_ref) = refs[:groups], refs[groups : 2 * groups], refs[2 * groups : 2 * groups + 2]
    outs, (y_sum, dh_sum) = refs[-2 * groups - 6 : -2], refs[-2:]
    y_refs, dh_refs, (hid_ref, dgu_ref, h_ref, g_ref) = outs[:groups], outs[groups:-4], outs[-4:]
    part = h_refs[0].shape[0]
    step = down_ref.shape[0]

    @pl.when(pl.program_id(0) == 0)
    def _():
        for j in range(groups):
            h_ref[pl.ds(j * part, part), :] = h_refs[j][...]
            g_ref[pl.ds(j * part, part), :] = g_refs[j][0]
        y_sum[...] = jnp.zeros_like(y_sum)
        dh_sum[...] = jnp.zeros_like(dh_sum)

    wg, wu, wd = gu_ref[:, pl.ds(0, step)], gu_ref[:, pl.ds(step, step)], down_ref[...]
    gate, up, dhid = nn(h_ref[...], wg), nn(h_ref[...], wu), nt(g_ref[...], wd)
    square = gate * gate
    th = jnp.tanh(gate * (GELU_A + (GELU_A * GELU_B) * square))
    half = 0.5 + 0.5 * th
    act = gate * half
    slope = half + (0.5 * gate) * (1.0 - th * th) * (GELU_A + (3.0 * GELU_A * GELU_B) * square)
    hidden = (act * up).astype(BF)
    dgate = (dhid * up * slope).astype(BF)
    dup = (dhid * act).astype(BF)
    hid_ref[...] = hidden
    dgu_ref[:, pl.ds(0, step)] = dgate
    dgu_ref[:, pl.ds(step, step)] = dup
    y_sum[...] += nn(hidden, wd)
    dh_sum[...] += nt(dgate, wg) + nt(dup, wu)

    @pl.when(pl.program_id(0) == pl.num_programs(0) - 1)
    def _():
        for j in range(groups):
            at = pl.ds(j * part, part)
            y_refs[j][0] = y_sum[at, :].astype(BF)
            dh_refs[j][...] = dh_sum[at, :].astype(BF)


def feed(c, h_parts, g_parts, wgu, wd, kept):
    groups = len(h_parts)
    part, width = h_parts[0].shape
    ff = wd.shape[0]
    tokens = groups * part

    def whole(a):
        return pl.BlockSpec(a.shape, lambda i: (0,) * a.ndim)

    def halves(n, columns_at_once):
        if columns_at_once == n:
            return pl.BlockSpec((tokens, n), lambda i: (c, 0))
        return pl.BlockSpec((tokens, columns_at_once), lambda i: (c, i))

    wide = ((ff, FS), (2 * ff, 2 * FS), (width, width), (width, width))
    of_half = pl.BlockSpec((1, part, width), lambda i: (c, 0, 0))
    made = [0 + i for i in range(groups)] + [2 * groups + i for i in range(len(wide))]
    return pl.pallas_call(
        functools.partial(feed_kernel, groups),
        grid=(ff // FS,),
        in_specs=[whole(h) for h in h_parts]
        + [of_half] * groups
        + [
            pl.BlockSpec((width, 2 * FS), lambda i: (0, i)),
            pl.BlockSpec((FS, width), lambda i: (i, 0)),
        ]
        + [pl.BlockSpec(memory_space=pl.ANY)] * len(kept),
        out_specs=[of_half] * groups
        + [whole(h) for h in h_parts]
        + [halves(*n) for n in wide],
        out_shape=[jax.ShapeDtypeStruct((2, part, width), BF)] * groups
        + [jax.ShapeDtypeStruct((part, width), BF)] * groups
        + [jax.ShapeDtypeStruct((2 * tokens, n), BF) for n, _ in wide],
        scratch_shapes=[pltpu.VMEM((tokens, width), F32)] * 2,
        input_output_aliases={2 * groups + 2 + i: made[i] for i in range(len(kept))},
        compiler_params=pltpu.CompilerParams(vmem_limit_bytes=VMEM),
        cost_estimate=BRIEF,
        name="feed",
    )(*h_parts, *g_parts, wgu, wd, *kept)


def pick_kernel(modes, halves, source, mode, x_ref, *o_refs):
    per_mode = x_ref.shape[0] // modes
    for j in range(modes):
        first = jnp.bitwise_xor(mode[0], j) * per_mode

        def move(r, carry, j=j, first=first):
            row = source[first + r]
            if halves:
                for c in range(halves):
                    o_refs[j][c, r] = x_ref[row, c]
            else:
                o_refs[j][r] = x_ref[row]
            return carry

        lax.fori_loop(0, per_mode, move, 0)


def put_kernel(modes, halves, source, mode, *refs):
    o_ref = refs[-1]
    per_mode = o_ref.shape[0] // modes
    for j in range(modes):
        first = jnp.bitwise_xor(mode[0], j) * per_mode

        def move(r, carry, j=j, first=first):
            row = source[first + r]
            if halves:
                for c in range(halves):
                    o_ref[row, c] = refs[j][c, r]
            else:
                o_ref[row] = refs[j][r]
            return carry

        lax.fori_loop(0, per_mode, move, 0)


def mode_number():
    return lax.axis_index("mode").astype(jnp.int32)[None]


def by_rows(kernel, source, ins, outs, name):
    def whole(shape):
        return pl.BlockSpec(shape, lambda i, source, mode: (0,) * len(shape))

    return pl.pallas_call(
        kernel,
        grid_spec=pltpu.PrefetchScalarGridSpec(
            num_scalar_prefetch=2,
            grid=(1,),
            in_specs=[whole(a.shape) for a in ins],
            out_specs=[whole(shape) for shape in outs],
        ),
        out_shape=[jax.ShapeDtypeStruct(shape, BF) for shape in outs],
        compiler_params=pltpu.CompilerParams(vmem_limit_bytes=16777216),
        cost_estimate=pl.CostEstimate(
            flops=0, bytes_accessed=4 * sum(a.size for a in ins), transcendentals=0
        ),
        name=name,
    )(source, mode_number(), *ins)


def to_mode(spread, source):
    per_mode, modes = lax.axis_size("dp"), lax.axis_size("mode")
    piece = spread.shape[-2:]
    if spread.ndim == 4:
        outs = [(spread.shape[1], per_mode) + piece] * modes
    else:
        outs = [(per_mode,) + piece] * modes
    parts = by_rows(
        functools.partial(pick_kernel, modes, spread.shape[1] if spread.ndim == 4 else 0),
        source,
        [spread],
        outs,
        "pick",
    )
    got = [parts[0]] + [swap(parts[j], per_mode * j) for j in range(1, modes)]
    if spread.ndim == 4:
        return [part.reshape(part.shape[0], -1, part.shape[-1]) for part in got]
    return [part.reshape(-1, part.shape[-1]) for part in got]


def swap_modes(parts):
    per_mode = lax.axis_size("dp")
    lead = parts[0].shape[:-2]
    parts = [part.reshape(lead + (per_mode, -1, part.shape[-1])) for part in parts]
    return [parts[0]] + [swap(parts[j], per_mode * j) for j in range(1, len(parts))]


def put_back(parts, source):
    halves = parts[0].shape[0] if parts[0].ndim == 4 else 0
    shape = (lax.axis_size(ALL),) + ((halves,) if halves else ()) + parts[0].shape[-2:]
    return by_rows(
        functools.partial(put_kernel, len(parts), halves), source, parts, [shape], "put"
    )[0]


def dealt(value):
    count = lax.axis_size(ALL)
    return value.reshape(count, -1, value.shape[-1])


def to_all(value):
    return lax.all_to_all(value, ALL, 0, 0, tiled=True)


def swap(value, j):
    count = lax.axis_size(ALL)
    return lax.ppermute(value, ALL, [(i, i ^ j) for i in range(count)])


def device_number():
    return lax.axis_index(ALL).astype(jnp.int32)[None]


def place_kernel(me, even_ref, odd_ref, *o_refs):
    first = 0
    for o_ref in o_refs:
        at = pl.ds(first, o_ref.shape[2])
        first += o_ref.shape[2]
        for t in range(even_ref.shape[0]):
            o_ref[jnp.bitwise_xor(2 * t, me[0])] = even_ref[t, :, at]
            o_ref[jnp.bitwise_xor(2 * t + 1, me[0])] = odd_ref[t, :, at]


def place(even, odd, widths, number):
    count, rows, width = even.shape
    shapes = [(2 * count, rows, w) for w in widths]

    def whole(shape):
        return pl.BlockSpec(shape, lambda i, me: (0, 0, 0))

    return pl.pallas_call(
        place_kernel,
        grid_spec=pltpu.PrefetchScalarGridSpec(
            num_scalar_prefetch=1,
            grid=(1,),
            in_specs=[whole(even.shape)] * 2,
            out_specs=[whole(shape) for shape in shapes],
        ),
        out_shape=[jax.ShapeDtypeStruct(shape, even.dtype) for shape in shapes],
        compiler_params=pltpu.CompilerParams(vmem_limit_bytes=29360128),
        cost_estimate=BRIEF,
        name="place",
    )(number, even, odd)


def pack_kernel(counts, *refs):
    ins, outs = refs[: sum(counts)], refs[sum(counts) :]
    taken = 0
    for count, o_ref in zip(counts, outs):
        first = 0
        for part in ins[taken : taken + count]:
            o_ref[:, pl.ds(first, part.shape[1])] = part[...]
            first += part.shape[1]
        taken += count


def pack(*lists):
    cut = lambda e: e if not isinstance(e, tuple) else e[0]
    shape = lambda e: e.shape if not isinstance(e, tuple) else (e[0].shape[0], e[2])
    at = lambda e: 0 if not isinstance(e, tuple) else e[1] // e[2]
    entries = [e for group in lists for e in group]
    return pl.pallas_call(
        functools.partial(pack_kernel, [len(group) for group in lists]),
        grid=(1,),
        in_specs=[pl.BlockSpec(shape(e), lambda i, e=e: (0, at(e))) for e in entries],
        out_specs=[
            pl.BlockSpec((shape(group[0])[0], sum(shape(e)[1] for e in group)), lambda i: (0, 0))
            for group in lists
        ],
        out_shape=[
            jax.ShapeDtypeStruct((shape(group[0])[0], sum(shape(e)[1] for e in group)), BF)
            for group in lists
        ],
        name="pack",
    )(*[cut(e) for e in entries])


def gather_column(piece, late=None):
    per_mode = lax.axis_size("dp")
    got = [swap(piece, 2 * j) for j in range(1, per_mode // 2)]
    return jnp.stack([piece] + (got if late is None else tied(got, late)))


def gather_rest(column, widths, late=None):
    per_mode, modes = lax.axis_size("dp"), lax.axis_size("mode")
    got = [swap(column, per_mode * j) for j in range(1, modes)]
    if late is not None:
        got = tied(got, late)
    plane = jnp.stack([column] + got)
    plane = plane.reshape((-1,) + column.shape[1:])
    placed = place(plane, swap(plane, 1), widths, device_number())
    return [a.reshape(-1, a.shape[2]) for a in placed]


def take_kernel(parts, me, *refs):
    ins, (keep_ref, send_ref) = refs[:parts], refs[parts:]
    first = 0
    for in_ref in ins:
        at = pl.ds(first, in_ref.shape[2])
        first += in_ref.shape[2]
        for t in range(keep_ref.shape[0]):
            keep_ref[t, :, at] = in_ref[jnp.bitwise_xor(2 * t, me[0])]
            send_ref[t, :, at] = in_ref[jnp.bitwise_xor(2 * t + 1, me[0])]


def take(parts):
    count, rows = parts[0].shape[:2]
    width = sum(part.shape[2] for part in parts)
    half = jax.ShapeDtypeStruct((count // 2, rows, width), parts[0].dtype)

    def whole(shape):
        return pl.BlockSpec(shape, lambda i, me: (0, 0, 0))

    return pl.pallas_call(
        functools.partial(take_kernel, len(parts)),
        grid_spec=pltpu.PrefetchScalarGridSpec(
            num_scalar_prefetch=1,
            grid=(1,),
            in_specs=[whole(part.shape) for part in parts],
            out_specs=[whole(half.shape)] * 2,
        ),
        out_shape=[half, half],
        compiler_params=pltpu.CompilerParams(vmem_limit_bytes=50331648),
        cost_estimate=BRIEF,
        name="take",
    )(device_number(), *parts)


def add_up(parts):
    return functools.reduce(jnp.add, [part.astype(F32) for part in parts])


def scatter_pairs(parts):
    count = lax.axis_size(ALL)
    parts = [part.reshape(count, part.shape[0] // count, part.shape[1]) for part in parts]
    keep, send = take(parts)
    return add_up([keep, swap(send, 1)]).astype(BF)


def scatter_plane(pair):
    per_mode, modes = lax.axis_size("dp"), lax.axis_size("mode")
    plane = pair.reshape((modes, per_mode // 2) + pair.shape[1:])
    return add_up([plane[0]] + [swap(plane[j], per_mode * j) for j in range(1, modes)]).astype(BF)


def scatter_column(column):
    per_mode = lax.axis_size("dp")
    return add_up([column[0]] + [swap(column[j], 2 * j) for j in range(1, per_mode // 2)])


def later(lens, tokens):
    return lens - jnp.array([tokens, 0], jnp.int32)


def tied(first, second):
    return lax.optimization_barrier((first, second))[0]


def lanes_of(*vectors):
    columns_ = jnp.stack(vectors, axis=1)
    return jnp.pad(columns_, ((0, 0), (0, 128 - len(vectors))))


def on_device(
    rows,
    memory,
    cotangent,
    mode_ids,
    target_lengths,
    encoder_lengths,
    self_q,
    self_k,
    self_v,
    self_o,
    self_gain,
    cross_q,
    cross_k,
    cross_v,
    cross_o,
    cross_gain,
    ffn_gain,
    ffn_gate,
    ffn_up,
    ffn_down,
):
    devices = lax.axis_size(ALL)
    per_mode = lax.axis_size("dp")
    here = lax.axis_index(ALL)
    width = rows.shape[2]
    ff = ffn_gate.shape[2]
    index = jnp.arange(devices, dtype=jnp.int32)
    same = mode_ids[:, None] == mode_ids[None, :]
    earlier = index[None, :] < index[:, None]
    rank = jnp.sum(jnp.where(same & earlier, 1, 0), axis=1).astype(jnp.int32)
    target = mode_ids * per_mode + rank
    source = jnp.sum(
        jnp.where(target[:, None] == index[None, :], index[:, None], 0), axis=0
    ).astype(jnp.int32)
    live_len = jnp.sum(jnp.where(index == here, target_lengths, 0))
    memory_len = jnp.sum(jnp.where(index == here, encoder_lengths, 0))
    lens = jnp.stack([live_len, memory_len]).astype(jnp.int32)
    tokens, memory_row, incoming = rows[0], memory[0], cotangent[0]
    length = tokens.shape[0]
    half = length // 2
    key_count = memory_row.shape[0]
    valid = (jnp.arange(length, dtype=jnp.int32) < live_len)[:, None]
    grad_low = jnp.where(valid, incoming, jnp.zeros_like(incoming))

    group_pairs = HEADS // 4
    part = group_pairs * PAIR

    def of_group(g):
        return tuple((a, g * part, part) for a in (self_q, self_k, self_v))

    own_piece, rest_piece = pack(
        of_group(0) + of_group(1) + (lanes_of(self_gain, cross_gain, ffn_gain),),
        (self_o, cross_q, cross_k, cross_v, cross_o),
    )
    column = gather_column(own_piece)
    own_0, own_1, gain_columns = gather_rest(column, (3 * part, 3 * part, 128))
    crossing = lax.all_gather(rest_piece, ALL, axis=0, tiled=True)

    def weight(array, i, wide=width):
        return (array, (width, wide), (0, i))

    h1, qkv, gains = by_tokens(
        enter_kernel,
        length,
        [(tokens, 0)],
        [(a, a.shape, (0, 0)) for a in (own_0, own_1, gain_columns)],
        [(width, BF), (6 * part, BF), (None, F32)],
        "enter",
    )
    all_gains = (gains, gains.shape, (0, 0))
    pairs = HEADS // 2

    def of_pair(i):
        return lambda g: (g // group_pairs) * 3 * group_pairs + i * group_pairs + g % group_pairs

    grad_dealt = grad_low.reshape(2, devices, -1, width).swapaxes(0, 1)
    grad_spread = to_all(grad_dealt)

    wgu = lax.all_gather(
        jnp.concatenate(
            [a[0][:, i : i + FS] for i in range(0, ff, FS) for a in (ffn_gate, ffn_up)], axis=1
        ),
        "dp",
        axis=0,
        tiled=True,
    )
    wd = lax.all_gather(ffn_down[0], "dp", axis=0, tiled=True)

    mixed, log_self = attend_forward(
        (qkv, of_pair(0), 0),
        (qkv, of_pair(1)),
        (qkv, of_pair(2)),
        lens,
        True,
        length,
        length,
        pairs,
    )
    wo, cq, ckv, co = (
        crossing[:, i * width : j * width] for i, j in ((0, 1), (1, 2), (2, 4), (4, 5))
    )

    def forward_middle(c):
        first = c * (half // QB)
        return by_tokens(
            middle_kernel,
            half,
            [(tokens, first), (mixed, first)],
            [all_gains, weight(wo, 0), weight(cq, 0)],
            [(width, F32), (width, BF), (width, BF)],
            "middle",
        )

    def forward_cross(c, query):
        return attend_forward(
            (query, 0, 0),
            (cross_kv, 0),
            (cross_kv, pairs),
            later(lens, c * half),
            False,
            half,
            key_count,
            pairs,
        )

    def forward_outer(x1, cross_mixed):
        return by_tokens(
            outer_kernel,
            half,
            [(x1, 0), (cross_mixed, 0)],
            [all_gains, weight(co, 0)],
            [(width, F32), (width, BF)],
            "outer",
        )

    x1_a, h2_a, query_a = forward_middle(0)
    (cross_kv,) = by_tokens(
        product_kernel,
        key_count,
        [(memory_row, 0)],
        [(ckv, ckv.shape, (0, 0))],
        [(2 * width, BF)],
        "memory",
    )
    cross_a, log_cross_a = forward_cross(0, query_a)
    x2_a, h3_a = forward_outer(x1_a, cross_a)
    spread_a = to_all(dealt(tied(h3_a, grad_spread)))
    grad_parts = to_mode(grad_spread, source)
    x1_b, h2_b, query_b = forward_middle(1)
    query_b = tied(query_b, h3_a)
    cross_b, log_cross_b = forward_cross(1, query_b)
    cross_b, grad_parts = lax.optimization_barrier((cross_b, grad_parts))
    x2_b, h3_b = forward_outer(x1_b, cross_b)
    routed_a = to_mode(tied(spread_a, cross_b), source)
    spread_b = to_all(dealt(h3_b))

    modes = len(routed_a)
    routed_b = to_mode(spread_b, source)
    fed_a = feed(0, tied(routed_a, routed_b), grad_parts, wgu, wd, ())
    y_a, dh_a, kept_a = fed_a[:modes], fed_a[modes : 2 * modes], fed_a[2 * modes :]
    back_a = put_back(swap_modes(dh_a), source)
    routed_b, back_a = lax.optimization_barrier((routed_b, back_a))
    home_a = to_all(back_a).reshape(half, width)
    fed_b = feed(1, routed_b, grad_parts, wgu, wd, y_a + kept_a)
    y, dh_b = fed_b[:modes], fed_b[modes : 2 * modes]
    hidden, dgu, routed_h, routed_grad = fed_b[2 * modes :]
    back_b = swap_modes(dh_b)
    grad_wd = weight_grad([(tied(hidden, home_a), routed_grad)], 512)
    grad_wgu = weight_grad([(routed_h, dgu)], 256)
    grad_wgu, back_b = lax.optimization_barrier((tied(grad_wgu, grad_wd), back_b))
    back_b = put_back(back_b, source)
    sum_wgu = lax.psum_scatter(grad_wgu, "dp", scatter_dimension=0, tiled=True)
    sum_wd = lax.psum_scatter(grad_wd, "dp", scatter_dimension=0, tiled=True)
    home_b = to_all(back_b).reshape(half, width)
    home_a = tied(home_a, back_b)
    y_mode = swap_modes(tied(y, back_b))

    def back_outer(c, dh, x2):
        return by_tokens(
            outer_back_kernel,
            half,
            [(dh, 0), (x2, 0), (grad_low, c * (half // QB))],
            [all_gains, weight(co, 0)],
            [(width, BF), (width, F32), (width, BF), (None, F32)],
            "outer_back",
        )

    def back_middle(c, dq, x1, dx2, kept):
        return by_tokens(
            middle_back_kernel,
            half,
            [(dq, 0), (x1, 0), (dx2, 0)],
            [all_gains, weight(cq, 0), weight(wo, 0)],
            [(width, F32), (width, BF), (width, BF), (None, F32)],
            "middle_back",
            c,
            kept,
        )

    def back_cross(c, query, mixed, grad, lse, carried):
        return attend_backward(
            (query, 0, 0),
            (cross_kv, 0),
            (cross_kv, pairs),
            (mixed, 0),
            (grad, 0),
            lse,
            later(lens, c * half),
            False,
            0,
            half,
            key_count,
            pairs,
            carried,
            c == 1,
        )

    def back_self(grad):
        return attend_backward(
            (qkv, of_pair(0), 0),
            (qkv, of_pair(1)),
            (qkv, of_pair(2)),
            (mixed, 0),
            (grad, 0),
            log_self,
            lens,
            True,
            0,
            length,
            length,
            pairs,
            None,
            True,
        )

    d2_a, dx2_a, do2_a, dgain_ffn_a = back_outer(0, home_a, x2_a)
    dcq_a, dck_a, dcv_a = back_cross(0, query_a, cross_a, do2_a, log_cross_a, None)
    *halves, dgain_cross_a = back_middle(0, dcq_a, x1_a, dx2_a, ())
    home_b, y_mode = lax.optimization_barrier((tied(home_b, halves), y_mode))
    d2_b, dx2_b, do2_b, dgain_ffn_b = back_outer(1, home_b, x2_b)
    y_put, do2_b = lax.optimization_barrier((put_back(y_mode, source), do2_b))
    y_home = to_all(y_put)
    dcq_b, dck, dcv = back_cross(1, query_b, cross_b, do2_b, log_cross_b, (dck_a, dcv_a))
    dx1, d1, do1, dgain_cross_b = back_middle(1, dcq_b, x1_b, dx2_b, halves)
    cross_pair = scatter_pairs(
        [
            weight_grad([(h2_a, dcq_a), (h2_b, dcq_b)], 256),
            weight_grad([(memory_row, dck)], 256),
            weight_grad([(memory_row, dcv)], 256),
            weight_grad([(cross_a, d2_a), (cross_b, d2_b)], 256),
            weight_grad([(mixed, d1)], 256),
        ]
    )
    do1, cross_pair = lax.optimization_barrier((do1, cross_pair))
    cross_plane = scatter_plane(cross_pair)
    grads = back_self(do1)
    grads, y_home, sum_wgu, sum_wd = lax.optimization_barrier((grads, y_home, sum_wgu, sum_wd))
    own_pair = scatter_pairs([tn(h1, d).astype(BF) for d in grads])
    own_pair, cross_plane = lax.optimization_barrier((own_pair, cross_plane))
    own_plane = scatter_plane(own_pair)
    cross_sum = scatter_column(cross_plane)
    grads, dck, dcv = tied((grads, dck, dcv), own_pair)
    y_home = tied(y_home, own_plane)
    grad_tokens, dgain_self = by_tokens(
        enter_back_kernel,
        length,
        [(tokens, 0), (dx1, 0)] + [(d, 0) for d in grads],
        [all_gains] + [weight(own, i, part) for i in range(3) for own in (own_0, own_1)],
        [(width, BF), (None, F32)],
        "enter_back",
    )
    gain_grads = jnp.stack(
        [dgain_self[0], dgain_cross_a[0] + dgain_cross_b[0], dgain_ffn_a[0] + dgain_ffn_b[0]]
    )
    own_plane, gain_grads = lax.optimization_barrier((own_plane, gain_grads))
    own_sum = scatter_column(own_plane)
    gain_grads = gain_grads.reshape(3, devices, -1).swapaxes(0, 1)
    gain_sums = jnp.sum(to_all(gain_grads), axis=0)
    grad_memory = (nt(dck, ckv[:, :width]) + nt(dcv, ckv[:, width:])).astype(BF)
    y = y_home.swapaxes(0, 1).reshape(length, width)
    result = jnp.where(valid, jnp.concatenate([x2_a, x2_b]) + y.astype(F32), 0.0).astype(BF)

    def turns(which):
        picked = [sum_wgu[:, i : i + FS] for i in range(which * FS, 2 * ff, 2 * FS)]
        return jnp.concatenate(picked, axis=1).astype(F32)[None]

    def block(value, i):
        return value[:, i * width : (i + 1) * width]

    return (
        result[None],
        grad_tokens[None],
        grad_memory[None],
        block(own_sum, 0),
        block(own_sum, 1),
        block(own_sum, 2),
        block(cross_sum, 4),
        gain_sums[0],
        block(cross_sum, 0),
        block(cross_sum, 1),
        block(cross_sum, 2),
        block(cross_sum, 3),
        gain_sums[1],
        gain_sums[2],
        turns(0),
        turns(1),
        sum_wd.astype(F32)[None],
    )


def solution(mesh):
    rows = P(ALL, None, None)
    weight = P(ALL, None)
    gain = P(ALL)
    feeding = P("mode", "dp", None)
    return jax.shard_map(
        on_device,
        mesh=mesh,
        in_specs=(
            (rows,) * 3
            + (P(),) * 3
            + (weight,) * 4
            + (gain,)
            + (weight,) * 4
            + (gain,) * 2
            + (feeding,) * 3
        ),
        out_specs=(
            (rows,) * 3
            + (weight,) * 4
            + (gain,)
            + (weight,) * 4
            + (gain,) * 2
            + (feeding,) * 3
        ),
        check_vma=False,
    )
```
